128 devices in a mesh: dp: 4 (over x), expert: 8 (over z, core), tensor: 4 (over y).
Axes of the slice: x: 4, y: 4, z: 4, core: 2. Of those that a mesh axis runs over, the one named last changes fastest.
Arguments:
- tokens: bfloat16 [4096, 2048], P(('dp', 'expert')), may hold values from -6 to 6
- cotangent: bfloat16 [4096, 2048], P(('dp', 'expert')), may hold values from -6 to 6
- seq_lengths: int32 [32, 3], P(('dp', 'expert')), may hold values from 1 to 64, 128 in all within a row
- deal_order: int32 [4096], P(('dp', 'expert')), may hold values from 0 to 4095, as said below
- expert_ids: int32 [4096, 8], P(('dp', 'expert')), may hold values from 0 to 15, all different within a row
- slot_order: int32 [4096, 8], P(('dp', 'expert')), may hold values from 0 to 1023, as said below
- qkv_weight: bfloat16 [3, 2048, 2048], P(None, ('dp', 'expert'), 'tensor'), may hold values from -0.125 to 0.125
- out_weight: bfloat16 [2048, 2048], P('tensor', ('dp', 'expert')), may hold values from -0.5 to 0.5
- router_weight: bfloat16 [16, 2048], P(None, ('dp', 'expert')), may hold values from -0.0625 to 0.0625
- gate_weight: bfloat16 [16, 2048, 1024], P('expert', 'dp', 'tensor'), may hold values from -0.125 to 0.125
- up_weight: bfloat16 [16, 2048, 1024], P('expert', 'dp', 'tensor'), may hold values from -0.125 to 0.125
- down_weight: bfloat16 [16, 2048, 1024], P('expert', 'dp', 'tensor'), may hold values from -0.75 to 0.75
- gain_first: float32 [2048], replicated, may hold values from 0.5 to 1.5
- gain_second: float32 [2048], replicated, may hold values from 0.5 to 1.5
Outputs:
- layer_out: bfloat16 [4096, 2048], P(('dp', 'expert'), 'tensor')
- input_grad: bfloat16 [4096, 2048], P(('dp', 'expert'), 'tensor')
- qkv_grad: float32 [3, 2048, 2048], P(None, ('dp', 'expert'), 'tensor')
- out_grad: float32 [2048, 2048], P('tensor', ('dp', 'expert'))
- router_grad: float32 [16, 2048], P(None, ('dp', 'expert'))
- gate_grad: float32 [16, 2048, 1024], P('expert', 'dp', 'tensor')
- up_grad: float32 [16, 2048, 1024], P('expert', 'dp', 'tensor')
- down_grad: float32 [16, 2048, 1024], P('expert', 'dp', 'tensor')
- gain_first_grad: float32 [2048], P(('dp', 'expert'))
- gain_second_grad: float32 [2048], P(('dp', 'expert'))
The draws below stay inside these ranges and needn't reach their ends.
Inputs may be any that keep to these rules, and one draw needn't show every extreme that they name: `deal_order`: A permutation of the token rows. Row t of group g = t // 128 is dealt to a group d with d // 8 == g // 8, at a position from d * 128 + (g % 8) * 16 up to 16 more; each such block of 16 positions is filled from group g exactly. `slot_order`: in each aligned block of 128 rows the 1024 entries are a permutation. `seq_lengths`: each row sums to 128. `expert_ids`: each row names 8 different experts.
All inputs are finite; a program needn't handle non-finite values.
Results may differ from the reference program's by a relative error of at most 0.023.
Values may be sent and summed in bfloat16 or wider, within the bound.
No kernel may reach another device: no remote copies, remote signals or barrier semaphores. Data moves between devices by JAX's collectives and lax.ppermute only.
A program may use at most 128 MiB of HBM per device.

```python
import math
from functools import partial
import jax
import jax.numpy as jnp
import numpy as np
from jax import lax

D = 2048
HEADS = 16
HEAD_DIM = 128
FF = 1024
TOPK = 8
TOK_GRP = 128
SEQS = 3
EXPERTS = 16
GROUPS = 32
PEERS = 8
SHARE = 16
TOKENS = 4096
CAP = 80


def draw_deal_order(key, part):
    key = jax.random.fold_in(key, 11)
    key_list = jax.random.split(key, GROUPS)
    shuffled = jax.vmap(partial_perm_deal)(key_list)
    group_index = jnp.arange(GROUPS, dtype=jnp.int32)[:, None]
    dest_part = shuffled // SHARE
    inner_index = shuffled % SHARE
    dest_group = group_index // PEERS * PEERS + dest_part
    placed = dest_group * TOK_GRP + group_index % PEERS * SHARE + inner_index
    return placed.reshape(TOKENS).astype(jnp.int32)


def partial_perm_deal(one_key):
    return jax.random.permutation(one_key, TOK_GRP).astype(jnp.int32)


def partial_perm_pairs(one_key):
    return jax.random.permutation(one_key, TOK_GRP * TOPK).astype(jnp.int32)


def draw_slot_order(key, part):
    key = jax.random.fold_in(key, 23)
    key_list = jax.random.split(key, GROUPS)
    shuffled = jax.vmap(partial_perm_pairs)(key_list)
    return shuffled.reshape(TOKENS, TOPK).astype(jnp.int32)


def levels(key, dims, shards, smallest, largest):
    loudness, own = 1.0, jax.random.fold_in(key, 6)
    for dim, shards_of in shards:
        draws = jnp.exp(jax.random.uniform(jax.random.fold_in(own, dim), (shards_of,), jnp.float32, smallest / len(shards), largest / len(shards)))
        loudness = loudness * jnp.repeat(draws, dims[dim] // shards_of).reshape([-1 if axis == dim else 1 for axis in range(len(dims))])
    return loudness


def choose_distinct(rng, rows, number_of, top, lift):
    order = jax.random.permutation(jax.random.fold_in(rng, 1), number_of)
    pull = order
    for power in range(3):
        pull = pull * pull // number_of
    pull = pull * lift // number_of
    tickets = jax.random.randint(jax.random.fold_in(rng, 2), (rows, number_of), 0, 4096) + pull
    fixed_rows = jax.random.permutation(jax.random.fold_in(rng, 3), rows)[jnp.arange(number_of) % rows]
    tickets = jnp.where(jnp.arange(rows)[:, None] == fixed_rows[None, :], 1 << 14, tickets)
    merit = tickets * number_of + jnp.arange(number_of)
    return lax.top_k(merit.astype(jnp.int32), top)[1].astype(jnp.int32)


def length_profile(amount, total, reach, lean):
    loads = [(1 << 20) // math.isqrt(standing ** lean) + 1 for standing in range(2, amount + 1)]
    rest, counts = total - reach - (amount - 1), [1] * (amount - 1)
    while rest > 0:
        free = [i for i in range(amount - 1) if counts[i] < reach]
        whole, left = sum([loads[i] for i in free]), rest
        for i in free:
            addition = min(reach - counts[i], max(1, left * loads[i] // whole), rest)
            counts[i] = counts[i] + addition
            rest = rest - addition
    return np.array([reach] + counts)


def uneven_parts(stream_key, amount, total, bound, lean):
    if amount == 2:
        one = jax.random.randint(stream_key, (), max(1, total - bound), min(bound, total - 1) + 1)
        return jnp.stack([one, total - one])
    sizes = jnp.asarray(length_profile(amount, total, bound, lean), jnp.int32)
    couples = (amount - 1) // 2
    giver, taker = sizes[1:1 + 2 * couples:2], sizes[2:2 + 2 * couples:2]
    room = jnp.minimum(giver - 1, bound - taker)
    passed = jax.random.randint(jax.random.fold_in(stream_key, 1), (couples,), 0, 1 << 20) % (room + 1)
    sizes = sizes.at[1:1 + 2 * couples:2].set(giver - passed).at[2:2 + 2 * couples:2].set(taker + passed)
    return sizes[jax.random.permutation(jax.random.fold_in(stream_key, 2), amount)]


def scatter_about(key, shape, deviation, most, shards=(), kind=jnp.bfloat16):
    gain = levels(key, shape, shards, -0.22, 0.18) if shards else 1.0
    array = jax.random.normal(key, shape, jnp.float32) * deviation * gain
    return jnp.minimum(jnp.maximum(array, -most), most).astype(kind)


def setup_inputs(seed: int = 0) -> dict:
    key_of = jax.random.split(jax.random.key(seed), 15)
    return {
        "tokens": scatter_about(key_of[0], (TOKENS, D), 1.0, 6.0, ((0, 32),)),
        "cotangent": scatter_about(key_of[1], (TOKENS, D), 1.0, 6.0, ((0, 32),)),
        "seq_lengths": jax.vmap(lambda own: uneven_parts(own, SEQS, TOK_GRP, TOK_GRP // 2, 1))(jax.random.split(key_of[2], GROUPS)).reshape((GROUPS, SEQS)).astype(jnp.int32),
        "deal_order": draw_deal_order(jax.random.fold_in(key_of[14], 71), 0),
        "expert_ids": choose_distinct(key_of[4], TOKENS, EXPERTS, TOPK, 4096),
        "slot_order": draw_slot_order(jax.random.fold_in(key_of[14], 71), 0),
        "qkv_weight": scatter_about(key_of[6], (3, D, D), D ** -0.5, 0.125, ((1, 32), (2, 4))),
        "out_weight": scatter_about(key_of[7], (D, D), (D // 16) ** -0.5, 0.5, ((0, 4), (1, 32))),
        "router_weight": scatter_about(key_of[8], (EXPERTS, D), (4 * D) ** -0.5, 0.0625, ((1, 32),)),
        "gate_weight": scatter_about(key_of[9], (EXPERTS, D, FF), D ** -0.5, 0.125, ((0, 8), (1, 4), (2, 4))),
        "up_weight": scatter_about(key_of[10], (EXPERTS, D, FF), D ** -0.5, 0.125, ((0, 8), (1, 4), (2, 4))),
        "down_weight": scatter_about(key_of[11], (EXPERTS, D, FF), (FF // 16) ** -0.5, 0.75, ((0, 8), (1, 4), (2, 4))),
        "gain_first": jnp.clip(1.0 + 0.1 * jax.random.normal(key_of[12], (D,), jnp.float32), 0.5, 1.5),
        "gain_second": jnp.clip(1.0 + 0.1 * jax.random.normal(key_of[13], (D,), jnp.float32), 0.5, 1.5),
    }


@jax.custom_vjp
def low(v):
    return lax.optimization_barrier(v.astype(jnp.bfloat16)).astype(jnp.float32)

@jax.custom_vjp
def low_back(v):
    return v

def low_keep(v):
    return (low(v), None)

def low_pass(kept, grad):
    return (grad,)

def back_keep(v):
    return (v, None)

def back_low(kept, grad):
    return (low(grad),)
low.defvjp(low_keep, low_pass)
low_back.defvjp(back_keep, back_low)
EPSILON = 1e-05
HIGHEST = lax.Precision.HIGHEST

def rounded_both(value):
    return low(low_back(value))

def norm_rows(values, gain_vector):
    factor = lax.rsqrt(lax.optimization_barrier(jnp.mean(values * values, axis=-1, keepdims=True)) + EPSILON)
    return values * factor * gain_vector

def segment_of(seq_lengths, row_count):
    seq_ends = jnp.cumsum(seq_lengths)
    position = jnp.arange(row_count, dtype=jnp.int32)
    return lax.optimization_barrier(jnp.sum((position[:, None] >= seq_ends[None, :]).astype(jnp.int32), axis=1))

def slot_targets(chosen, pair_order, experts, capacity):
    flat_ids = chosen.reshape(-1)
    flat_order = pair_order.reshape(-1)
    pair_count = flat_ids.shape[0]
    by_rank = jnp.zeros((pair_count,), jnp.int32).at[flat_order].set(jnp.arange(pair_count, dtype=jnp.int32))
    ranked_ids = flat_ids[by_rank]
    expert_match = (ranked_ids[:, None] == jnp.arange(experts, dtype=jnp.int32)[None, :]).astype(jnp.int32)
    earlier = jnp.cumsum(expert_match, axis=0) - expert_match
    ranked_slot = lax.optimization_barrier(jnp.sum(earlier * expert_match, axis=1))
    slot_index = jnp.zeros((pair_count,), jnp.int32).at[by_rank].set(ranked_slot)
    slot_target = jnp.where(slot_index < capacity, flat_ids * capacity + slot_index, experts * capacity)
    return slot_target.reshape(chosen.shape)

def group_layer(params, inputs):
    qkv_proj, out_proj, router_proj, gate_proj, up_proj, down_proj, gain_one, gain_two = params
    group_rows, segment, chosen, slot_target = inputs
    normed = low(norm_rows(group_rows, gain_one))
    queries = rounded_both(jnp.dot(normed, qkv_proj[0], precision=HIGHEST)).reshape(TOK_GRP, HEADS, HEAD_DIM)
    keys_here = rounded_both(jnp.dot(normed, qkv_proj[1], precision=HIGHEST)).reshape(TOK_GRP, HEADS, HEAD_DIM)
    values_here = rounded_both(jnp.dot(normed, qkv_proj[2], precision=HIGHEST)).reshape(TOK_GRP, HEADS, HEAD_DIM)
    scores = low_back(jnp.einsum('qhd,khd->hqk', queries, keys_here, precision=HIGHEST) * HEAD_DIM ** (-0.5))
    same_seq = segment[:, None] == segment[None, :]
    scores = jnp.where(same_seq[None, :, :], scores, -1000000000.0)
    weights = low(jax.nn.softmax(scores, axis=-1))
    mixed_heads = rounded_both(jnp.einsum('hqk,khd->qhd', weights, values_here, precision=HIGHEST).reshape(TOK_GRP, D))
    resid = group_rows + low_back(jnp.dot(mixed_heads, out_proj, precision=HIGHEST))
    hidden = low(norm_rows(resid, gain_two))
    router_logits = low_back(jnp.dot(hidden, router_proj.T, precision=HIGHEST))
    picked_logits = jnp.take_along_axis(router_logits, chosen, axis=1)
    gate_values = jax.nn.softmax(picked_logits, axis=-1)
    pair_rows = jnp.broadcast_to(hidden[:, None, :], (TOK_GRP, TOPK, D)).reshape(TOK_GRP * TOPK, D)
    buffer = jnp.zeros((EXPERTS * CAP + 1, D), jnp.float32).at[slot_target.reshape(-1)].set(pair_rows)
    sent = low_back(buffer[:-1].reshape(EXPERTS, CAP, D))
    gate_part = low_back(jnp.einsum('ecd,edf->ecf', sent, gate_proj, precision=HIGHEST))
    up_part = low_back(jnp.einsum('ecd,edf->ecf', sent, up_proj, precision=HIGHEST))
    active = low(jax.nn.silu(gate_part) * up_part)
    returned = rounded_both(jnp.einsum('ecf,edf->ecd', active, down_proj, precision=HIGHEST))
    back_table = jnp.concatenate([returned.reshape(EXPERTS * CAP, D), jnp.zeros((1, D), jnp.float32)], axis=0)
    picked = back_table[slot_target]
    return resid + lax.optimization_barrier(jnp.sum(gate_values[:, :, None] * picked, axis=1))

def reference(tokens, cotangent, seq_lengths, deal_order, expert_ids, slot_order, qkv_weight, out_weight, router_weight, gate_weight, up_weight, down_weight, gain_first, gain_second):
    dealt_rows = jnp.zeros((TOKENS, D), jnp.float32).at[deal_order].set(tokens.astype(jnp.float32))
    dealt_grad = jnp.zeros((TOKENS, D), jnp.float32).at[deal_order].set(cotangent.astype(jnp.float32))
    segments = jax.vmap(partial(segment_of, row_count=TOK_GRP))(seq_lengths)
    grouped_ids = expert_ids.reshape(GROUPS, TOK_GRP, TOPK)
    targets = jax.vmap(partial(slot_targets, experts=EXPERTS, capacity=CAP))(grouped_ids, slot_order.reshape(GROUPS, TOK_GRP, TOPK))
    params = (qkv_weight.astype(jnp.float32), out_weight.astype(jnp.float32), router_weight.astype(jnp.float32), gate_weight.astype(jnp.float32), up_weight.astype(jnp.float32), down_weight.astype(jnp.float32), gain_first.astype(jnp.float32), gain_second.astype(jnp.float32))

    def forward(weight_set, rows_in):
        group_step = jax.checkpoint(partial(group_layer, weight_set))
        stacked = (rows_in.reshape(GROUPS, TOK_GRP, D), segments, grouped_ids, targets)
        return lax.map(group_step, stacked).reshape(TOKENS, D)
    dealt_out, pullback = jax.vjp(forward, params, dealt_rows)
    weight_grads, rows_grad = pullback(dealt_grad)
    return (dealt_out[deal_order].astype(jnp.bfloat16), rows_grad[deal_order].astype(jnp.bfloat16), weight_grads[0], weight_grads[1], weight_grads[2], weight_grads[3], weight_grads[4], weight_grads[5], weight_grads[6], weight_grads[7])
```

```python
import jax
import jax.numpy as jnp
from jax import lax
from jax.sharding import Mesh
from jax.sharding import PartitionSpec as P

HEAD_DIM = 128
EPSILON = 1e-05
F32 = jnp.float32
BF16 = jnp.bfloat16
BIG = 1 << 30


def shift(values, axis, step):
    size = lax.axis_size(axis)
    return lax.ppermute(values, axis, [(i, (i + step) % size) for i in range(size)])


def pick(parts, index):
    return lax.dynamic_index_in_dim(parts, index, 0, keepdims=False)


def ring_sum(parts, axis):
    size = lax.axis_size(axis)
    me = lax.axis_index(axis)
    total = pick(parts, me).astype(F32)
    got = [shift(pick(parts, (me + k) % size), axis, k) for k in (1, size - 1, 2)]
    for piece in got:
        total = total + piece.astype(F32)
    return total


def ring_gather(values, axis):
    size = lax.axis_size(axis)
    me = lax.axis_index(axis)
    held = {0: values}
    for k in (size - 1, 1, 2):
        held[(size - k) % size] = shift(values, axis, k)
    stacked = jnp.stack([held[k] for k in range(size)])
    return [pick(stacked, (j - me) % size) for j in range(size)]


def core_swap(values):
    return lax.ppermute(values, "core", [(0, 1), (1, 0)])


def hi_lo(values):
    high = values.astype(BF16)
    return high, (values - high.astype(F32)).astype(BF16)


def segment_of(seq_lengths, row_count):
    seq_ends = jnp.cumsum(seq_lengths)
    position = jnp.arange(row_count, dtype=jnp.int32)
    return jnp.sum((position[:, None] >= seq_ends[None, :]).astype(jnp.int32), axis=1)


def local(
    tokens,
    cotangent,
    seq_lengths,
    deal_order,
    expert_ids,
    slot_order,
    qkv_weight,
    out_weight,
    router_weight,
    gate_weight,
    up_weight,
    down_weight,
    gain_first,
    gain_second,
):
    rows, width = tokens.shape
    zc = ("z", "core")
    peers = lax.axis_size("z") * lax.axis_size("core")
    tensors = lax.axis_size("tensor")
    dps = lax.axis_size("dp")
    zs = lax.axis_size("z")
    share = rows // peers
    part = width // tensors
    me_core = lax.axis_index("core")
    me_z = lax.axis_index("z")
    me = me_z * 2 + me_core
    me_y = lax.axis_index("tensor")
    experts = router_weight.shape[0]
    top = expert_ids.shape[1]
    capacity = (5 * rows * top + 4 * experts - 1) // (4 * experts)
    here = gate_weight.shape[0]
    hidden_part = gate_weight.shape[2]
    head_width = qkv_weight.shape[2]
    heads = head_width // HEAD_DIM
    scale = HEAD_DIM ** (-0.5)
    feats = qkv_weight.shape[1]

    attn_local = jnp.concatenate(
        [
            qkv_weight[0],
            qkv_weight[1],
            qkv_weight[2],
            out_weight.T,
            jnp.pad(router_weight.T, ((0, 0), (0, 128 - experts))),
        ],
        axis=1,
    )
    attn_full = lax.all_gather(attn_local, ("dp", "z", "core"), axis=0, tiled=True)
    expert_local = jnp.concatenate([gate_weight, up_weight, down_weight], axis=0)
    expert_full = lax.all_gather(expert_local, "dp", axis=1, tiled=True)

    dest_group = deal_order // rows % peers
    place = dest_group * share + (deal_order % rows - me * share)
    deal_matrix = (place[None, :] == jnp.arange(rows, dtype=jnp.int32)[:, None]).astype(BF16)
    both = jnp.dot(
        deal_matrix, jnp.concatenate([tokens, cotangent], axis=1), preferred_element_type=F32
    ).astype(BF16)
    got = lax.all_to_all(
        both[:, :width].reshape(peers, share, width), zc, split_axis=0, concat_axis=0, tiled=True
    )
    resid_in = got.reshape(rows, width).astype(F32)
    cot_part = lax.dynamic_slice_in_dim(both[:, width:], me_y * part, part, 1)
    cot_cols = lax.all_gather(cot_part, zc, axis=0, tiled=False)
    cot_cols = cot_cols.reshape(peers, peers, share, part).transpose(1, 0, 2, 3)
    cot_all = lax.all_gather(
        cot_cols.reshape(peers * rows, part), "tensor", axis=1, tiled=True
    )
    cot_all3 = cot_all.reshape(peers, rows, width)
    upstream = lax.dynamic_index_in_dim(cot_all3, me, 0, keepdims=False).astype(F32)

    match = expert_ids[:, :, None] == jnp.arange(experts, dtype=jnp.int32)[None, None, :]
    order = jnp.min(jnp.where(match, slot_order[:, :, None], BIG), axis=1)
    chosen = order < BIG
    earlier = jnp.sum((order[None, :, :] < order[:, None, :]).astype(jnp.int32), axis=1)
    code = chosen.astype(F32) + (chosen & (earlier < capacity)).astype(F32)
    code_all = lax.all_gather(
        jnp.pad(code, ((0, 0), (0, 128 - experts))).astype(BF16), zc, axis=0, tiled=True
    )[:, :experts]
    chosen_all = code_all > 0.5
    kept_all = code_all > 1.5

    factor_first = lax.rsqrt(jnp.mean(resid_in * resid_in, axis=-1, keepdims=True) + EPSILON)
    unit_first = resid_in * factor_first
    normed = (unit_first * gain_first).astype(BF16)
    qkv_full = attn_full[:, : 3 * head_width]
    out_t = attn_full[:, 3 * head_width : 4 * head_width]
    router_t = attn_full[:, 4 * head_width : 4 * head_width + experts]
    projected = jnp.dot(normed, qkv_full, preferred_element_type=F32).astype(BF16)
    queries = projected[:, :head_width].reshape(rows, heads, HEAD_DIM)
    keys = projected[:, head_width : 2 * head_width].reshape(rows, heads, HEAD_DIM)
    values = projected[:, 2 * head_width :].reshape(rows, heads, HEAD_DIM)
    segment = segment_of(seq_lengths[0], rows)
    same_seq = (segment[:, None] == segment[None, :])[None, :, :]
    scores = jnp.einsum("qhd,khd->hqk", queries, keys, preferred_element_type=F32) * scale
    scores = jnp.where(same_seq, scores, -1000000000.0)
    peak = jnp.max(scores, axis=-1, keepdims=True)
    exponent = jnp.exp(scores - peak)
    weights = exponent / jnp.sum(exponent, axis=-1, keepdims=True)
    weights_low = weights.astype(BF16)
    mixed = jnp.einsum("hqk,khd->qhd", weights_low, values, preferred_element_type=F32)
    mixed = mixed.astype(BF16).reshape(rows, head_width)
    mixed_all = lax.all_gather(mixed, zc, axis=0, tiled=True)
    branch = lax.dot_general(
        mixed, out_t, (((1,), (1,)), ((), ())), preferred_element_type=F32
    ).astype(BF16)
    branch = branch.reshape(rows, tensors, part).transpose(1, 0, 2)
    resid_part = lax.dynamic_slice_in_dim(resid_in, me_y * part, part, 1) + ring_sum(
        branch, "tensor"
    )
    resid_rows = jnp.concatenate(ring_gather(resid_part.astype(BF16), "tensor"), axis=1)
    resid_z = jnp.stack(ring_gather(resid_rows, "z"))
    resid_other = core_swap(resid_z)
    first = jnp.where(me_core == 0, resid_z, resid_other)
    second = jnp.where(me_core == 0, resid_other, resid_z)
    resid_all = jnp.stack([first, second], axis=1).reshape(peers * rows, width).astype(F32)

    factor_all = lax.rsqrt(jnp.mean(resid_all * resid_all, axis=-1, keepdims=True) + EPSILON)
    hidden = (resid_all * factor_all * gain_second).astype(BF16)
    logits = jnp.dot(hidden, router_t, preferred_element_type=F32)
    top_logit = jnp.max(jnp.where(chosen_all, logits, -jnp.inf), axis=-1, keepdims=True)
    lifted = jnp.where(chosen_all, jnp.exp(logits - top_logit), 0.0)
    gates_all = lifted / jnp.sum(lifted, axis=-1, keepdims=True)
    used_all = jnp.where(kept_all, gates_all, 0.0)
    used = lax.dynamic_slice_in_dim(used_all, me * here, here, 1)
    gate_w = expert_full[:here]
    up_w = expert_full[here : 2 * here]
    down_w = expert_full[2 * here :]
    gate_part = jnp.einsum("td,edf->tef", hidden, gate_w, preferred_element_type=F32)
    up_part = jnp.einsum("td,edf->tef", hidden, up_w, preferred_element_type=F32)
    sigmoid = jax.nn.sigmoid(gate_part)
    silu = gate_part * sigmoid
    active = silu * up_part
    active_used = (active * used[:, :, None]).astype(BF16)
    back = jnp.einsum("td,edf->tef", cot_all, down_w, preferred_element_type=F32)
    gate_dot = jnp.sum(back * active, axis=-1)
    back = back * used[:, :, None]
    grad_gate = (back * up_part * sigmoid * (1.0 + gate_part * (1.0 - sigmoid))).astype(BF16)
    grad_up = (back * silu).astype(BF16)
    grad_rows = jnp.einsum("tef,edf->td", grad_gate, gate_w, preferred_element_type=F32)
    grad_rows = grad_rows + jnp.einsum("tef,edf->td", grad_up, up_w, preferred_element_type=F32)
    kept_here = lax.dynamic_slice_in_dim(kept_all, me * here, here, 1)
    gate_dot = jnp.where(kept_here, gate_dot, 0.0)
    dot_table = jnp.zeros((peers * rows, experts), F32)
    dot_table = lax.dynamic_update_slice_in_dim(dot_table, gate_dot, me * here, 1)
    dot_high, dot_low = hi_lo(dot_table)
    dot_cols = jnp.concatenate(
        [dot_high, dot_low, jnp.zeros((peers * rows, 128 - 2 * experts), BF16)], axis=1
    )
    sent = jnp.concatenate([grad_rows.astype(BF16), dot_cols], axis=1)
    sent = sent.reshape(zs, 2, rows, width + 128)
    own = lax.dynamic_index_in_dim(sent, me_core, 1, keepdims=False)
    swapped = core_swap(lax.dynamic_index_in_dim(sent, 1 - me_core, 1, keepdims=False))
    paired = (own.astype(F32) + swapped.astype(F32)).astype(BF16)
    at_group = ring_sum(paired, "z")
    dots_here = at_group[:, width : width + experts] + at_group[:, width + experts : width + 2 * experts]
    dots_here = jnp.concatenate(
        [*hi_lo(dots_here), jnp.zeros((rows, 128 - 2 * experts), BF16)], axis=1
    )
    cols = at_group[:, :width].astype(BF16).reshape(rows, tensors, part).transpose(1, 0, 2)
    cols = jnp.concatenate(
        [cols, jnp.broadcast_to(dots_here[None], (tensors, rows, 128))], axis=2
    )
    cols = ring_sum(cols, "tensor")
    dots = cols[:, part : part + experts] + cols[:, part + experts : part + 2 * experts]
    grad_hidden = jnp.concatenate(ring_gather(cols[:, :part].astype(BF16), "tensor"), axis=1).astype(F32)

    def own_rows(table):
        return lax.dynamic_slice_in_dim(table, me * rows, rows, 0)

    gates = own_rows(gates_all)
    hidden_here = own_rows(hidden)
    grad_logits = (gates * (dots - jnp.sum(dots * gates, axis=-1, keepdims=True))).astype(BF16)
    grad_hidden = grad_hidden + lax.dot_general(
        grad_logits, router_t, (((1,), (1,)), ((), ())), preferred_element_type=F32
    )
    grad_router = lax.dot_general(
        grad_logits, hidden_here, (((0,), (0,)), ((), ())), preferred_element_type=F32
    )
    factor_second = own_rows(factor_all)
    unit_second = own_rows(resid_all) * factor_second
    grad_gain_second = jnp.sum(grad_hidden * unit_second, axis=0)
    scaled = grad_hidden * gain_second
    grad_resid = upstream + factor_second * (
        scaled - unit_second * jnp.mean(scaled * unit_second, axis=-1, keepdims=True)
    )
    grad_branch = grad_resid.astype(BF16)

    grad_mixed = jnp.dot(grad_branch, out_t, preferred_element_type=F32)
    grad_mixed = grad_mixed.astype(BF16).reshape(rows, heads, HEAD_DIM)
    grad_values = jnp.einsum(
        "hqk,qhd->khd", weights_low, grad_mixed, preferred_element_type=F32
    ).astype(BF16)
    grad_weights = jnp.einsum("qhd,khd->hqk", grad_mixed, values, preferred_element_type=F32)
    offset = jnp.sum(grad_weights * weights, axis=-1, keepdims=True)
    grad_scores = (weights * (grad_weights - offset)).astype(BF16)
    grad_queries = (
        jnp.einsum("hqk,khd->qhd", grad_scores, keys, preferred_element_type=F32) * scale
    ).astype(BF16)
    grad_keys = (
        jnp.einsum("hqk,qhd->khd", grad_scores, queries, preferred_element_type=F32) * scale
    ).astype(BF16)
    grad_proj = jnp.concatenate(
        [
            grad_queries.reshape(rows, head_width),
            grad_keys.reshape(rows, head_width),
            grad_values.reshape(rows, head_width),
        ],
        axis=1,
    )
    grad_proj_all = lax.all_gather(grad_proj, zc, axis=0, tiled=True)

    def by_feature(table):
        count = table.shape[0]
        return (
            table.reshape(count, dps, peers, feats)
            .transpose(2, 0, 1, 3)
            .reshape(peers, count, dps * feats)
        )

    def to_feature(table):
        return lax.all_to_all(by_feature(table), zc, split_axis=0, concat_axis=0, tiled=True)

    normed_feat = to_feature(normed).reshape(peers * rows, dps * feats)
    branch_feat = to_feature(grad_branch).reshape(peers * rows, dps * feats)
    grad_out_t = lax.dot_general(
        branch_feat, mixed_all, (((0,), (0,)), ((), ())), preferred_element_type=F32
    )

    grad_normed = lax.dot_general(
        grad_proj, qkv_full, (((1,), (1,)), ((), ())), preferred_element_type=F32
    )
    gain_unit = gain_first * unit_first
    inner = jnp.sum(grad_normed * gain_unit, axis=-1, keepdims=True)
    grad_gain_first = jnp.sum(grad_normed * unit_first, axis=0)
    inner_cols = jnp.concatenate([*hi_lo(inner), jnp.zeros((rows, 126), BF16)], axis=1)
    normed_cols = grad_normed.astype(BF16).reshape(rows, tensors, part).transpose(1, 0, 2)
    normed_cols = jnp.concatenate(
        [normed_cols, jnp.broadcast_to(inner_cols[None], (tensors, rows, 128))], axis=2
    )
    normed_cols = ring_sum(normed_cols, "tensor")
    inner = (normed_cols[:, part : part + 1] + normed_cols[:, part + 1 : part + 2]) / width

    def own_cols(table):
        return lax.dynamic_slice_in_dim(table, me_y * part, part, table.ndim - 1)

    input_part = own_cols(grad_resid) + factor_first * (
        normed_cols[:, :part] * own_cols(gain_first) - own_cols(unit_first) * inner
    )

    gain_first_sum = sum(
        piece for piece in ring_gather(grad_gain_first.reshape(16, -1), "tensor")
    ).reshape(1, width)
    small = jnp.concatenate(
        [
            grad_router,
            grad_gain_second[None],
            gain_first_sum,
            jnp.zeros((32 - experts - 2, width), F32),
        ],
        axis=0,
    ).astype(BF16)
    small = jnp.sum(to_feature(small).astype(F32), axis=0)

    grad_qkv = lax.dot_general(
        normed_feat, grad_proj_all, (((0,), (0,)), ((), ())), preferred_element_type=F32
    )
    by_dp = jnp.concatenate(
        [
            grad_qkv.astype(BF16),
            grad_out_t.astype(BF16),
            jnp.pad(small.T, ((0, 0), (0, 96))).astype(BF16),
        ],
        axis=1,
    ).reshape(dps, feats, 4 * head_width + 128)
    by_dp = ring_sum(by_dp, "dp")
    qkv_grad = by_dp[:, : 3 * head_width].reshape(feats, 3, head_width).transpose(1, 0, 2)
    out_grad = by_dp[:, 3 * head_width : 4 * head_width].T
    tail = by_dp[:, 4 * head_width :]
    router_grad = tail[:, :experts].T
    gain_second_grad = tail[:, experts]
    gain_first_grad = tail[:, experts + 1]

    grad_gate_w = jnp.einsum("td,tef->edf", hidden, grad_gate, preferred_element_type=F32)
    grad_up_w = jnp.einsum("td,tef->edf", hidden, grad_up, preferred_element_type=F32)
    grad_down = jnp.einsum("td,tef->edf", cot_all, active_used, preferred_element_type=F32)
    expert_grads = jnp.concatenate(
        [g.astype(BF16).reshape(here, dps, -1, hidden_part) for g in (grad_gate_w, grad_up_w, grad_down)],
        axis=0,
    ).transpose(1, 0, 2, 3)
    expert_grads = lax.psum_scatter(expert_grads, "dp", scatter_dimension=0, tiled=False).astype(F32)

    expert_rows = jnp.einsum("tef,edf->td", active_used, down_w, preferred_element_type=F32)
    expert_rows = lax.psum_scatter(
        expert_rows.astype(BF16).reshape(peers, rows, width), zc, scatter_dimension=0, tiled=False
    )
    expert_rows = lax.psum_scatter(
        expert_rows.reshape(rows, tensors, part).transpose(1, 0, 2),
        "tensor",
        scatter_dimension=0,
        tiled=False,
    ).astype(F32)
    output_part = resid_part + expert_rows

    final = jnp.concatenate([output_part.astype(BF16), input_part.astype(BF16)], axis=1)
    final = lax.all_to_all(
        final.reshape(peers, share, 2 * part), zc, split_axis=0, concat_axis=0, tiled=True
    ).reshape(rows, 2 * part)
    final = lax.dot_general(
        deal_matrix, final, (((0,), (0,)), ((), ())), preferred_element_type=F32
    ).astype(BF16)
    return (
        final[:, :part],
        final[:, part:],
        qkv_grad,
        out_grad,
        router_grad,
        expert_grads[:here],
        expert_grads[here : 2 * here],
        expert_grads[2 * here :],
        gain_first_grad,
        gain_second_grad,
    )


def solution(mesh):
    sizes = mesh.shape
    split = Mesh(
        mesh.devices.reshape(sizes["dp"], sizes["expert"] // 2, 2, sizes["tensor"]),
        ("dp", "z", "core", "tensor"),
    )
    experts = ("z", "core")
    every = ("dp", "z", "core")
    placed = (
        P(every, None),
        P(every, None),
        P(every, None),
        P(every),
        P(every, None),
        P(every, None),
        P(None, every, "tensor"),
        P("tensor", every),
        P(None, every),
        P(experts, "dp", "tensor"),
        P(experts, "dp", "tensor"),
        P(experts, "dp", "tensor"),
        P(),
        P(),
    )
    return jax.shard_map(
        local,
        mesh=split,
        in_specs=placed,
        out_specs=(
            P(every, "tensor"),
            P(every, "tensor"),
            P(None, every, "tensor"),
            P("tensor", every),
            P(None, every),
            P(experts, "dp", "tensor"),
            P(experts, "dp", "tensor"),
            P(experts, "dp", "tensor"),
            P(every),
            P(every),
        ),
        check_vma=False,
    )
```

```python
import jax
import jax.numpy as jnp
from jax import lax
from jax.sharding import Mesh
from jax.sharding import PartitionSpec as P
from jax.experimental import pallas as pl
from jax.experimental.pallas import tpu as pltpu

HEAD_DIM = 128
EPSILON = 1e-05
F32 = jnp.float32
BF16 = jnp.bfloat16
BIG = 1 << 30
VMEM = pltpu.VMEM
ANY = pl.ANY


def shift(values, axis, step):
    size = lax.axis_size(axis)
    return lax.ppermute(values, axis, [(i, (i + step) % size) for i in range(size)])


def pick(parts, index):
    return lax.dynamic_index_in_dim(parts, index, 0, keepdims=False)


def ring_sum(parts, axis):
    size = lax.axis_size(axis)
    me = lax.axis_index(axis)
    total = pick(parts, me).astype(F32)
    got = [shift(pick(parts, (me + k) % size), axis, k) for k in (1, size - 1, 2)]
    for piece in got:
        total = total + piece.astype(F32)
    return total


def ring_gather(values, axis):
    size = lax.axis_size(axis)
    me = lax.axis_index(axis)
    held = {0: values}
    for k in (size - 1, 1, 2):
        held[(size - k) % size] = shift(values, axis, k)
    stacked = jnp.stack([held[k] for k in range(size)])
    return [pick(stacked, (j - me) % size) for j in range(size)]


def core_swap(values):
    return lax.ppermute(values, "core", [(0, 1), (1, 0)])


def hi_lo(values):
    high = values.astype(BF16)
    return high, (values - high.astype(F32)).astype(BF16)


def gather_near(values, axis):
    size = lax.axis_size(axis)
    got = {k: shift(values, axis, -k) for k in (1, size - 1, 2)}
    return [values] + [got[k] for k in range(1, size)]


def sum_near(parts, axis):
    size = lax.axis_size(axis)
    total = parts[0].astype(F32)
    for k in (1, size - 1, 2):
        total = total + shift(parts[k], axis, k).astype(F32)
    return total


def in_order(near, axis):
    size = lax.axis_size(axis)
    me = lax.axis_index(axis)
    stacked = near if hasattr(near, "shape") else jnp.stack(near)
    return [pick(stacked, (j - me) % size) for j in range(size)]


def segment_of(seq_lengths, row_count):
    seq_ends = jnp.cumsum(seq_lengths)
    position = jnp.arange(row_count, dtype=jnp.int32)
    return jnp.sum((position[:, None] >= seq_ends[None, :]).astype(jnp.int32), axis=1)


def nt(a,b): return lax.dot_general(a,b,(((1,),(1,)),((),())),preferred_element_type=F32)
def tn(a,b): return lax.dot_general(a,b,(((0,),(0,)),((),())),preferred_element_type=F32)

def spec(space):
    return pl.BlockSpec(memory_space=space)


def params(megabytes):
    return pltpu.CompilerParams(vmem_limit_bytes=megabytes * 1024 * 1024)


def cost(flops, moved):
    return pl.CostEstimate(flops=flops, bytes_accessed=moved, transcendentals=0)


def pack_kernel(qkv, out, router, packed):
    for s in range(3):
        packed[:, s * 512 : (s + 1) * 512] = qkv[s]
    packed[:, 1536:2048] = out[...].astype(F32).T.astype(BF16)
    wide = jnp.concatenate([router[...].astype(F32), jnp.zeros((112, 64), F32)], axis=0)
    packed[:, 2048:] = wide.T.astype(BF16)


def pack_call(qkv, out, router):
    return pl.pallas_call(
        pack_kernel,
        out_shape=jax.ShapeDtypeStruct((64, 2176), BF16),
        cost_estimate=cost(1000, 6 * 10**5),
        name="pack",
    )(qkv, out, router)


def spread_features(values, out, row):
    count = values.shape[0]
    for e in range(8):
        for d in range(4):
            at = d * 512 + e * 64
            out[e, row : row + count, d * 64 : (d + 1) * 64] = values[:, at : at + 64]


def norm_kernel(tokens, gain, normed_out, feat_out):
    values = tokens[...].astype(F32)
    factor = lax.rsqrt(jnp.mean(values * values, axis=-1, keepdims=True) + EPSILON)
    normed = (values * factor * gain[...]).astype(BF16)
    normed_out[...] = normed
    spread_features(normed, feat_out, 0)


def norm_call(tokens, gain):
    shape = jax.ShapeDtypeStruct
    return pl.pallas_call(
        norm_kernel,
        out_shape=(shape((128, 2048), BF16), shape((8, 128, 256), BF16)),
        cost_estimate=cost(10**6, 15 * 10**5),
        name="norm",
    )(tokens, gain)


def attention_kernel(
    where, normed, same, packed, proj_out, prob_out, mixed_out, branch, w_buf, o_buf, sem_w, sem_o
):
    y0 = where[0]
    loads = [
        pltpu.make_async_copy(
            packed.at[pl.ds(i * 512, 512), 0:1536], w_buf.at[pl.ds(i * 512, 512)], sem_w.at[i]
        )
        for i in range(4)
    ]
    for load in loads:
        load.start()
    out_load = pltpu.make_async_copy(packed.at[:, 1536:2048], o_buf, sem_o)
    out_load.start()
    for load in loads:
        load.wait()
    for s in range(3):
        proj_out[s] = jnp.dot(
            normed[...], w_buf[:, s * 512 : (s + 1) * 512], preferred_element_type=F32
        ).astype(BF16)
    mask = same[...] > 0.5
    scale = HEAD_DIM ** (-0.5)
    for h in range(4):
        cols = slice(h * HEAD_DIM, (h + 1) * HEAD_DIM)
        scores = jnp.where(
            mask, nt(proj_out[0, :, cols], proj_out[1, :, cols]) * scale, -1000000000.0
        )
        grown = jnp.exp(scores - jnp.max(scores, axis=-1, keepdims=True))
        prob = grown / jnp.sum(grown, axis=-1, keepdims=True)
        prob_out[h] = prob
        mixed_out[:, cols] = jnp.dot(
            prob.astype(BF16), proj_out[2, :, cols], preferred_element_type=F32
        ).astype(BF16)
    out_load.wait()
    for k in range(4):
        at = pl.multiple_of(((y0 + k) & 3) * 512, 512)
        branch[k] = nt(mixed_out[...], o_buf[pl.ds(at, 512), :]).astype(BF16)


def attention_call(where, normed, same, packed):
    shape = jax.ShapeDtypeStruct
    dma = pltpu.SemaphoreType.DMA
    return pl.pallas_call(
        attention_kernel,
        out_shape=(
            shape((3, 128, 512), BF16),
            shape((4, 128, 128), F32),
            shape((128, 512), BF16),
            shape((4, 128, 512), BF16),
        ),
        in_specs=[spec(pltpu.SMEM), spec(VMEM), spec(VMEM), spec(ANY)],
        out_specs=(spec(VMEM),) * 4,
        scratch_shapes=[VMEM((2048, 1536), BF16), VMEM((2048, 512), BF16), dma((4,)), dma],
        compiler_params=params(40),
        cost_estimate=cost(2 * 10**9, 10 * 10**6),
        name="attention",
    )(where, normed, same, packed)


def attention_back_kernel(
    where, g0, g1, g2, g3, dots, gates, hidden, resid, c0, c1, c2, c3, packed, proj_in, prob_in, gain,
    feat_out, grad_proj, own_out,
    o_buf, h_buf, c_buf, x_buf, d_buf, x_low, d_low, proj, prob, sem_o, sem_h, sem_c, sem_x, sem_d, sem_p,
):
    y0 = where[0]
    offs = [pl.multiple_of(((y0 + k) & 3) * 512, 512) for k in range(4)]
    d_loads = [
        pltpu.make_async_copy(g, d_low.at[:, pl.ds(offs[k], 512)], sem_d.at[k])
        for k, g in enumerate((g0, g1, g2, g3))
    ]
    x_loads = [
        pltpu.make_async_copy(resid.at[k], x_low.at[:, pl.ds(offs[k], 512)], sem_x.at[k])
        for k in range(4)
    ]
    h_load = pltpu.make_async_copy(hidden.at[0:128], h_buf, sem_h)
    o_load = pltpu.make_async_copy(packed.at[:, 1536:2176], o_buf, sem_o)
    c_loads = [
        pltpu.make_async_copy(c.at[0:128], c_buf.at[:, pl.ds(offs[k], 512)], sem_c.at[k])
        for k, c in enumerate((c0, c1, c2, c3))
    ]
    p_loads = [
        pltpu.make_async_copy(proj_in, proj, sem_p.at[0]),
        pltpu.make_async_copy(prob_in, prob, sem_p.at[1]),
    ]
    for load in [*x_loads, *d_loads, h_load, o_load, *c_loads, *p_loads]:
        load.start()
    for load in [*x_loads, *d_loads]:
        load.wait()
    x_buf[...] = x_low[...].astype(F32)
    d_buf[...] = d_low[...].astype(F32)
    share = gates[...]
    dot = dots[...]
    grad_logits = (share * (dot - jnp.sum(dot * share, axis=-1, keepdims=True))).astype(BF16)
    o_load.wait()
    h_load.wait()
    router = tn(grad_logits, h_buf[...])
    grad_hidden = d_buf[...] + nt(grad_logits, o_buf[:, 512:])
    resid_rows = x_buf[...]
    factor = lax.rsqrt(jnp.mean(resid_rows * resid_rows, axis=-1, keepdims=True) + EPSILON)
    unit = resid_rows * factor
    gain_sum = jnp.sum(grad_hidden * unit, axis=0, keepdims=True)
    scaled = grad_hidden * gain[...]
    for load in c_loads:
        load.wait()
    grad = c_buf[...].astype(F32) + factor * (
        scaled - unit * jnp.mean(scaled * unit, axis=-1, keepdims=True)
    )
    d_buf[...] = grad
    own_out[...] = d_buf[:, pl.ds(offs[0], 512)]
    low = grad.astype(BF16)
    spread_features(low, feat_out, 0)
    spread_features(router[:16].astype(BF16), feat_out, 128)
    high = gain_sum.astype(BF16)
    rest = (gain_sum - high.astype(F32)).astype(BF16)
    tail = jnp.concatenate(
        [high.astype(F32), rest.astype(F32), jnp.zeros((14, 2048), F32)], axis=0
    ).astype(BF16)
    spread_features(tail, feat_out, 144)
    feat_out[:, 160:] = jnp.zeros((8, 16, 256), BF16)
    mixed = jnp.dot(low, o_buf[:, :512], preferred_element_type=F32).astype(BF16)
    for load in p_loads:
        load.wait()
    scale = HEAD_DIM ** (-0.5)
    for h in range(4):
        cols = slice(h * HEAD_DIM, (h + 1) * HEAD_DIM)
        weights = prob[h]
        back = mixed[:, cols]
        grad_proj[:, 1024 + h * HEAD_DIM : 1024 + (h + 1) * HEAD_DIM] = tn(
            weights.astype(BF16), back
        ).astype(BF16)
        weight_grad = nt(back, proj[2, :, cols])
        offset = jnp.sum(weight_grad * weights, axis=-1, keepdims=True)
        score = (weights * (weight_grad - offset)).astype(BF16)
        grad_proj[:, cols] = (
            jnp.dot(score, proj[1, :, cols], preferred_element_type=F32) * scale
        ).astype(BF16)
        grad_proj[:, 512 + h * HEAD_DIM : 512 + (h + 1) * HEAD_DIM] = (
            tn(score, proj[0, :, cols]) * scale
        ).astype(BF16)


def attention_back_call(where, grads, dots, gates, hidden, resid, cots, packed, proj, prob, gain):
    shape = jax.ShapeDtypeStruct
    dma = pltpu.SemaphoreType.DMA
    return pl.pallas_call(
        attention_back_kernel,
        out_shape=(
            shape((8, 176, 256), BF16),
            shape((128, 1536), BF16),
            shape((128, 512), F32),
        ),
        in_specs=[spec(pltpu.SMEM)]
        + [spec(ANY)] * 4
        + [spec(VMEM)] * 2
        + [spec(ANY)] * 9
        + [spec(VMEM)],
        out_specs=(spec(VMEM),) * 3,
        scratch_shapes=[
            VMEM((2048, 640), BF16),
            VMEM((128, 2048), BF16),
            VMEM((128, 2048), BF16),
            VMEM((128, 2048), F32),
            VMEM((128, 2048), F32),
            VMEM((128, 2048), BF16),
            VMEM((128, 2048), BF16),
            VMEM((3, 128, 512), BF16),
            VMEM((4, 128, 128), F32),
            dma,
            dma,
            dma((4,)),
            dma((4,)),
            dma((4,)),
            dma((2,)),
        ],
        compiler_params=params(40),
        cost_estimate=cost(10**9, 6 * 10**6),
        name="attention_back",
    )(where, *grads, dots, gates, hidden, resid, *cots, packed, proj, prob, gain)


def normed_back_kernel(where, grad_proj, tokens, gain, packed, out, w_buf, sem_w):
    y0 = where[0]
    order = [(y0 + k) & 3 for k in (1, 3, 2, 0)]
    loads = [
        pltpu.make_async_copy(
            packed.at[pl.ds(pl.multiple_of(at * 512, 512), 512), 0:1536], w_buf.at[i], sem_w.at[i]
        )
        for i, at in enumerate(order)
    ]
    for load in loads:
        load.start()
    values = tokens[...].astype(F32)
    factor = lax.rsqrt(jnp.mean(values * values, axis=-1, keepdims=True) + EPSILON)
    inner = jnp.zeros((128, 1), F32)
    sums = []
    for i, k in enumerate((1, 3, 2, 0)):
        loads[i].wait()
        grad = nt(grad_proj[...], w_buf[i])
        cols = pl.ds(pl.multiple_of(order[i] * 512, 512), 512)
        unit = tokens[:, cols].astype(F32) * factor
        inner = inner + jnp.sum(grad * unit * gain[:, cols], axis=-1, keepdims=True)
        sums.append(jnp.sum(grad * unit, axis=0, keepdims=True))
        out[k, 0:128, 0:512] = grad.astype(BF16)
    lane = lax.broadcasted_iota(jnp.int32, (128, 128), 1)
    high = inner.astype(BF16).astype(F32)
    both = jnp.where(lane == 0, high, jnp.where(lane == 1, inner - high, 0.0)).astype(BF16)
    row = lax.broadcasted_iota(jnp.int32, (16, 512), 0)
    table = jnp.zeros((16, 512), F32)
    for at, piece in zip(order, sums):
        top = piece.astype(BF16).astype(F32)
        table = jnp.where(row == at, top, jnp.where(row == at + 4, piece - top, table))
    for k in range(4):
        out[k, 0:128, 512:] = both
        out[k, 128:, 0:512] = table.astype(BF16)
        out[k, 128:, 512:] = jnp.zeros((16, 128), BF16)


def normed_back_call(where, grad_proj, tokens, gain, packed):
    return pl.pallas_call(
        normed_back_kernel,
        out_shape=jax.ShapeDtypeStruct((4, 144, 640), BF16),
        in_specs=[spec(pltpu.SMEM), spec(VMEM), spec(VMEM), spec(VMEM), spec(ANY)],
        out_specs=spec(VMEM),
        scratch_shapes=[VMEM((4, 512, 1536), BF16), pltpu.SemaphoreType.DMA((4,))],
        compiler_params=params(40),
        cost_estimate=cost(10**9, 8 * 10**6),
        name="normed_back",
    )(where, grad_proj, tokens, gain, packed)


def expert_kernel(where, x_own, x_other, g0, g1, g2, g3, code, weights, router, gain,
                  sent_own, sent_other, h_out, g_out, mid, gates_out,
                  x_buf, g_buf, w_buf, h_buf, d_buf, r_buf, sem_r, sem_x, sem_g, sem_w, sem_h, sem_go, sem_d):
    y = where[0]; me = where[1]
    xs = (x_own, x_other); gs = (g0,g1,g2,g3)
    rows, part, parts = 128, 512, 4
    width = 2048; block = 512; experts = 16
    offs = [pl.multiple_of(((y + k) & 3) * part, part) for k in range(4)]
    x_copies = [pltpu.make_async_copy(xs[b], x_buf.at[b], sem_x.at[b]) for b in range(2)]
    x_copies[0].start()
    w_copies = [pltpu.make_async_copy(weights.at[pl.ds(2*i,2)], w_buf.at[pl.ds(2*i,2)], sem_w.at[i]) for i in range(3)]
    w_copies[0].start(); w_copies[1].start()
    r_copy = pltpu.make_async_copy(router.at[:, 2048:2176], r_buf, sem_r)
    r_copy.start()
    g_copies = [[pltpu.make_async_copy(gs[k].at[pl.ds(b*block,block)], g_buf.at[pl.ds(b*block,block), pl.ds(offs[k],part)], sem_g.at[b,k]) for k in range(4)] for b in range(2)]
    for c in g_copies[0]: c.start()
    w_copies[2].start()
    x_copies[1].start()
    for c in g_copies[1]: c.start()
    h_copies=[]; go_copies=[]; d_copies=[]
    lane = lax.broadcasted_iota(jnp.int32, (block, 128), 1)
    for b in range(2):
        x_copies[b].wait()
        def norm(r, _):
            ssq = jnp.zeros((rows,1), F32)
            for k in range(4):
                v = x_buf[b, r, k].astype(F32)
                ssq = ssq + jnp.sum(v*v, axis=-1, keepdims=True)
            f = lax.rsqrt(ssq * (1.0/width) + EPSILON)
            for k in range(4):
                gk = gain[pl.ds((y+k)&3, 1), :]
                h_buf[pl.ds(pl.multiple_of(b*block + r*rows, rows), rows), pl.ds(offs[k], part)] = (x_buf[b, r, k].astype(F32) * f * gk).astype(BF16)
            return 0
        lax.fori_loop(0, 4, norm, 0)
        here = pl.ds(b*block, block)
        hc = pltpu.make_async_copy(h_buf.at[here], h_out.at[here], sem_h.at[b]); hc.start(); h_copies.append(hc)
        if b == 0:
            r_copy.wait()
        logits = jnp.dot(h_buf[here,:], r_buf[...], preferred_element_type=F32)
        codes = code[here,:].astype(F32)
        chosen = codes > 0.5
        top = jnp.max(jnp.where(chosen, logits, -jnp.inf), axis=-1, keepdims=True)
        lifted = jnp.where(chosen, jnp.exp(logits - top), 0.0)
        gates = lifted / jnp.sum(lifted, axis=-1, keepdims=True)
        if b == 0:
            gates_out[...] = gates[:rows]
        used = jnp.where(codes > 1.5, gates, 0.0)
        dots = jnp.zeros((block,128), F32)
        for c in g_copies[b]: c.wait()
        gc = pltpu.make_async_copy(g_buf.at[here], g_out.at[here], sem_go.at[b]); gc.start(); go_copies.append(gc)
        if b == 0:
            w_copies[0].wait(); w_copies[1].wait(); w_copies[2].wait()
        for e in range(2):
            mine = lane == me*2 + e
            use = jnp.sum(jnp.where(mine, used, 0.0), axis=-1, keepdims=True)
            keep = jnp.sum(jnp.where(mine & (codes > 1.5), 1.0, 0.0), axis=-1, keepdims=True)
            h = h_buf[here,:]
            u = jnp.dot(h, w_buf[e], preferred_element_type=F32)
            w = jnp.dot(h, w_buf[2+e], preferred_element_type=F32)
            z = jnp.dot(g_buf[here,:], w_buf[4+e], preferred_element_type=F32)
            s = 1.0/(1.0+jnp.exp(-u))
            silu = u*s
            act = silu*w
            dot = jnp.sum(z*act, axis=-1, keepdims=True)*keep
            high = dot.astype(BF16).astype(F32)
            dots = jnp.where(mine, high, dots)
            dots = jnp.where(lane == me*2 + e + experts, dot-high, dots)
            z = z*use
            cols = pl.ds(e*256,256)
            mid[0, here, cols] = (z*w*s*(1.0+u*(1.0-s))).astype(BF16)
            mid[1, here, cols] = (z*silu).astype(BF16)
            mid[2, here, cols] = (act*use).astype(BF16)
        dots = dots.astype(BF16)
        for k in range(4):
            acc = None
            for e in range(2):
                cols = pl.ds(e*256,256)
                for m in range(2):
                    t = nt(mid[m, here, cols], w_buf[2*m+e, pl.ds(offs[k],part), :])
                    acc = t if acc is None else acc + t
            acc = acc.astype(BF16)
            for r in range(4):
                d_buf[b,k,r,:,0:part] = acc[r*rows:(r+1)*rows]
                d_buf[b,k,r,:,part:] = dots[r*rows:(r+1)*rows]
            dc = pltpu.make_async_copy(d_buf.at[b,k], (sent_own, sent_other)[b].at[k], sem_d.at[b,k]); dc.start(); d_copies.append(dc)
    for c in h_copies+go_copies+d_copies: c.wait()


def experts_call(where, x_own, x_other, gs, code, weights, router, gain):
    S=jax.ShapeDtypeStruct
    return pl.pallas_call(
        expert_kernel,
        out_shape=(S((4,4,128,640),BF16), S((4,4,128,640),BF16), S((1024,2048),BF16), S((1024,2048),BF16), S((3,1024,512),BF16), S((128,128),F32)),
        in_specs=[pl.BlockSpec(memory_space=pltpu.SMEM)]+[pl.BlockSpec(memory_space=ANY)]*6+[pl.BlockSpec(memory_space=VMEM), pl.BlockSpec(memory_space=ANY), pl.BlockSpec(memory_space=ANY), pl.BlockSpec(memory_space=VMEM)],
        out_specs=(pl.BlockSpec(memory_space=ANY),)*4+(pl.BlockSpec(memory_space=VMEM),)*2,
        scratch_shapes=[VMEM((2,4,4,128,512),BF16), VMEM((1024,2048),BF16), VMEM((6,2048,256),BF16), VMEM((1024,2048),BF16), VMEM((2,4,4,128,640),BF16), VMEM((2048,128),BF16), pltpu.SemaphoreType.DMA,
            pltpu.SemaphoreType.DMA((2,)),pltpu.SemaphoreType.DMA((2,4)),pltpu.SemaphoreType.DMA((3,)),pltpu.SemaphoreType.DMA((2,)),pltpu.SemaphoreType.DMA((2,)),pltpu.SemaphoreType.DMA((2,4))],
        compiler_params=pltpu.CompilerParams(vmem_limit_bytes=56*1024*1024),
        cost_estimate=pl.CostEstimate(flops=11*10**9, bytes_accessed=28*10**6, transcendentals=10**6),
        name="experts",
    )(where, x_own, x_other, *gs, code, weights, router, gain)

def grads_kernel(h, g, mid, out):
    for i, src in ((0,h),(1,h),(2,g)):
        t = tn(src[...], mid[i])
        for e in range(2):
            out[0, 2*i+e] = t[:, e*256:(e+1)*256].astype(BF16)

def grads_call(h, g, mid):
    S=jax.ShapeDtypeStruct
    return pl.pallas_call(grads_kernel, grid=(4,),
        out_shape=S((4,6,512,256),BF16),
        in_specs=[pl.BlockSpec((1024,512),lambda j:(0,j)),pl.BlockSpec((1024,512),lambda j:(0,j)),pl.BlockSpec((3,1024,512),lambda j:(0,0,0))],
        out_specs=pl.BlockSpec((1,6,512,256),lambda j:(j,0,0,0)),
        compiler_params=pltpu.CompilerParams(vmem_limit_bytes=56*1024*1024),
        cost_estimate=pl.CostEstimate(flops=7*10**9, bytes_accessed=18*10**6, transcendentals=0),
        name="grads")(h,g,mid)

def rows_kernel(mid, w, own, other):
    acc = nt(mid[0, :, 0:256], w[0]) + nt(mid[0, :, 256:512], w[1])
    own[...] = acc[:512].astype(BF16)
    other[...] = acc[512:].astype(BF16)


def rows_call(mid, weights):
    shape = jax.ShapeDtypeStruct
    return pl.pallas_call(
        rows_kernel,
        grid=(4,),
        out_shape=(shape((512, 2048), BF16),) * 2,
        in_specs=[
            pl.BlockSpec((1, 1024, 512), lambda j: (2, 0, 0)),
            pl.BlockSpec((2, 512, 256), lambda j: (2, j, 0)),
        ],
        out_specs=(pl.BlockSpec((512, 512), lambda j: (0, j)),) * 2,
        compiler_params=params(56),
        cost_estimate=cost(2 * 10**9, 7 * 10**6),
        name="rows",
    )(mid, weights)


def local(
    tokens,
    cotangent,
    seq_lengths,
    deal_order,
    expert_ids,
    slot_order,
    qkv_weight,
    out_weight,
    router_weight,
    gate_weight,
    up_weight,
    down_weight,
    gain_first,
    gain_second,
):
    rows, width = tokens.shape
    zc = ("z", "core")
    peers = lax.axis_size("z") * lax.axis_size("core")
    tensors = lax.axis_size("tensor")
    dps = lax.axis_size("dp")
    zs = lax.axis_size("z")
    share = rows // peers
    part = width // tensors
    me_core = lax.axis_index("core")
    me_z = lax.axis_index("z")
    me = me_z * 2 + me_core
    me_y = lax.axis_index("tensor")
    experts = router_weight.shape[0]
    top = expert_ids.shape[1]
    capacity = (5 * rows * top + 4 * experts - 1) // (4 * experts)
    here = gate_weight.shape[0]
    head_width = qkv_weight.shape[2]
    feats = qkv_weight.shape[1]

    place_now = jnp.stack([me_y, me]).astype(jnp.int32)

    packed = lax.all_gather(
        pack_call(qkv_weight, out_weight, router_weight), ("dp", "z", "core"), axis=0, tiled=True
    )
    expert_local = jnp.concatenate([gate_weight, up_weight, down_weight], axis=0)

    dest_group = deal_order // rows % peers
    place = dest_group * share + (deal_order % rows - me * share)
    deal_matrix = (place[None, :] == jnp.arange(rows, dtype=jnp.int32)[:, None]).astype(BF16)
    dealt = jnp.dot(deal_matrix, tokens, preferred_element_type=F32).astype(BF16)
    got = lax.all_to_all(
        dealt.reshape(peers, share, width), zc, split_axis=0, concat_axis=0, tiled=True
    ).reshape(rows, width)
    cot_part = lax.dynamic_slice_in_dim(cotangent, me_y * part, part, 1)
    cot_part = jnp.dot(deal_matrix, cot_part, preferred_element_type=F32).astype(BF16)

    match = expert_ids[:, :, None] == jnp.arange(experts, dtype=jnp.int32)[None, None, :]
    order = jnp.min(jnp.where(match, slot_order[:, :, None], BIG), axis=1)
    chosen = order < BIG
    earlier = jnp.sum((order[None, :, :] < order[:, None, :]).astype(jnp.int32), axis=1)
    code = chosen.astype(F32) + (chosen & (earlier < capacity)).astype(F32)
    table = jnp.pad(code, ((0, 0), (0, 128 - experts))).astype(BF16)
    cot_own = jnp.stack(gather_near(jnp.concatenate([cot_part, table], axis=1), "z"))
    cot_block = jnp.stack([cot_own, core_swap(cot_own)]).reshape(peers * rows, part + 128)
    code_all = cot_block[:, part:]
    number = jnp.arange(peers * rows, dtype=jnp.int32)
    dest, source, inner = number // rows, number // share % peers, number % share
    dest_row = ((me_z + dest % zs) % zs * 2 + (me_core + dest // zs) % 2) * share + inner
    source_block = (source // 2 - me_z) % zs + (source + me_core) % 2 * zs
    block_matrix = ((source_block * rows + dest_row)[:, None] == number[None, :]).astype(BF16)
    cot_rows = jnp.dot(block_matrix, cot_block[:, :part], preferred_element_type=F32).astype(BF16)
    cot_near = gather_near(cot_rows, "tensor")

    segment = segment_of(seq_lengths[0], rows)
    same_seq = (segment[:, None] == segment[None, :]).astype(F32)
    normed, normed_feat = norm_call(got, gain_first.reshape(1, width))
    normed_feat = lax.all_to_all(normed_feat, zc, split_axis=0, concat_axis=0, tiled=True)
    expert_local, normed = lax.optimization_barrier((expert_local, normed))
    expert_full = lax.all_gather(expert_local, "dp", axis=1, tiled=True)
    normed, normed_feat, cot_near, code_all, packed = lax.optimization_barrier(
        (normed, normed_feat, cot_near, code_all, packed)
    )
    projected, weights, mixed, branch = attention_call(place_now, normed, same_seq, packed)
    mixed_all = lax.all_gather(mixed, zc, axis=0, tiled=True)
    resid_in = got.astype(F32)
    resid_part = lax.dynamic_slice_in_dim(resid_in, me_y * part, part, 1) + sum_near(
        branch, "tensor"
    )
    resid_near = jnp.stack(gather_near(resid_part.astype(BF16), "tensor"))
    resid_own = jnp.stack(gather_near(resid_near, "z"))
    resid_other = core_swap(resid_own)

    sent_own, sent_other, hidden, cot_all, mids, gates = experts_call(
        place_now,
        resid_own,
        resid_other,
        cot_near,
        code_all,
        expert_full,
        packed,
        gain_second.reshape(tensors, part),
    )
    rows_own, rows_other = rows_call(mids, expert_full)
    paired = (sent_own.astype(F32) + core_swap(sent_other).astype(F32)).astype(BF16)
    expert_rows = (rows_own.astype(F32) + core_swap(rows_other).astype(F32)).astype(BF16)
    expert_grads = grads_call(hidden, cot_all, mids)
    cols, expert_grads, expert_rows = lax.optimization_barrier(
        (sum_near(paired, "tensor"), expert_grads, expert_rows)
    )
    expert_rows = sum_near(expert_rows.reshape(zs, rows, width), "z").astype(BF16)
    dots = cols[..., part : part + experts] + cols[..., part + experts : part + 2 * experts]
    cols = jnp.concatenate(
        [cols[..., :part].astype(BF16), *hi_lo(dots), jnp.zeros((zs, rows, 128 - 2 * experts), BF16)], axis=-1
    )
    cols = sum_near(cols, "z")
    dots = cols[:, part : part + experts] + cols[:, part + experts : part + 2 * experts]
    dots = jnp.pad(dots, ((0, 0), (0, 128 - experts)))
    grads_near = gather_near(cols[:, :part].astype(BF16), "tensor")
    grads_near, expert_rows = lax.optimization_barrier((grads_near, expert_rows))

    branch_feat, grad_proj, grad_own = attention_back_call(
        place_now,
        grads_near,
        dots,
        gates,
        hidden,
        resid_near,
        cot_near,
        packed,
        projected,
        weights,
        gain_second.reshape(1, width),
    )
    grad_z = jnp.stack(gather_near(grad_proj, "z"))
    grad_proj_all = jnp.stack([grad_z, core_swap(grad_z)]).reshape(peers * rows, 3 * head_width)
    normed_cols = sum_near(
        normed_back_call(place_now, grad_proj, got, gain_first.reshape(1, width), packed), "tensor"
    )
    inner = normed_cols[:rows, part : part + 1] + normed_cols[:rows, part + 1 : part + 2]
    inner = inner / width
    gain_sum = (normed_cols[rows : rows + 4, :part] + normed_cols[rows + 4 : rows + 8, :part]).reshape(
        dps, peers, feats
    )
    gain_sum = gain_sum.transpose(1, 0, 2).reshape(peers, 1, dps * feats).astype(BF16)
    branch_feat = lax.dynamic_update_slice(branch_feat, gain_sum, (0, rows + 32, 0))
    branch_feat = lax.all_to_all(branch_feat, zc, split_axis=0, concat_axis=0, tiled=True)
    small = jnp.sum(branch_feat[:, rows:].astype(F32), axis=0)
    grad_out_t = lax.dot_general(
        branch_feat[:, :rows].reshape(peers * rows, dps * feats),
        mixed_all,
        (((0,), (0,)), ((), ())),
        preferred_element_type=F32,
    )

    def own_cols(table):
        return lax.dynamic_slice_in_dim(table, me_y * part, part, table.ndim - 1)

    factor_first = lax.rsqrt(jnp.mean(resid_in * resid_in, axis=-1, keepdims=True) + EPSILON)
    input_part = grad_own + factor_first * (
        normed_cols[:rows, :part] * own_cols(gain_first) - own_cols(resid_in) * factor_first * inner
    )

    expert_grads = lax.psum_scatter(expert_grads, "dp", scatter_dimension=0, tiled=False).astype(F32)

    expert_rows = ring_sum(expert_rows.reshape(rows, tensors, part).transpose(1, 0, 2), "tensor")
    output_part = resid_part + expert_rows

    final = jnp.concatenate([output_part.astype(BF16), input_part.astype(BF16)], axis=1)
    normed_feat = normed_feat.reshape(zs, 2, rows, dps * feats)
    normed_feat = jnp.stack(
        [
            lax.dynamic_slice(
                normed_feat,
                ((me_z + r % zs) % zs, (me_core + r // zs) % 2, 0, 0),
                (1, 1, rows, dps * feats),
            )
            for r in range(peers)
        ]
    ).reshape(peers * rows, dps * feats)
    grad_qkv = lax.dot_general(
        normed_feat, grad_proj_all, (((0,), (0,)), ((), ())), preferred_element_type=F32
    )
    by_dp = jnp.concatenate(
        [
            grad_qkv.astype(BF16),
            grad_out_t.astype(BF16),
            jnp.pad(small.T, ((0, 0), (0, 80))).astype(BF16),
        ],
        axis=1,
    ).reshape(dps, feats, 4 * head_width + 128)
    by_dp, final = lax.optimization_barrier((by_dp, final))
    by_dp = ring_sum(by_dp, "dp")
    back = lax.all_to_all(
        final.reshape(peers, share, 2 * part), zc, split_axis=0, concat_axis=0, tiled=True
    ).reshape(rows, 2 * part)
    final = lax.dot_general(
        deal_matrix, back, (((0,), (0,)), ((), ())), preferred_element_type=F32
    ).astype(BF16)
    qkv_grad = by_dp[:, : 3 * head_width].reshape(feats, 3, head_width).transpose(1, 0, 2)
    out_grad = by_dp[:, 3 * head_width : 4 * head_width].T
    tail = by_dp[:, 4 * head_width :]
    router_grad = tail[:, :experts].T
    gain_second_grad = tail[:, experts] + tail[:, experts + 1]
    gain_first_grad = tail[:, experts + 16]

    return (
        final[:, :part],
        final[:, part:],
        qkv_grad,
        out_grad,
        router_grad,
        expert_grads[:here],
        expert_grads[here : 2 * here],
        expert_grads[2 * here :],
        gain_first_grad,
        gain_second_grad,
    )


def solution(mesh):
    sizes = mesh.shape
    split = Mesh(
        mesh.devices.reshape(sizes["dp"], sizes["expert"] // 2, 2, sizes["tensor"]),
        ("dp", "z", "core", "tensor"),
    )
    experts = ("z", "core")
    every = ("dp", "z", "core")
    placed = (
        P(every, None),
        P(every, None),
        P(every, None),
        P(every),
        P(every, None),
        P(every, None),
        P(None, every, "tensor"),
        P("tensor", every),
        P(None, every),
        P(experts, "dp", "tensor"),
        P(experts, "dp", "tensor"),
        P(experts, "dp", "tensor"),
        P(),
        P(),
    )
    return jax.shard_map(
        local,
        mesh=split,
        in_specs=placed,
        out_specs=(
            P(every, "tensor"),
            P(every, "tensor"),
            P(None, every, "tensor"),
            P("tensor", every),
            P(None, every),
            P(experts, "dp", "tensor"),
            P(experts, "dp", "tensor"),
            P(experts, "dp", "tensor"),
            P(every),
            P(every),
        ),
        check_vma=False,
    )
```

```python
import jax
import jax.numpy as jnp
from jax import lax
from jax.sharding import Mesh
from jax.sharding import PartitionSpec as P
from jax.experimental import pallas as pl
from jax.experimental.pallas import tpu as pltpu

HEAD_DIM = 128
EPSILON = 1e-05
F32 = jnp.float32
BF16 = jnp.bfloat16
BIG = 1 << 30
VMEM = pltpu.VMEM
ANY = pl.ANY


def shift(values, axis, step):
    size = lax.axis_size(axis)
    return lax.ppermute(values, axis, [(i, (i + step) % size) for i in range(size)])


def core_swap(values):
    return lax.ppermute(values, "core", [(0, 1), (1, 0)])


def gather_near(values, axis):
    size = lax.axis_size(axis)
    got = {k: shift(values, axis, -k) for k in (1, size - 1, 2)}
    return [values] + [got[k] for k in range(1, size)]


def sum_near(parts, axis):
    size = lax.axis_size(axis)
    total = parts[0].astype(F32)
    for k in (1, size - 1, 2):
        total = total + shift(parts[k], axis, k).astype(F32)
    return total


def swap_near(parts, axis):
    size = lax.axis_size(axis)
    return [parts[0]] + [shift(parts[k], axis, k) for k in (1, size - 1, 2)]


def total(parts):
    return sum(part.astype(F32) for part in parts)


def segment_of(seq_lengths, row_count):
    seq_ends = jnp.cumsum(seq_lengths)
    position = jnp.arange(row_count, dtype=jnp.int32)
    return jnp.sum((position[:, None] >= seq_ends[None, :]).astype(jnp.int32), axis=1)


def nt(a,b): return lax.dot_general(a,b,(((1,),(1,)),((),())),preferred_element_type=F32)
def tn(a,b): return lax.dot_general(a,b,(((0,),(0,)),((),())),preferred_element_type=F32)

def spec(space):
    return pl.BlockSpec(memory_space=space)


def params(megabytes=62):
    return pltpu.CompilerParams(vmem_limit_bytes=megabytes * 1024 * 1024)


def cost(flops, moved):
    return pl.CostEstimate(flops=flops, bytes_accessed=moved, transcendentals=0)


def pack_kernel(qkv, out, router, packed):
    for s in range(3):
        packed[:, s * 512 : (s + 1) * 512] = qkv[s]
    packed[:, 1536:2048] = out[...]
    wide = jnp.concatenate([router[...].astype(F32), jnp.zeros((112, 64), F32)], axis=0)
    packed[:, 2048:] = wide.T.astype(BF16)


def pack_call(qkv, out, router):
    return pl.pallas_call(
        pack_kernel,
        out_shape=jax.ShapeDtypeStruct((64, 2176), BF16),
        cost_estimate=cost(1000, 6 * 10**5),
        compiler_params=params(),
        grid=(1,),
        name="pack",
    )(qkv, out, router)


def spread_features(values, out, row):
    count = values.shape[0]
    for e in range(8):
        for d in range(4):
            at = d * 512 + e * 64
            out[e, row : row + count, d * 64 : (d + 1) * 64] = values[:, at : at + 64]


def norm_kernel(tokens, gain, normed_out, feat_out):
    values = tokens[...].astype(F32)
    factor = lax.rsqrt(jnp.mean(values * values, axis=-1, keepdims=True) + EPSILON)
    normed = (values * factor * gain[...]).astype(BF16)
    normed_out[...] = normed
    spread_features(normed, feat_out, 0)


def norm_call(tokens, gain):
    shape = jax.ShapeDtypeStruct
    return pl.pallas_call(
        norm_kernel,
        out_shape=(shape((128, 2048), BF16), shape((8, 128, 256), BF16)),
        cost_estimate=cost(10**6, 15 * 10**5),
        compiler_params=params(),
        grid=(1,),
        name="norm",
    )(tokens, gain)


def attention_kernel(
    where, normed, same, packed, proj_out, prob_out, mixed_out, branch, w_buf, o_buf, sem_w, sem_o
):
    y0 = where[0]
    loads = [
        pltpu.make_async_copy(packed.at[:, s * 512 : (s + 1) * 512], w_buf.at[s], sem_w.at[s])
        for s in range(3)
    ]
    for load in loads:
        load.start()
    out_load = pltpu.make_async_copy(packed.at[:, 1536:2048], o_buf, sem_o)
    out_load.start()
    for s in range(3):
        loads[s].wait()
        proj_out[s] = jnp.dot(normed[...], w_buf[s], preferred_element_type=F32).astype(BF16)
    mask = same[...] > 0.5
    scale = HEAD_DIM ** (-0.5)
    for h in range(4):
        cols = slice(h * HEAD_DIM, (h + 1) * HEAD_DIM)
        scores = jnp.where(
            mask, nt(proj_out[0, :, cols], proj_out[1, :, cols]) * scale, -1000000000.0
        )
        grown = jnp.exp(scores - jnp.max(scores, axis=-1, keepdims=True))
        prob = grown / jnp.sum(grown, axis=-1, keepdims=True)
        prob_out[h] = prob
        mixed_out[:, cols] = jnp.dot(
            prob.astype(BF16), proj_out[2, :, cols], preferred_element_type=F32
        ).astype(BF16)
    out_load.wait()
    for k in range(4):
        at = pl.multiple_of(((y0 + k) & 3) * 512, 512)
        branch[k] = nt(mixed_out[...], o_buf[pl.ds(at, 512), :]).astype(BF16)


def attention_call(where, normed, same, packed):
    shape = jax.ShapeDtypeStruct
    dma = pltpu.SemaphoreType.DMA
    return pl.pallas_call(
        attention_kernel,
        out_shape=(
            shape((3, 128, 512), BF16),
            shape((4, 128, 128), F32),
            shape((128, 512), BF16),
            shape((4, 128, 512), BF16),
        ),
        in_specs=[spec(pltpu.SMEM), spec(VMEM), spec(VMEM), spec(ANY)],
        out_specs=(spec(VMEM),) * 4,
        scratch_shapes=[VMEM((3, 2048, 512), BF16), VMEM((2048, 512), BF16), dma((3,)), dma],
        compiler_params=params(),
        cost_estimate=cost(2 * 10**9, 10 * 10**6),
        grid=(1,),
        name="attention",
    )(where, normed, same, packed)


def attention_back_kernel(
    where, g0, g1, g2, g3, dots, gates, hidden, resid, cots, packed, proj_in, prob_in, gain,
    feat_out, grad_proj, own_out,
    o_buf, h_buf, c_buf, x_buf, d_buf, x_low, d_low, proj, prob, sem_o, sem_h, sem_c, sem_x, sem_d, sem_p,
):
    y0 = where[0]
    offs = [pl.multiple_of(((y0 + k) & 3) * 512, 512) for k in range(4)]
    d_loads = [
        pltpu.make_async_copy(g, d_low.at[:, pl.ds(offs[k], 512)], sem_d.at[k])
        for k, g in enumerate((g0, g1, g2, g3))
    ]
    x_loads = [
        pltpu.make_async_copy(resid.at[k], x_low.at[:, pl.ds(offs[k], 512)], sem_x.at[k])
        for k in range(4)
    ]
    h_load = pltpu.make_async_copy(hidden.at[0:128], h_buf, sem_h)
    o_load = pltpu.make_async_copy(packed.at[:, 1536:2176], o_buf, sem_o)
    c_load = pltpu.make_async_copy(cots, c_buf, sem_c)
    p_loads = [
        pltpu.make_async_copy(proj_in, proj, sem_p.at[0]),
        pltpu.make_async_copy(prob_in, prob, sem_p.at[1]),
    ]
    for load in [*x_loads, *d_loads, h_load, o_load, c_load, *p_loads]:
        load.start()
    for load in [*x_loads, *d_loads]:
        load.wait()
    x_buf[...] = x_low[...].astype(F32)
    d_buf[...] = d_low[...].astype(F32)
    share = gates[...]
    dot = dots[...]
    grad_logits = (share * (dot - jnp.sum(dot * share, axis=-1, keepdims=True))).astype(BF16)
    o_load.wait()
    h_load.wait()
    router = tn(grad_logits, h_buf[...])
    grad_hidden = d_buf[...] + nt(grad_logits, o_buf[:, 512:])
    resid_rows = x_buf[...]
    factor = lax.rsqrt(jnp.mean(resid_rows * resid_rows, axis=-1, keepdims=True) + EPSILON)
    unit = resid_rows * factor
    gain_sum = jnp.sum(grad_hidden * unit, axis=0, keepdims=True)
    scaled = grad_hidden * gain[...]
    c_load.wait()
    grad = c_buf[...].astype(F32) + factor * (
        scaled - unit * jnp.mean(scaled * unit, axis=-1, keepdims=True)
    )
    d_buf[...] = grad
    own_out[...] = d_buf[:, pl.ds(offs[0], 512)]
    low = grad.astype(BF16)
    spread_features(low, feat_out, 0)
    spread_features(router[:16].astype(BF16), feat_out, 128)
    high = gain_sum.astype(BF16)
    rest = (gain_sum - high.astype(F32)).astype(BF16)
    tail = jnp.concatenate(
        [high.astype(F32), rest.astype(F32), jnp.zeros((14, 2048), F32)], axis=0
    ).astype(BF16)
    spread_features(tail, feat_out, 144)
    mixed = jnp.dot(low, o_buf[:, :512], preferred_element_type=F32).astype(BF16)
    for load in p_loads:
        load.wait()
    scale = HEAD_DIM ** (-0.5)
    for h in range(4):
        cols = slice(h * HEAD_DIM, (h + 1) * HEAD_DIM)
        weights = prob[h]
        back = mixed[:, cols]
        grad_proj[:, 1024 + h * HEAD_DIM : 1024 + (h + 1) * HEAD_DIM] = tn(
            weights.astype(BF16), back
        ).astype(BF16)
        weight_grad = nt(back, proj[2, :, cols])
        offset = jnp.sum(weight_grad * weights, axis=-1, keepdims=True)
        score = (weights * (weight_grad - offset)).astype(BF16)
        grad_proj[:, cols] = (
            jnp.dot(score, proj[1, :, cols], preferred_element_type=F32) * scale
        ).astype(BF16)
        grad_proj[:, 512 + h * HEAD_DIM : 512 + (h + 1) * HEAD_DIM] = (
            tn(score, proj[0, :, cols]) * scale
        ).astype(BF16)


def attention_back_call(where, grads, dots, gates, hidden, resid, cots, packed, proj, prob, gain):
    shape = jax.ShapeDtypeStruct
    dma = pltpu.SemaphoreType.DMA
    return pl.pallas_call(
        attention_back_kernel,
        out_shape=(
            shape((8, 160, 256), BF16),
            shape((128, 1536), BF16),
            shape((128, 512), F32),
        ),
        in_specs=[spec(pltpu.SMEM)]
        + [spec(ANY)] * 4
        + [spec(VMEM)] * 2
        + [spec(ANY)] * 6
        + [spec(VMEM)],
        out_specs=(spec(VMEM),) * 3,
        scratch_shapes=[
            VMEM((2048, 640), BF16),
            VMEM((128, 2048), BF16),
            VMEM((128, 2048), BF16),
            VMEM((128, 2048), F32),
            VMEM((128, 2048), F32),
            VMEM((128, 2048), BF16),
            VMEM((128, 2048), BF16),
            VMEM((3, 128, 512), BF16),
            VMEM((4, 128, 128), F32),
            dma,
            dma,
            dma,
            dma((4,)),
            dma((4,)),
            dma((2,)),
        ],
        compiler_params=params(),
        cost_estimate=cost(10**9, 6 * 10**6),
        grid=(1,),
        name="attention_back",
    )(where, *grads, dots, gates, hidden, resid, cots, packed, proj, prob, gain)


def normed_back_kernel(where, grad_proj, tokens, gain, packed, o0, o1, o2, o3, w_buf, sem_w):
    y0 = where[0]
    outs = (o0, o1, o2, o3)
    order = [(y0 + k) & 3 for k in (1, 3, 2, 0)]
    loads = [
        pltpu.make_async_copy(
            packed.at[pl.ds(pl.multiple_of(at * 512, 512), 512), 0:1536], w_buf.at[i], sem_w.at[i]
        )
        for i, at in enumerate(order)
    ]
    for load in loads:
        load.start()
    values = tokens[...].astype(F32)
    factor = lax.rsqrt(jnp.mean(values * values, axis=-1, keepdims=True) + EPSILON)
    inner = jnp.zeros((128, 1), F32)
    sums = []
    for i, k in enumerate((1, 3, 2, 0)):
        loads[i].wait()
        grad = nt(grad_proj[...], w_buf[i])
        cols = pl.ds(pl.multiple_of(order[i] * 512, 512), 512)
        unit = tokens[:, cols].astype(F32) * factor
        inner = inner + jnp.sum(grad * unit * gain[:, cols], axis=-1, keepdims=True)
        sums.append(jnp.sum(grad * unit, axis=0, keepdims=True))
        outs[k][0:128, 0:512] = grad.astype(BF16)
    lane = lax.broadcasted_iota(jnp.int32, (128, 128), 1)
    high = inner.astype(BF16).astype(F32)
    both = jnp.where(lane == 0, high, jnp.where(lane == 1, inner - high, 0.0)).astype(BF16)
    row = lax.broadcasted_iota(jnp.int32, (16, 512), 0)
    table = jnp.zeros((16, 512), F32)
    for at, piece in zip(order, sums):
        top = piece.astype(BF16).astype(F32)
        table = jnp.where(row == at, top, jnp.where(row == at + 4, piece - top, table))
    for out in outs:
        out[0:128, 512:] = both
        out[128:, 0:512] = table.astype(BF16)
        out[128:, 512:] = jnp.zeros((16, 128), BF16)


def normed_back_call(where, grad_proj, tokens, gain, packed):
    return pl.pallas_call(
        normed_back_kernel,
        out_shape=(jax.ShapeDtypeStruct((144, 640), BF16),) * 4,
        in_specs=[spec(pltpu.SMEM), spec(VMEM), spec(VMEM), spec(VMEM), spec(ANY)],
        out_specs=(spec(VMEM),) * 4,
        scratch_shapes=[VMEM((4, 512, 1536), BF16), pltpu.SemaphoreType.DMA((4,))],
        compiler_params=params(),
        cost_estimate=cost(10**9, 8 * 10**6),
        grid=(1,),
        name="normed_back",
    )(where, grad_proj, tokens, gain, packed)


def pair_kernel(own, other, *outs):
    for k, out in enumerate(outs):
        out[...] = own[k] + other[k]


def pair_call(own, other):
    shape = own.shape[1:]
    block = (shape[0] // 4,) + shape[1:]
    rest = (0,) * (len(shape) - 1)
    return pl.pallas_call(
        pair_kernel,
        out_shape=(jax.ShapeDtypeStruct(shape, BF16),) * 4,
        grid=(4,),
        in_specs=[pl.BlockSpec((4,) + block, lambda i: (0, i) + rest)] * 2,
        out_specs=(pl.BlockSpec(block, lambda i: (i,) + rest),) * 4,
        compiler_params=params(),
        cost_estimate=cost(10**6, 6 * own.size),
        name="pair",
    )(own, other)


def gather_dots(total):
    lane = lax.broadcasted_iota(jnp.int32, total.shape, 1)
    return jnp.where(lane < 16, total + pltpu.roll(total, 112, 1), 0.0)


def split_dots(dots):
    high = dots.astype(BF16).astype(F32)
    return high + pltpu.roll(dots - high, 16, 1)


def combine_kernel(p0, p1, p2, p3, *outs):
    for r, out in enumerate(outs):
        total = (p0[r].astype(F32) + p1[r].astype(F32)) + (p2[r].astype(F32) + p3[r].astype(F32))
        out[:, :512] = total[:, :512].astype(BF16)
        out[:, 512:] = split_dots(gather_dots(total[:, 512:])).astype(BF16)


def combine_call(pieces):
    return pl.pallas_call(
        combine_kernel,
        out_shape=(jax.ShapeDtypeStruct((128, 640), BF16),) * 4,
        grid=(4,),
        in_specs=[pl.BlockSpec((4, 32, 640), lambda i: (0, i, 0))] * 4,
        out_specs=(pl.BlockSpec((32, 640), lambda i: (i, 0)),) * 4,
        compiler_params=params(),
        cost_estimate=cost(10**6, 3 * 10**6),
        name="combine",
    )(*pieces)


def finish_kernel(p0, p1, p2, p3, cols, dots):
    total = (p0[...].astype(F32) + p1[...].astype(F32)) + (p2[...].astype(F32) + p3[...].astype(F32))
    cols[...] = total[:, :512].astype(BF16)
    dots[...] = gather_dots(total[:, 512:])


def finish_call(pieces):
    shape = jax.ShapeDtypeStruct
    return pl.pallas_call(
        finish_kernel,
        out_shape=(shape((128, 512), BF16), shape((128, 128), F32)),
        cost_estimate=cost(10**6, 10**6),
        compiler_params=params(),
        grid=(1,),
        name="finish",
    )(*pieces)


def columns_kernel(where, p0, p1, p2, p3, *outs):
    y0 = where[0]
    for k, out in enumerate(outs):
        cols = pl.ds(pl.multiple_of(((y0 + k) & 3) * 512, 512), 512)
        total = (p0[:, cols].astype(F32) + p1[:, cols].astype(F32)) + (
            p2[:, cols].astype(F32) + p3[:, cols].astype(F32)
        )
        out[...] = total.astype(BF16)


def columns_call(where, pieces):
    return pl.pallas_call(
        columns_kernel,
        out_shape=(jax.ShapeDtypeStruct((128, 512), BF16),) * 4,
        grid=(4,),
        in_specs=[spec(pltpu.SMEM)] + [pl.BlockSpec((32, 2048), lambda i: (i, 0))] * 4,
        out_specs=(pl.BlockSpec((32, 512), lambda i: (i, 0)),) * 4,
        compiler_params=params(),
        cost_estimate=cost(10**6, 3 * 10**6),
        name="columns",
    )(where, *pieces)


def tail_kernel(
    where, normed, own, other, branch, mixed, o0, o1, o2, o3, n_buf, p_buf, a_buf, sem
):
    me, d0 = where[1], where[2]
    loads = [
        pltpu.make_async_copy(piece.at[r], p_buf.at[pl.ds((c * 4 + r) * 128, 128)], sem.at[c, r])
        for c, piece in enumerate((own, other))
        for r in range(4)
    ]
    for load in loads:
        load.start()
    for r in range(8):
        at = (((me >> 1) + (r & 3)) & 3) * 2 + (((me & 1) + (r >> 2)) & 1)
        n_buf[r * 128 : (r + 1) * 128] = normed[at]
    a_buf[:, 1536:2048] = tn(branch[:, 0:128, :].reshape(1024, 256), mixed[...])
    small = jnp.sum(branch[:, 128:160, :].astype(F32), axis=0)
    a_buf[:, 2048:] = jnp.concatenate([small, jnp.zeros((96, 256), F32)], axis=0).T
    for load in loads:
        load.wait()
    for s in range(3):
        a_buf[:, s * 512 : (s + 1) * 512] = tn(n_buf[...], p_buf[:, s * 512 : (s + 1) * 512])
    for k, out in enumerate((o0, o1, o2, o3)):
        out[...] = a_buf[pl.ds(pl.multiple_of(((d0 + k) & 3) * 64, 64), 64), :].astype(BF16)


def tail_call(where, normed, own, other, branch, mixed):
    dma = pltpu.SemaphoreType.DMA
    return pl.pallas_call(
        tail_kernel,
        out_shape=(jax.ShapeDtypeStruct((64, 2176), BF16),) * 4,
        in_specs=[spec(pltpu.SMEM), spec(VMEM), spec(ANY), spec(ANY)] + [spec(VMEM)] * 2,
        out_specs=(spec(VMEM),) * 4,
        scratch_shapes=[
            VMEM((1024, 256), BF16),
            VMEM((1024, 1536), BF16),
            VMEM((256, 2176), F32),
            dma((2, 4)),
        ],
        compiler_params=params(),
        cost_estimate=cost(10**9, 8 * 10**6),
        grid=(1,),
        name="tail",
    )(where, normed, own, other, branch, mixed)


def block_row(me, r, s):
    group = (((me >> 1) + (r & 3)) & 3) * 2 + (((me & 1) + (r >> 2)) & 1)
    source = (((s >> 1) - (me >> 1)) & 3) + (((s & 1) + (me & 1)) & 1) * 4
    return pl.multiple_of(r * 128 + s * 16, 16), pl.multiple_of(source * 128 + group * 16, 16)


def back_kernel(
    where, g_own, g_other, w0, w1, w2, w3, g_out, back, own_rows, w_out,
    g_buf, w_buf, z_buf, sem_g, sem_w, sem_o,
):
    y0, me = where[0], where[1]
    offs = [pl.multiple_of(((y0 + k) & 3) * 512, 512) for k in range(4)]
    loads = [
        pltpu.make_async_copy(
            piece.at[k], g_buf.at[pl.ds(c * 512, 512), pl.ds(offs[k], 512)], sem_g.at[c, k]
        )
        for c, piece in enumerate((g_own, g_other))
        for k in range(4)
    ]
    w_loads = [
        pltpu.make_async_copy(
            piece,
            w_buf.at[:, pl.ds(pl.multiple_of(((where[2] + k) & 3) * 512, 512), 512), :],
            sem_w.at[k],
        )
        for k, piece in enumerate((w0, w1, w2, w3))
    ]
    for load in loads + w_loads:
        load.start()
    for load in loads:
        load.wait()
    out = pltpu.make_async_copy(g_buf, g_out, sem_o.at[0])
    out.start()
    for load in w_loads:
        load.wait()
    down_out = pltpu.make_async_copy(w_buf, w_out, sem_o.at[1])
    down_out.start()
    for e in range(2):
        z_buf[:, e * 256 : (e + 1) * 256] = jnp.dot(g_buf[...], w_buf[e], preferred_element_type=F32)

    def move(i, _):
        to, at = block_row(me, i >> 3, i & 7)
        back[pl.ds(to, 16), :] = z_buf[pl.ds(at, 16), :]
        return 0

    lax.fori_loop(0, 64, move, 0)
    for s in range(8):
        _, at = block_row(me, 0, s)
        own_rows[s * 16 : (s + 1) * 16, :] = g_buf[pl.ds(at, 16), :]
    out.wait()
    down_out.wait()


def back_call(where, g_own, g_other, down):
    shape = jax.ShapeDtypeStruct
    dma = pltpu.SemaphoreType.DMA
    return pl.pallas_call(
        back_kernel,
        out_shape=(shape((1024, 2048), BF16), shape((1024, 512), F32), shape((128, 2048), BF16), shape((2, 2048, 256), BF16)),
        in_specs=[spec(pltpu.SMEM)] + [spec(ANY)] * 6,
        out_specs=(spec(ANY), spec(VMEM), spec(VMEM), spec(ANY)),
        scratch_shapes=[
            VMEM((1024, 2048), BF16),
            VMEM((2, 2048, 256), BF16),
            VMEM((1024, 512), F32),
            dma((2, 4)),
            dma((4,)),
            dma((2,)),
        ],
        compiler_params=params(),
        cost_estimate=cost(2 * 10**9, 13 * 10**6),
        grid=(1,),
        name="back",
    )(where, g_own, g_other, *down)


def expert_kernel(
    where, x_own, x_other, back, code, weights, packed, gain,
    sent_own, sent_other, h_out, mid_out, source_out, gates_out,
    x_buf, b_buf, w_buf, h_buf, d_buf, r_buf, mid, by_source,
    sem_x, sem_b, sem_w, sem_r, sem_h, sem_m, sem_d,
):
    y0, me = where[0], where[1]
    offs = [pl.multiple_of(((y0 + k) & 3) * 512, 512) for k in range(4)]
    x_loads = [
        pltpu.make_async_copy(piece, x_buf.at[b], sem_x.at[b])
        for b, piece in enumerate((x_own, x_other))
    ]
    w_load = pltpu.make_async_copy(weights.at[pl.ds(0, 4)], w_buf, sem_w)
    r_load = pltpu.make_async_copy(packed.at[:, 2048:2176], r_buf, sem_r)
    b_load = pltpu.make_async_copy(back, b_buf, sem_b)
    x_loads[0].start()
    r_load.start()
    w_load.start()
    b_load.start()
    x_loads[1].start()
    stores = []
    lane = lax.broadcasted_iota(jnp.int32, (512, 128), 1)
    for b in range(2):
        x_loads[b].wait()

        def norm(r, _):
            square = jnp.zeros((128, 1), F32)
            for k in range(4):
                value = x_buf[b, r, k].astype(F32)
                square = square + jnp.sum(value * value, axis=-1, keepdims=True)
            factor = lax.rsqrt(square * (1.0 / 2048) + EPSILON)
            at = pl.ds(pl.multiple_of(b * 512 + r * 128, 128), 128)
            for k in range(4):
                part = gain[pl.ds((y0 + k) & 3, 1), :]
                h_buf[at, pl.ds(offs[k], 512)] = (x_buf[b, r, k].astype(F32) * factor * part).astype(BF16)
            return 0

        lax.fori_loop(0, 4, norm, 0)
        here = pl.ds(b * 512, 512)
        stores.append(pltpu.make_async_copy(h_buf.at[here], h_out.at[here], sem_h.at[b]))
        stores[-1].start()
        if b == 0:
            r_load.wait()
        logits = jnp.dot(h_buf[here, :], r_buf[...], preferred_element_type=F32)
        codes = code[here, :].astype(F32)
        chosen = codes > 0.5
        top = jnp.max(jnp.where(chosen, logits, -jnp.inf), axis=-1, keepdims=True)
        lifted = jnp.where(chosen, jnp.exp(logits - top), 0.0)
        gates = lifted / jnp.sum(lifted, axis=-1, keepdims=True)
        if b == 0:
            gates_out[...] = gates[:128]
            w_load.wait()
            b_load.wait()
        used = jnp.where(codes > 1.5, gates, 0.0)
        dots = jnp.zeros((512, 128), F32)
        for e in range(2):
            mine = lane == me * 2 + e
            use = jnp.sum(jnp.where(mine, used, 0.0), axis=-1, keepdims=True)
            keep = jnp.sum(jnp.where(mine & (codes > 1.5), 1.0, 0.0), axis=-1, keepdims=True)
            cols = pl.ds(e * 256, 256)
            u = jnp.dot(h_buf[here, :], w_buf[e], preferred_element_type=F32)
            w = jnp.dot(h_buf[here, :], w_buf[2 + e], preferred_element_type=F32)
            z = b_buf[here, cols]
            s = 1.0 / (1.0 + jnp.exp(-u))
            silu = u * s
            act = silu * w
            dot = jnp.sum(z * act, axis=-1, keepdims=True) * keep
            high = dot.astype(BF16).astype(F32)
            dots = jnp.where(mine, high, dots)
            dots = jnp.where(lane == me * 2 + e + 16, dot - high, dots)
            z = z * use
            mid[0, here, cols] = (z * w * s * (1.0 + u * (1.0 - s))).astype(BF16)
            mid[1, here, cols] = (z * silu).astype(BF16)
            mid[2, here, cols] = (act * use).astype(BF16)
        dots = dots.astype(BF16)
        for k in range(4):
            acc = None
            for e in range(2):
                for m in range(2):
                    term = nt(mid[m, here, pl.ds(e * 256, 256)], w_buf[2 * m + e, pl.ds(offs[k], 512), :])
                    acc = term if acc is None else acc + term
            acc = acc.astype(BF16)
            for r in range(4):
                d_buf[b, k, r, :, 0:512] = acc[r * 128 : (r + 1) * 128]
                d_buf[b, k, r, :, 512:] = dots[r * 128 : (r + 1) * 128]
            target = (sent_own, sent_other)[b].at[k]
            stores.append(pltpu.make_async_copy(d_buf.at[b, k], target, sem_d.at[b, k]))
            stores[-1].start()
    stores.append(pltpu.make_async_copy(mid, mid_out, sem_m.at[0]))
    stores[-1].start()

    def move(i, _):
        at, to = block_row(me, i >> 3, i & 7)
        by_source[pl.ds(to, 16), :] = mid[2, pl.ds(at, 16), :]
        return 0

    lax.fori_loop(0, 64, move, 0)
    stores.append(pltpu.make_async_copy(by_source, source_out, sem_m.at[1]))
    stores[-1].start()
    for store in stores:
        store.wait()


def experts_call(where, x_own, x_other, back, code, weights, packed, gain):
    shape = jax.ShapeDtypeStruct
    dma = pltpu.SemaphoreType.DMA
    return pl.pallas_call(
        expert_kernel,
        out_shape=(
            shape((4, 4, 128, 640), BF16),
            shape((4, 4, 128, 640), BF16),
            shape((1024, 2048), BF16),
            shape((3, 1024, 512), BF16),
            shape((1024, 512), BF16),
            shape((128, 128), F32),
        ),
        in_specs=[spec(pltpu.SMEM)]
        + [spec(ANY)] * 3
        + [spec(VMEM)]
        + [spec(ANY)] * 2
        + [spec(VMEM)],
        out_specs=(spec(ANY),) * 5 + (spec(VMEM),),
        scratch_shapes=[
            VMEM((2, 4, 4, 128, 512), BF16),
            VMEM((1024, 512), F32),
            VMEM((4, 2048, 256), BF16),
            VMEM((1024, 2048), BF16),
            VMEM((2, 4, 4, 128, 640), BF16),
            VMEM((2048, 128), BF16),
            VMEM((3, 1024, 512), BF16),
            VMEM((1024, 512), BF16),
            dma((2,)),
            dma,
            dma,
            dma,
            dma((2,)),
            dma((2,)),
            dma((2, 4)),
        ],
        compiler_params=params(),
        cost_estimate=cost(9 * 10**9, 26 * 10**6),
        grid=(1,),
        name="experts",
    )(where, x_own, x_other, back, code, weights, packed, gain)


def grads_kernel(h, g, mid, by_source, out):
    for i, (rows, cols) in enumerate(((h, mid[0]), (h, mid[1]), (g, by_source[...]))):
        grad = tn(rows[...], cols)
        for e in range(2):
            out[0, 2 * i + e] = grad[:, e * 256 : (e + 1) * 256].astype(BF16)


def grads_call(h, g, mid, by_source):
    return pl.pallas_call(
        grads_kernel,
        grid=(4,),
        out_shape=jax.ShapeDtypeStruct((4, 6, 512, 256), BF16),
        in_specs=[
            pl.BlockSpec((1024, 512), lambda j: (0, j)),
            pl.BlockSpec((1024, 512), lambda j: (0, j)),
            pl.BlockSpec((2, 1024, 512), lambda j: (0, 0, 0)),
            pl.BlockSpec((1024, 512), lambda j: (0, 0)),
        ],
        out_specs=pl.BlockSpec((1, 6, 512, 256), lambda j: (j, 0, 0, 0)),
        compiler_params=params(),
        cost_estimate=cost(7 * 10**9, 18 * 10**6),
        name="grads",
    )(h, g, mid, by_source)


def rows_kernel(mid, w, own, other):
    acc = nt(mid[0, :, 0:256], w[0]) + nt(mid[0, :, 256:512], w[1])
    own[...] = acc[:512].astype(BF16)
    other[...] = acc[512:].astype(BF16)


def rows_call(mid, weights):
    shape = jax.ShapeDtypeStruct
    return pl.pallas_call(
        rows_kernel,
        grid=(4,),
        out_shape=(shape((512, 2048), BF16),) * 2,
        in_specs=[
            pl.BlockSpec((1, 1024, 512), lambda j: (2, 0, 0)),
            pl.BlockSpec((2, 512, 256), lambda j: (0, j, 0)),
        ],
        out_specs=(pl.BlockSpec((512, 512), lambda j: (0, j)),) * 2,
        compiler_params=params(),
        cost_estimate=cost(2 * 10**9, 7 * 10**6),
        name="rows",
    )(mid, weights)


def local(
    tokens,
    cotangent,
    seq_lengths,
    deal_order,
    expert_ids,
    slot_order,
    qkv_weight,
    out_weight,
    router_weight,
    gate_weight,
    up_weight,
    down_weight,
    gain_first,
    gain_second,
):
    rows, width = tokens.shape
    zc = ("z", "core")
    peers = lax.axis_size("z") * lax.axis_size("core")
    tensors = lax.axis_size("tensor")
    dps = lax.axis_size("dp")
    zs = lax.axis_size("z")
    share = rows // peers
    part = width // tensors
    me_core = lax.axis_index("core")
    me_z = lax.axis_index("z")
    me = me_z * 2 + me_core
    me_y = lax.axis_index("tensor")
    experts = router_weight.shape[0]
    top = expert_ids.shape[1]
    capacity = (5 * rows * top + 4 * experts - 1) // (4 * experts)
    here = gate_weight.shape[0]
    head_width = qkv_weight.shape[2]
    feats = qkv_weight.shape[1]

    place_now = jnp.stack([me_y, me, lax.axis_index("dp")]).astype(jnp.int32)

    packed = lax.all_gather(
        pack_call(qkv_weight, out_weight.T, router_weight), ("dp", "z", "core"), axis=0, tiled=True
    )
    expert_local = jnp.concatenate([gate_weight, up_weight], axis=0)
    down_near = gather_near(down_weight, "dp")

    dest_group = deal_order // rows % peers
    place = dest_group * share + (deal_order % rows - me * share)
    deal_matrix = (place[None, :] == jnp.arange(rows, dtype=jnp.int32)[:, None]).astype(BF16)
    dealt = jnp.dot(deal_matrix, tokens, preferred_element_type=F32).astype(BF16)
    cot_part = lax.dynamic_slice_in_dim(cotangent, me_y * part, part, 1)
    cot_part = jnp.dot(deal_matrix, cot_part, preferred_element_type=F32).astype(BF16)

    match = expert_ids[:, :, None] == jnp.arange(experts, dtype=jnp.int32)[None, None, :]
    order = jnp.min(jnp.where(match, slot_order[:, :, None], BIG), axis=1)
    chosen = order < BIG
    earlier = jnp.sum((order[None, :, :] < order[:, None, :]).astype(jnp.int32), axis=1)
    code = chosen.astype(F32) + (chosen & (earlier < capacity)).astype(F32)
    table = jnp.pad(code, ((0, 0), (0, 128 - experts))).astype(BF16)
    cot_near = gather_near(jnp.concatenate([cot_part, table], axis=1), "z")
    code_own = jnp.stack([near[:, part:] for near in cot_near])
    code_all = jnp.stack([code_own, core_swap(code_own)]).reshape(peers * rows, 128)
    cot_own = jnp.stack([near[:, :part] for near in cot_near])
    dealt, cot_own = lax.optimization_barrier((dealt, cot_own))
    got = lax.all_to_all(
        dealt.reshape(peers, share, width), zc, split_axis=0, concat_axis=0, tiled=True
    ).reshape(rows, width)
    cot_own = jnp.stack(gather_near(cot_own, "tensor")).reshape(tensors, zs * rows, part)

    segment = segment_of(seq_lengths[0], rows)
    same_seq = (segment[:, None] == segment[None, :]).astype(F32)
    normed, normed_feat = norm_call(got, gain_first.reshape(1, width))
    normed_feat = lax.all_to_all(normed_feat, zc, split_axis=0, concat_axis=0, tiled=True)
    expert_local, normed = lax.optimization_barrier((expert_local, normed))
    expert_full = lax.all_gather(expert_local, "dp", axis=1, tiled=True)
    normed, normed_feat, cot_own, code_all, packed, down_near = lax.optimization_barrier(
        (normed, normed_feat, cot_own, code_all, packed, down_near)
    )
    cot_other = core_swap(cot_own)
    projected, weights, mixed, branch = attention_call(place_now, normed, same_seq, packed)
    mixed_all = lax.all_gather(mixed, zc, axis=0, tiled=True)
    resid_in = got.astype(F32)
    resid_part = lax.dynamic_slice_in_dim(resid_in, me_y * part, part, 1) + sum_near(
        branch, "tensor"
    )
    resid_near = jnp.stack(gather_near(resid_part.astype(BF16), "tensor"))
    resid_near, cot_other = lax.optimization_barrier((resid_near, cot_other))
    resid_own = jnp.stack(gather_near(resid_near, "z"))
    cot_all, back, upstream, down_full = back_call(place_now, cot_own, cot_other, down_near)
    resid_own, back = lax.optimization_barrier((resid_own, back))
    resid_other = core_swap(resid_own)

    sent_own, sent_other, hidden, mids, mid_source, gates = experts_call(
        place_now,
        resid_own,
        resid_other,
        back,
        code_all,
        expert_full,
        packed,
        gain_second.reshape(tensors, part),
    )
    rows_own, rows_other = rows_call(mids, down_full)
    paired = pair_call(sent_own, core_swap(sent_other))
    paired, rows_own, rows_other = lax.optimization_barrier((paired, rows_own, rows_other))
    expert_rows = pair_call(
        rows_own.reshape(zs, rows, width), core_swap(rows_other).reshape(zs, rows, width)
    )
    expert_grads = grads_call(hidden, cot_all, mids, mid_source)
    cols, expert_rows, expert_grads = lax.optimization_barrier(
        (swap_near(paired, "tensor"), swap_near(expert_rows, "z"), expert_grads)
    )
    cols, expert_rows = lax.optimization_barrier((combine_call(cols), expert_rows))
    cols, expert_rows = lax.optimization_barrier(
        (swap_near(cols, "z"), columns_call(place_now, expert_rows))
    )
    cols, dots = finish_call(cols)
    grads_near, expert_rows = lax.optimization_barrier(
        (gather_near(cols, "tensor"), swap_near(expert_rows, "tensor"))
    )

    branch_feat, grad_proj, grad_own = attention_back_call(
        place_now,
        grads_near,
        dots,
        gates,
        hidden,
        resid_near,
        upstream,
        packed,
        projected,
        weights,
        gain_second.reshape(1, width),
    )
    grad_z = jnp.stack(gather_near(grad_proj, "z"))
    grad_other = core_swap(grad_z)
    branch_feat = lax.all_to_all(branch_feat, zc, split_axis=0, concat_axis=0, tiled=True)
    normed_cols = sum_near(
        normed_back_call(place_now, grad_proj, got, gain_first.reshape(1, width), packed), "tensor"
    )
    inner = normed_cols[:rows, part : part + 1] + normed_cols[:rows, part + 1 : part + 2]
    inner = inner / width
    gain_sum = (normed_cols[rows : rows + 4, :part] + normed_cols[rows + 4 : rows + 8, :part]).reshape(
        dps, peers, feats
    )
    gain_sum = gain_sum.transpose(1, 0, 2).reshape(peers, 1, dps * feats)
    gain_high = gain_sum.astype(BF16)
    gain_low = (gain_sum - gain_high.astype(F32)).astype(BF16)
    gain_rows = jnp.pad(
        jnp.concatenate([gain_high, gain_low], axis=1), ((0, 0), (0, 14), (0, 2 * part - dps * feats))
    )

    def own_cols(table):
        return lax.dynamic_slice_in_dim(table, me_y * part, part, table.ndim - 1)

    factor_first = lax.rsqrt(jnp.mean(resid_in * resid_in, axis=-1, keepdims=True) + EPSILON)
    input_part = grad_own + factor_first * (
        normed_cols[:rows, :part] * own_cols(gain_first) - own_cols(resid_in) * factor_first * inner
    )

    expert_grads = lax.psum_scatter(expert_grads, "dp", scatter_dimension=0, tiled=False)
    expert_grads = [expert_grads[here * i : here * (i + 1)].astype(F32) for i in range(3)]

    output_part = resid_part + total(expert_rows)

    final = jnp.concatenate([output_part.astype(BF16), input_part.astype(BF16)], axis=1)
    final = jnp.concatenate([final.reshape(peers, share, 2 * part), gain_rows], axis=1)
    final = lax.all_to_all(final, zc, split_axis=0, concat_axis=0, tiled=True)
    by_dp = tail_call(place_now, normed_feat, grad_z, grad_other, branch_feat, mixed_all)
    final, _ = lax.optimization_barrier((final, by_dp))
    gain_sum = jnp.sum(final[:, share : share + 2, : dps * feats].astype(F32), axis=(0, 1))
    gain_sum = gain_sum.reshape(dps, 1, feats)
    dp_index = lax.axis_index("dp")
    gain_sum = [
        lax.dynamic_index_in_dim(gain_sum, (dp_index + k) % dps, 0, keepdims=False) for k in range(dps)
    ]
    final = lax.dot_general(
        deal_matrix,
        final[:, :share].reshape(rows, 2 * part),
        (((0,), (0,)), ((), ())),
        preferred_element_type=F32,
    ).astype(BF16)
    by_dp, gain_sum, final, expert_grads = lax.optimization_barrier(
        (swap_near(by_dp, "dp"), swap_near(gain_sum, "dp"), final, expert_grads)
    )
    by_dp = total(by_dp)
    qkv_grad = by_dp[:, : 3 * head_width].reshape(feats, 3, head_width).transpose(1, 0, 2)
    out_grad = by_dp[:, 3 * head_width : 4 * head_width].T
    tail = by_dp[:, 4 * head_width :]
    router_grad = tail[:, :experts].T
    gain_second_grad = tail[:, experts] + tail[:, experts + 1]
    gain_first_grad = total(gain_sum)[0]

    return (
        final[:, :part],
        final[:, part:],
        qkv_grad,
        out_grad,
        router_grad,
        *expert_grads,
        gain_first_grad,
        gain_second_grad,
    )


def solution(mesh):
    sizes = mesh.shape
    split = Mesh(
        mesh.devices.reshape(sizes["dp"], sizes["expert"] // 2, 2, sizes["tensor"]),
        ("dp", "z", "core", "tensor"),
    )
    experts = ("z", "core")
    every = ("dp", "z", "core")
    placed = (
        P(every, None),
        P(every, None),
        P(every, None),
        P(every),
        P(every, None),
        P(every, None),
        P(None, every, "tensor"),
        P("tensor", every),
        P(None, every),
        P(experts, "dp", "tensor"),
        P(experts, "dp", "tensor"),
        P(experts, "dp", "tensor"),
        P(),
        P(),
    )
    return jax.shard_map(
        local,
        mesh=split,
        in_specs=placed,
        out_specs=(
            P(every, "tensor"),
            P(every, "tensor"),
            P(None, every, "tensor"),
            P("tensor", every),
            P(None, every),
            P(experts, "dp", "tensor"),
            P(experts, "dp", "tensor"),
            P(experts, "dp", "tensor"),
            P(every),
            P(every),
        ),
        check_vma=False,
    )
```

```python
import jax
import jax.numpy as jnp
from jax import lax
from jax.sharding import Mesh
from jax.sharding import PartitionSpec as P
from jax.experimental import pallas as pl
from jax.experimental.pallas import tpu as pltpu

HEAD_DIM = 128
EPSILON = 1e-05
F32 = jnp.float32
BF16 = jnp.bfloat16
BIG = 1 << 30
VMEM = pltpu.VMEM
ANY = pl.ANY


def shift(values, axis, step):
    size = lax.axis_size(axis)
    return lax.ppermute(values, axis, [(i, (i + step) % size) for i in range(size)])


def core_swap(values):
    return lax.ppermute(values, "core", [(0, 1), (1, 0)])


def gather_near(values, axis):
    size = lax.axis_size(axis)
    got = {k: shift(values, axis, -k) for k in (1, size - 1, 2)}
    return [values] + [got[k] for k in range(1, size)]


def sum_near(parts, axis):
    size = lax.axis_size(axis)
    total = parts[0].astype(F32)
    for k in (1, size - 1, 2):
        total = total + shift(parts[k], axis, k).astype(F32)
    return total


def swap_near(parts, axis):
    size = lax.axis_size(axis)
    return [parts[0]] + [shift(parts[k], axis, k) for k in (1, size - 1, 2)]


def total(parts):
    return sum(part.astype(F32) for part in parts)


def segment_of(seq_lengths, row_count):
    seq_ends = jnp.cumsum(seq_lengths)
    position = jnp.arange(row_count, dtype=jnp.int32)
    return jnp.sum((position[:, None] >= seq_ends[None, :]).astype(jnp.int32), axis=1)


def nt(a,b): return lax.dot_general(a,b,(((1,),(1,)),((),())),preferred_element_type=F32)
def tn(a,b): return lax.dot_general(a,b,(((0,),(0,)),((),())),preferred_element_type=F32)

def spec(space):
    return pl.BlockSpec(memory_space=space)


def params(megabytes=62):
    return pltpu.CompilerParams(vmem_limit_bytes=megabytes * 1024 * 1024)


def cost(flops, moved):
    return pl.CostEstimate(flops=flops, bytes_accessed=moved, transcendentals=0)


def pack_kernel(qkv, out, router, packed):
    for s in range(3):
        packed[:, s * 512 : (s + 1) * 512] = qkv[s]
    packed[:, 1536:2048] = out[...]
    wide = jnp.concatenate([router[...].astype(F32), jnp.zeros((112, 64), F32)], axis=0)
    packed[:, 2048:] = wide.T.astype(BF16)


def pack_call(qkv, out, router):
    return pl.pallas_call(
        pack_kernel,
        out_shape=jax.ShapeDtypeStruct((64, 2176), BF16),
        cost_estimate=cost(1000, 6 * 10**5),
        compiler_params=params(),
        grid=(1,),
        name="pack",
    )(qkv, out, router)


def spread_features(values, out, row):
    count = values.shape[0]
    for e in range(8):
        for d in range(4):
            at = d * 512 + e * 64
            out[e, row : row + count, d * 64 : (d + 1) * 64] = values[:, at : at + 64]


def norm_kernel(tokens, gain, normed_out, feat_out):
    values = tokens[...].astype(F32)
    factor = lax.rsqrt(jnp.mean(values * values, axis=-1, keepdims=True) + EPSILON)
    normed = (values * factor * gain[...]).astype(BF16)
    normed_out[...] = normed
    spread_features(normed, feat_out, 0)


def norm_call(tokens, gain):
    shape = jax.ShapeDtypeStruct
    return pl.pallas_call(
        norm_kernel,
        out_shape=(shape((128, 2048), BF16), shape((8, 128, 256), BF16)),
        cost_estimate=cost(10**6, 15 * 10**5),
        compiler_params=params(),
        grid=(1,),
        name="norm",
    )(tokens, gain)


def attention_kernel(
    where, normed, same, packed, proj_out, prob_out, mixed_out, b0, b1, b2, b3, w_buf, o_buf, sem_w, sem_o
):
    y0 = where[0]
    loads = [
        pltpu.make_async_copy(packed.at[:, s * 512 : (s + 1) * 512], w_buf.at[s], sem_w.at[s])
        for s in range(3)
    ]
    for load in loads:
        load.start()
    out_load = pltpu.make_async_copy(packed.at[:, 1536:2048], o_buf, sem_o)
    out_load.start()
    for s in range(3):
        loads[s].wait()
        proj_out[s] = jnp.dot(normed[...], w_buf[s], preferred_element_type=F32).astype(BF16)
    mask = same[...] > 0.5
    scale = HEAD_DIM ** (-0.5)
    for h in range(4):
        cols = slice(h * HEAD_DIM, (h + 1) * HEAD_DIM)
        scores = jnp.where(
            mask, nt(proj_out[0, :, cols], proj_out[1, :, cols]) * scale, -1000000000.0
        )
        grown = jnp.exp(scores - jnp.max(scores, axis=-1, keepdims=True))
        prob = grown / jnp.sum(grown, axis=-1, keepdims=True)
        prob_out[h] = prob
        mixed_out[:, cols] = jnp.dot(
            prob.astype(BF16), proj_out[2, :, cols], preferred_element_type=F32
        ).astype(BF16)
    out_load.wait()
    for k, branch in enumerate((b0, b1, b2, b3)):
        at = pl.multiple_of(((y0 + k) & 3) * 512, 512)
        branch[...] = nt(mixed_out[...], o_buf[pl.ds(at, 512), :]).astype(BF16)


def attention_call(where, normed, same, packed):
    shape = jax.ShapeDtypeStruct
    dma = pltpu.SemaphoreType.DMA
    return pl.pallas_call(
        attention_kernel,
        out_shape=(
            shape((3, 128, 512), BF16),
            shape((4, 128, 128), F32),
            shape((128, 512), BF16),
        )
        + (shape((128, 512), BF16),) * 4,
        in_specs=[spec(pltpu.SMEM), spec(VMEM), spec(VMEM), spec(ANY)],
        out_specs=(spec(VMEM),) * 7,
        scratch_shapes=[VMEM((3, 2048, 512), BF16), VMEM((2048, 512), BF16), dma((3,)), dma],
        compiler_params=params(),
        cost_estimate=cost(2 * 10**9, 10 * 10**6),
        grid=(1,),
        name="attention",
    )(where, normed, same, packed)


def attention_back_kernel(
    where, g0, g1, g2, g3, dots, gates, hidden, resid, cots, packed, proj_in, prob_in, gain,
    feat_out, grad_proj, own_out,
    o_buf, h_buf, c_buf, x_buf, d_buf, x_low, d_low, proj, prob, sem_o, sem_h, sem_c, sem_x, sem_d, sem_p,
):
    y0 = where[0]
    offs = [pl.multiple_of(((y0 + k) & 3) * 512, 512) for k in range(4)]
    d_loads = [
        pltpu.make_async_copy(g, d_low.at[:, pl.ds(offs[k], 512)], sem_d.at[k])
        for k, g in enumerate((g0, g1, g2, g3))
    ]
    x_loads = [
        pltpu.make_async_copy(resid.at[k], x_low.at[:, pl.ds(offs[k], 512)], sem_x.at[k])
        for k in range(4)
    ]
    h_load = pltpu.make_async_copy(hidden.at[0:128], h_buf, sem_h)
    o_load = pltpu.make_async_copy(packed.at[:, 1536:2176], o_buf, sem_o)
    c_load = pltpu.make_async_copy(cots, c_buf, sem_c)
    p_loads = [
        pltpu.make_async_copy(proj_in, proj, sem_p.at[0]),
        pltpu.make_async_copy(prob_in, prob, sem_p.at[1]),
    ]
    for load in [*x_loads, *d_loads, h_load, o_load, c_load, *p_loads]:
        load.start()
    for load in [*x_loads, *d_loads]:
        load.wait()
    x_buf[...] = x_low[...].astype(F32)
    d_buf[...] = d_low[...].astype(F32)
    share = gates[...]
    dot = dots[...]
    grad_logits = (share * (dot - jnp.sum(dot * share, axis=-1, keepdims=True))).astype(BF16)
    o_load.wait()
    h_load.wait()
    router = tn(grad_logits, h_buf[...])
    grad_hidden = d_buf[...] + nt(grad_logits, o_buf[:, 512:])
    resid_rows = x_buf[...]
    factor = lax.rsqrt(jnp.mean(resid_rows * resid_rows, axis=-1, keepdims=True) + EPSILON)
    unit = resid_rows * factor
    gain_sum = jnp.sum(grad_hidden * unit, axis=0, keepdims=True)
    scaled = grad_hidden * gain[...]
    c_load.wait()
    grad = c_buf[...].astype(F32) + factor * (
        scaled - unit * jnp.mean(scaled * unit, axis=-1, keepdims=True)
    )
    d_buf[...] = grad
    own_out[...] = d_buf[:, pl.ds(offs[0], 512)]
    low = grad.astype(BF16)
    spread_features(low, feat_out, 0)
    spread_features(router[:16].astype(BF16), feat_out, 128)
    high = gain_sum.astype(BF16)
    rest = (gain_sum - high.astype(F32)).astype(BF16)
    tail = jnp.concatenate(
        [high.astype(F32), rest.astype(F32), jnp.zeros((14, 2048), F32)], axis=0
    ).astype(BF16)
    spread_features(tail, feat_out, 144)
    mixed = jnp.dot(low, o_buf[:, :512], preferred_element_type=F32).astype(BF16)
    for load in p_loads:
        load.wait()
    scale = HEAD_DIM ** (-0.5)
    for h in range(4):
        cols = slice(h * HEAD_DIM, (h + 1) * HEAD_DIM)
        weights = prob[h]
        back = mixed[:, cols]
        grad_proj[:, 1024 + h * HEAD_DIM : 1024 + (h + 1) * HEAD_DIM] = tn(
            weights.astype(BF16), back
        ).astype(BF16)
        weight_grad = nt(back, proj[2, :, cols])
        offset = jnp.sum(weight_grad * weights, axis=-1, keepdims=True)
        score = (weights * (weight_grad - offset)).astype(BF16)
        grad_proj[:, cols] = (
            jnp.dot(score, proj[1, :, cols], preferred_element_type=F32) * scale
        ).astype(BF16)
        grad_proj[:, 512 + h * HEAD_DIM : 512 + (h + 1) * HEAD_DIM] = (
            tn(score, proj[0, :, cols]) * scale
        ).astype(BF16)


def attention_back_call(where, grads, dots, gates, hidden, resid, cots, packed, proj, prob, gain):
    shape = jax.ShapeDtypeStruct
    dma = pltpu.SemaphoreType.DMA
    return pl.pallas_call(
        attention_back_kernel,
        out_shape=(
            shape((8, 160, 256), BF16),
            shape((128, 1536), BF16),
            shape((128, 512), F32),
        ),
        in_specs=[spec(pltpu.SMEM)]
        + [spec(ANY)] * 4
        + [spec(VMEM)] * 2
        + [spec(ANY)] * 6
        + [spec(VMEM)],
        out_specs=(spec(VMEM),) * 3,
        scratch_shapes=[
            VMEM((2048, 640), BF16),
            VMEM((128, 2048), BF16),
            VMEM((128, 2048), BF16),
            VMEM((128, 2048), F32),
            VMEM((128, 2048), F32),
            VMEM((128, 2048), BF16),
            VMEM((128, 2048), BF16),
            VMEM((3, 128, 512), BF16),
            VMEM((4, 128, 128), F32),
            dma,
            dma,
            dma,
            dma((4,)),
            dma((4,)),
            dma((2,)),
        ],
        compiler_params=params(),
        cost_estimate=cost(10**9, 6 * 10**6),
        grid=(1,),
        name="attention_back",
    )(where, *grads, dots, gates, hidden, resid, cots, packed, proj, prob, gain)


def normed_back_kernel(where, grad_proj, tokens, gain, packed, o0, o1, o2, o3, w_buf, sem_w):
    y0 = where[0]
    outs = (o0, o1, o2, o3)
    order = [(y0 + k) & 3 for k in (1, 3, 2, 0)]
    loads = [
        pltpu.make_async_copy(
            packed.at[pl.ds(pl.multiple_of(at * 512, 512), 512), 0:1536], w_buf.at[i], sem_w.at[i]
        )
        for i, at in enumerate(order)
    ]
    for load in loads:
        load.start()
    values = tokens[...].astype(F32)
    factor = lax.rsqrt(jnp.mean(values * values, axis=-1, keepdims=True) + EPSILON)
    inner = jnp.zeros((128, 1), F32)
    sums = []
    for i, k in enumerate((1, 3, 2, 0)):
        loads[i].wait()
        grad = nt(grad_proj[...], w_buf[i])
        cols = pl.ds(pl.multiple_of(order[i] * 512, 512), 512)
        unit = tokens[:, cols].astype(F32) * factor
        inner = inner + jnp.sum(grad * unit * gain[:, cols], axis=-1, keepdims=True)
        sums.append(jnp.sum(grad * unit, axis=0, keepdims=True))
        outs[k][0:128, 0:512] = grad.astype(BF16)
    lane = lax.broadcasted_iota(jnp.int32, (128, 128), 1)
    high = inner.astype(BF16).astype(F32)
    both = jnp.where(lane == 0, high, jnp.where(lane == 1, inner - high, 0.0)).astype(BF16)
    row = lax.broadcasted_iota(jnp.int32, (16, 512), 0)
    table = jnp.zeros((16, 512), F32)
    for at, piece in zip(order, sums):
        top = piece.astype(BF16).astype(F32)
        table = jnp.where(row == at, top, jnp.where(row == at + 4, piece - top, table))
    for out in outs:
        out[0:128, 512:] = both
        out[128:, 0:512] = table.astype(BF16)
        out[128:, 512:] = jnp.zeros((16, 128), BF16)


def normed_back_call(where, grad_proj, tokens, gain, packed):
    return pl.pallas_call(
        normed_back_kernel,
        out_shape=(jax.ShapeDtypeStruct((144, 640), BF16),) * 4,
        in_specs=[spec(pltpu.SMEM), spec(VMEM), spec(VMEM), spec(VMEM), spec(ANY)],
        out_specs=(spec(VMEM),) * 4,
        scratch_shapes=[VMEM((4, 512, 1536), BF16), pltpu.SemaphoreType.DMA((4,))],
        compiler_params=params(),
        cost_estimate=cost(10**9, 8 * 10**6),
        grid=(1,),
        name="normed_back",
    )(where, grad_proj, tokens, gain, packed)


def pair_kernel(own, other, *outs):
    for k, out in enumerate(outs):
        out[...] = own[k] + other[k]


def pair_call(own, other):
    shape = own.shape[1:]
    block = (shape[0] // 4,) + shape[1:]
    rest = (0,) * (len(shape) - 1)
    return pl.pallas_call(
        pair_kernel,
        out_shape=(jax.ShapeDtypeStruct(shape, BF16),) * 4,
        grid=(4,),
        in_specs=[pl.BlockSpec((4,) + block, lambda i: (0, i) + rest)] * 2,
        out_specs=(pl.BlockSpec(block, lambda i: (i,) + rest),) * 4,
        compiler_params=params(),
        cost_estimate=cost(10**6, 6 * own.size),
        name="pair",
    )(own, other)


def gather_dots(total):
    lane = lax.broadcasted_iota(jnp.int32, total.shape, 1)
    return jnp.where(lane < 16, total + pltpu.roll(total, 112, 1), 0.0)


def split_dots(dots):
    high = dots.astype(BF16).astype(F32)
    return high + pltpu.roll(dots - high, 16, 1)


def combine_kernel(p0, p1, p2, p3, *outs):
    for r, out in enumerate(outs):
        total = (p0[r].astype(F32) + p1[r].astype(F32)) + (p2[r].astype(F32) + p3[r].astype(F32))
        out[:, :512] = total[:, :512].astype(BF16)
        out[:, 512:] = split_dots(gather_dots(total[:, 512:])).astype(BF16)


def combine_call(pieces):
    return pl.pallas_call(
        combine_kernel,
        out_shape=(jax.ShapeDtypeStruct((128, 640), BF16),) * 4,
        grid=(4,),
        in_specs=[pl.BlockSpec((4, 32, 640), lambda i: (0, i, 0))] * 4,
        out_specs=(pl.BlockSpec((32, 640), lambda i: (i, 0)),) * 4,
        compiler_params=params(),
        cost_estimate=cost(10**6, 3 * 10**6),
        name="combine",
    )(*pieces)


def finish_kernel(p0, p1, p2, p3, cols, dots):
    total = (p0[...].astype(F32) + p1[...].astype(F32)) + (p2[...].astype(F32) + p3[...].astype(F32))
    cols[...] = total[:, :512].astype(BF16)
    dots[...] = gather_dots(total[:, 512:])


def finish_call(pieces):
    shape = jax.ShapeDtypeStruct
    return pl.pallas_call(
        finish_kernel,
        out_shape=(shape((128, 512), BF16), shape((128, 128), F32)),
        cost_estimate=cost(10**6, 10**6),
        compiler_params=params(),
        grid=(1,),
        name="finish",
    )(*pieces)


def columns_kernel(where, p0, p1, p2, p3, *outs):
    y0 = where[0]
    for k, out in enumerate(outs):
        cols = pl.ds(pl.multiple_of(((y0 + k) & 3) * 512, 512), 512)
        total = (p0[:, cols].astype(F32) + p1[:, cols].astype(F32)) + (
            p2[:, cols].astype(F32) + p3[:, cols].astype(F32)
        )
        out[...] = total.astype(BF16)


def columns_call(where, pieces):
    return pl.pallas_call(
        columns_kernel,
        out_shape=(jax.ShapeDtypeStruct((128, 512), BF16),) * 4,
        grid=(4,),
        in_specs=[spec(pltpu.SMEM)] + [pl.BlockSpec((32, 2048), lambda i: (i, 0))] * 4,
        out_specs=(pl.BlockSpec((32, 512), lambda i: (i, 0)),) * 4,
        compiler_params=params(),
        cost_estimate=cost(10**6, 3 * 10**6),
        name="columns",
    )(where, *pieces)


def tail_kernel(
    where, normed, own, other, branch, mixed, o0, o1, o2, o3, n_buf, p_buf, a_buf, sem
):
    me, d0 = where[1], where[2]
    loads = [
        pltpu.make_async_copy(piece.at[r], p_buf.at[pl.ds((c * 4 + r) * 128, 128)], sem.at[c, r])
        for c, piece in enumerate((own, other))
        for r in range(4)
    ]
    for load in loads:
        load.start()
    for r in range(8):
        at = (((me >> 1) + (r & 3)) & 3) * 2 + (((me & 1) + (r >> 2)) & 1)
        n_buf[r * 128 : (r + 1) * 128] = normed[at]
    a_buf[:, 1536:2048] = tn(branch[:, 0:128, :].reshape(1024, 256), mixed[...])
    small = jnp.sum(branch[:, 128:160, :].astype(F32), axis=0)
    a_buf[:, 2048:] = jnp.concatenate([small, jnp.zeros((96, 256), F32)], axis=0).T
    for load in loads:
        load.wait()
    for s in range(3):
        a_buf[:, s * 512 : (s + 1) * 512] = tn(n_buf[...], p_buf[:, s * 512 : (s + 1) * 512])
    for k, out in enumerate((o0, o1, o2, o3)):
        out[...] = a_buf[pl.ds(pl.multiple_of(((d0 + k) & 3) * 64, 64), 64), :].astype(BF16)


def tail_call(where, normed, own, other, branch, mixed):
    dma = pltpu.SemaphoreType.DMA
    return pl.pallas_call(
        tail_kernel,
        out_shape=(jax.ShapeDtypeStruct((64, 2176), BF16),) * 4,
        in_specs=[spec(pltpu.SMEM), spec(VMEM), spec(ANY), spec(ANY)] + [spec(VMEM)] * 2,
        out_specs=(spec(VMEM),) * 4,
        scratch_shapes=[
            VMEM((1024, 256), BF16),
            VMEM((1024, 1536), BF16),
            VMEM((256, 2176), F32),
            dma((2, 4)),
        ],
        compiler_params=params(),
        cost_estimate=cost(10**9, 8 * 10**6),
        grid=(1,),
        name="tail",
    )(where, normed, own, other, branch, mixed)


def block_row(me, r, s):
    group = (((me >> 1) + (r & 3)) & 3) * 2 + (((me & 1) + (r >> 2)) & 1)
    source = (((s >> 1) - (me >> 1)) & 3) + (((s & 1) + (me & 1)) & 1) * 4
    return pl.multiple_of(r * 128 + s * 16, 16), pl.multiple_of(source * 128 + group * 16, 16)


def back_kernel(
    where, g_own, g_other, w0, w1, w2, w3, g_out, back, own_rows, w_out,
    g_buf, w_buf, z_buf, sem_g, sem_w, sem_o,
):
    y0, me = where[0], where[1]
    offs = [pl.multiple_of(((y0 + k) & 3) * 512, 512) for k in range(4)]
    loads = [
        pltpu.make_async_copy(
            piece.at[k], g_buf.at[pl.ds(c * 512, 512), pl.ds(offs[k], 512)], sem_g.at[c, k]
        )
        for c, piece in enumerate((g_own, g_other))
        for k in range(4)
    ]
    w_loads = [
        pltpu.make_async_copy(
            piece,
            w_buf.at[:, pl.ds(pl.multiple_of(((where[2] + k) & 3) * 512, 512), 512), :],
            sem_w.at[k],
        )
        for k, piece in enumerate((w0, w1, w2, w3))
    ]
    for load in loads + w_loads:
        load.start()
    for load in loads:
        load.wait()
    out = pltpu.make_async_copy(g_buf, g_out, sem_o.at[0])
    out.start()
    for load in w_loads:
        load.wait()
    down_out = pltpu.make_async_copy(w_buf, w_out, sem_o.at[1])
    down_out.start()
    for e in range(2):
        z_buf[:, e * 256 : (e + 1) * 256] = jnp.dot(g_buf[...], w_buf[e], preferred_element_type=F32)

    def move(i, _):
        to, at = block_row(me, i >> 3, i & 7)
        back[pl.ds(to, 16), :] = z_buf[pl.ds(at, 16), :]
        return 0

    lax.fori_loop(0, 64, move, 0)
    for s in range(8):
        _, at = block_row(me, 0, s)
        own_rows[s * 16 : (s + 1) * 16, :] = g_buf[pl.ds(at, 16), :]
    out.wait()
    down_out.wait()


def back_call(where, g_own, g_other, down):
    shape = jax.ShapeDtypeStruct
    dma = pltpu.SemaphoreType.DMA
    return pl.pallas_call(
        back_kernel,
        out_shape=(shape((1024, 2048), BF16), shape((1024, 512), F32), shape((128, 2048), BF16), shape((2, 2048, 256), BF16)),
        in_specs=[spec(pltpu.SMEM)] + [spec(ANY)] * 6,
        out_specs=(spec(ANY), spec(VMEM), spec(VMEM), spec(ANY)),
        scratch_shapes=[
            VMEM((1024, 2048), BF16),
            VMEM((2, 2048, 256), BF16),
            VMEM((1024, 512), F32),
            dma((2, 4)),
            dma((4,)),
            dma((2,)),
        ],
        compiler_params=params(),
        cost_estimate=cost(2 * 10**9, 13 * 10**6),
        grid=(1,),
        name="back",
    )(where, g_own, g_other, *down)


def expert_kernel(
    where, near_own, far_own, near_other, far_other, back, code, weights, packed, gain,
    sent_own, sent_other, h_out, mid_out, source_out, gates_out,
    x_buf, b_buf, w_buf, h_buf, d_buf, r_buf, mid, by_source,
    sem_x, sem_b, sem_w, sem_r, sem_h, sem_m, sem_d,
):
    y0, me = where[0], where[1]
    offs = [pl.multiple_of(((y0 + k) & 3) * 512, 512) for k in range(4)]
    x_loads = [
        [
            pltpu.make_async_copy(piece, x_buf.at[b, r], sem_x.at[b, r])
            for r, piece in enumerate((near.at[0], near.at[1], far, near.at[2]))
        ]
        for b, (near, far) in enumerate(((near_own, far_own), (near_other, far_other)))
    ]
    w_load = pltpu.make_async_copy(weights.at[pl.ds(0, 4)], w_buf, sem_w)
    r_load = pltpu.make_async_copy(packed.at[:, 2048:2176], r_buf, sem_r)
    b_load = pltpu.make_async_copy(back, b_buf, sem_b)
    for load in x_loads[0]:
        load.start()
    r_load.start()
    w_load.start()
    b_load.start()
    for load in x_loads[1]:
        load.start()
    stores = []
    lane = lax.broadcasted_iota(jnp.int32, (512, 128), 1)
    for b in range(2):
        for load in x_loads[b]:
            load.wait()

        def norm(r, _):
            square = jnp.zeros((128, 1), F32)
            for k in range(4):
                value = x_buf[b, r, k].astype(F32)
                square = square + jnp.sum(value * value, axis=-1, keepdims=True)
            factor = lax.rsqrt(square * (1.0 / 2048) + EPSILON)
            at = pl.ds(pl.multiple_of(b * 512 + r * 128, 128), 128)
            for k in range(4):
                part = gain[pl.ds((y0 + k) & 3, 1), :]
                h_buf[at, pl.ds(offs[k], 512)] = (x_buf[b, r, k].astype(F32) * factor * part).astype(BF16)
            return 0

        lax.fori_loop(0, 4, norm, 0)
        here = pl.ds(b * 512, 512)
        stores.append(pltpu.make_async_copy(h_buf.at[here], h_out.at[here], sem_h.at[b]))
        stores[-1].start()
        if b == 0:
            r_load.wait()
        logits = jnp.dot(h_buf[here, :], r_buf[...], preferred_element_type=F32)
        codes = code[here, :].astype(F32)
        chosen = codes > 0.5
        top = jnp.max(jnp.where(chosen, logits, -jnp.inf), axis=-1, keepdims=True)
        lifted = jnp.where(chosen, jnp.exp(logits - top), 0.0)
        gates = lifted / jnp.sum(lifted, axis=-1, keepdims=True)
        if b == 0:
            gates_out[...] = gates[:128]
            w_load.wait()
            b_load.wait()
        used = jnp.where(codes > 1.5, gates, 0.0)
        dots = jnp.zeros((512, 128), F32)
        for e in range(2):
            mine = lane == me * 2 + e
            use = jnp.sum(jnp.where(mine, used, 0.0), axis=-1, keepdims=True)
            keep = jnp.sum(jnp.where(mine & (codes > 1.5), 1.0, 0.0), axis=-1, keepdims=True)
            cols = pl.ds(e * 256, 256)
            u = jnp.dot(h_buf[here, :], w_buf[e], preferred_element_type=F32)
            w = jnp.dot(h_buf[here, :], w_buf[2 + e], preferred_element_type=F32)
            z = b_buf[here, cols]
            s = 1.0 / (1.0 + jnp.exp(-u))
            silu = u * s
            act = silu * w
            dot = jnp.sum(z * act, axis=-1, keepdims=True) * keep
            high = dot.astype(BF16).astype(F32)
            dots = jnp.where(mine, high, dots)
            dots = jnp.where(lane == me * 2 + e + 16, dot - high, dots)
            z = z * use
            mid[0, here, cols] = (z * w * s * (1.0 + u * (1.0 - s))).astype(BF16)
            mid[1, here, cols] = (z * silu).astype(BF16)
            mid[2, here, cols] = (act * use).astype(BF16)
        dots = dots.astype(BF16)
        for k in range(4):
            acc = None
            for e in range(2):
                for m in range(2):
                    term = nt(mid[m, here, pl.ds(e * 256, 256)], w_buf[2 * m + e, pl.ds(offs[k], 512), :])
                    acc = term if acc is None else acc + term
            acc = acc.astype(BF16)
            for r in range(4):
                d_buf[b, k, r, :, 0:512] = acc[r * 128 : (r + 1) * 128]
                d_buf[b, k, r, :, 512:] = dots[r * 128 : (r + 1) * 128]
            target = (sent_own, sent_other)[b].at[k]
            stores.append(pltpu.make_async_copy(d_buf.at[b, k], target, sem_d.at[b, k]))
            stores[-1].start()
    stores.append(pltpu.make_async_copy(mid, mid_out, sem_m.at[0]))
    stores[-1].start()

    def move(i, _):
        at, to = block_row(me, i >> 3, i & 7)
        by_source[pl.ds(to, 16), :] = mid[2, pl.ds(at, 16), :]
        return 0

    lax.fori_loop(0, 64, move, 0)
    stores.append(pltpu.make_async_copy(by_source, source_out, sem_m.at[1]))
    stores[-1].start()
    for store in stores:
        store.wait()


def experts_call(where, resid, back, code, weights, packed, gain):
    shape = jax.ShapeDtypeStruct
    dma = pltpu.SemaphoreType.DMA
    return pl.pallas_call(
        expert_kernel,
        out_shape=(
            shape((4, 4, 128, 640), BF16),
            shape((4, 4, 128, 640), BF16),
            shape((1024, 2048), BF16),
            shape((3, 1024, 512), BF16),
            shape((1024, 512), BF16),
            shape((128, 128), F32),
        ),
        in_specs=[spec(pltpu.SMEM)]
        + [spec(ANY)] * 5
        + [spec(VMEM)]
        + [spec(ANY)] * 2
        + [spec(VMEM)],
        out_specs=(spec(ANY),) * 5 + (spec(VMEM),),
        scratch_shapes=[
            VMEM((2, 4, 4, 128, 512), BF16),
            VMEM((1024, 512), F32),
            VMEM((4, 2048, 256), BF16),
            VMEM((1024, 2048), BF16),
            VMEM((2, 4, 4, 128, 640), BF16),
            VMEM((2048, 128), BF16),
            VMEM((3, 1024, 512), BF16),
            VMEM((1024, 512), BF16),
            dma((2, 4)),
            dma,
            dma,
            dma,
            dma((2,)),
            dma((2,)),
            dma((2, 4)),
        ],
        compiler_params=params(),
        cost_estimate=cost(9 * 10**9, 26 * 10**6),
        grid=(1,),
        name="experts",
    )(where, *resid, back, code, weights, packed, gain)


def grads_kernel(h, g, mid, by_source, out):
    for i, (rows, cols) in enumerate(((h, mid[0]), (h, mid[1]), (g, by_source[...]))):
        grad = tn(rows[...], cols)
        for e in range(2):
            out[0, 2 * i + e] = grad[:, e * 256 : (e + 1) * 256].astype(BF16)


def grads_call(h, g, mid, by_source):
    return pl.pallas_call(
        grads_kernel,
        grid=(4,),
        out_shape=jax.ShapeDtypeStruct((4, 6, 512, 256), BF16),
        in_specs=[
            pl.BlockSpec((1024, 512), lambda j: (0, j)),
            pl.BlockSpec((1024, 512), lambda j: (0, j)),
            pl.BlockSpec((2, 1024, 512), lambda j: (0, 0, 0)),
            pl.BlockSpec((1024, 512), lambda j: (0, 0)),
        ],
        out_specs=pl.BlockSpec((1, 6, 512, 256), lambda j: (j, 0, 0, 0)),
        compiler_params=params(),
        cost_estimate=cost(7 * 10**9, 18 * 10**6),
        name="grads",
    )(h, g, mid, by_source)


def rows_kernel(mid, w, own, other):
    acc = nt(mid[0, :, 0:256], w[0]) + nt(mid[0, :, 256:512], w[1])
    own[...] = acc[:512].astype(BF16)
    other[...] = acc[512:].astype(BF16)


def rows_call(mid, weights):
    shape = jax.ShapeDtypeStruct
    return pl.pallas_call(
        rows_kernel,
        grid=(4,),
        out_shape=(shape((512, 2048), BF16),) * 2,
        in_specs=[
            pl.BlockSpec((1, 1024, 512), lambda j: (2, 0, 0)),
            pl.BlockSpec((2, 512, 256), lambda j: (0, j, 0)),
        ],
        out_specs=(pl.BlockSpec((512, 512), lambda j: (0, j)),) * 2,
        compiler_params=params(),
        cost_estimate=cost(2 * 10**9, 7 * 10**6),
        name="rows",
    )(mid, weights)


def local(
    tokens,
    cotangent,
    seq_lengths,
    deal_order,
    expert_ids,
    slot_order,
    qkv_weight,
    out_weight,
    router_weight,
    gate_weight,
    up_weight,
    down_weight,
    gain_first,
    gain_second,
):
    rows, width = tokens.shape
    zc = ("z", "core")
    peers = lax.axis_size("z") * lax.axis_size("core")
    tensors = lax.axis_size("tensor")
    dps = lax.axis_size("dp")
    zs = lax.axis_size("z")
    share = rows // peers
    part = width // tensors
    me_core = lax.axis_index("core")
    me_z = lax.axis_index("z")
    me = me_z * 2 + me_core
    me_y = lax.axis_index("tensor")
    experts = router_weight.shape[0]
    top = expert_ids.shape[1]
    capacity = (5 * rows * top + 4 * experts - 1) // (4 * experts)
    here = gate_weight.shape[0]
    head_width = qkv_weight.shape[2]
    feats = qkv_weight.shape[1]

    place_now = jnp.stack([me_y, me, lax.axis_index("dp")]).astype(jnp.int32)

    packed = lax.all_gather(
        pack_call(qkv_weight, out_weight.T, router_weight), ("dp", "z", "core"), axis=0, tiled=True
    )
    expert_local = jnp.concatenate([gate_weight, up_weight], axis=0)
    down_near = gather_near(down_weight, "dp")

    dest_group = deal_order // rows % peers
    place = dest_group * share + (deal_order % rows - me * share)
    deal_matrix = (place[None, :] == jnp.arange(rows, dtype=jnp.int32)[:, None]).astype(BF16)
    dealt = jnp.dot(deal_matrix, tokens, preferred_element_type=F32).astype(BF16)
    cot_part = lax.dynamic_slice_in_dim(cotangent, me_y * part, part, 1)
    cot_part = jnp.dot(deal_matrix, cot_part, preferred_element_type=F32).astype(BF16)

    match = expert_ids[:, :, None] == jnp.arange(experts, dtype=jnp.int32)[None, None, :]
    order = jnp.min(jnp.where(match, slot_order[:, :, None], BIG), axis=1)
    chosen = order < BIG
    earlier = jnp.sum((order[None, :, :] < order[:, None, :]).astype(jnp.int32), axis=1)
    code = chosen.astype(F32) + (chosen & (earlier < capacity)).astype(F32)
    table = jnp.pad(code, ((0, 0), (0, 128 - experts))).astype(BF16)
    cot_near = gather_near(jnp.concatenate([cot_part, table], axis=1), "z")
    code_own = jnp.stack([near[:, part:] for near in cot_near])
    code_all = jnp.stack([code_own, core_swap(code_own)]).reshape(peers * rows, 128)
    cot_own = jnp.stack([near[:, :part] for near in cot_near])
    dealt, cot_own = lax.optimization_barrier((dealt, cot_own))
    got = lax.all_to_all(
        dealt.reshape(peers, share, width), zc, split_axis=0, concat_axis=0, tiled=True
    ).reshape(rows, width)
    cot_own = jnp.stack(gather_near(cot_own, "tensor")).reshape(tensors, zs * rows, part)

    segment = segment_of(seq_lengths[0], rows)
    same_seq = (segment[:, None] == segment[None, :]).astype(F32)
    normed, normed_feat = norm_call(got, gain_first.reshape(1, width))
    normed_feat = lax.all_to_all(normed_feat, zc, split_axis=0, concat_axis=0, tiled=True)
    expert_local, normed = lax.optimization_barrier((expert_local, normed))
    expert_full = lax.all_gather(expert_local, "dp", axis=1, tiled=True)
    normed, normed_feat, cot_own, code_all, packed, down_near = lax.optimization_barrier(
        (normed, normed_feat, cot_own, code_all, packed, down_near)
    )
    cot_other = core_swap(cot_own)
    projected, weights, mixed, *branch = attention_call(place_now, normed, same_seq, packed)
    mixed_all = lax.all_gather(mixed, zc, axis=0, tiled=True)
    resid_in = got.astype(F32)
    resid_part = lax.dynamic_slice_in_dim(resid_in, me_y * part, part, 1) + sum_near(
        branch, "tensor"
    )
    resid_near = jnp.stack(gather_near(resid_part.astype(BF16), "tensor"))
    resid_near, cot_other = lax.optimization_barrier((resid_near, cot_other))
    left, right = shift(resid_near, "z", 1), shift(resid_near, "z", -1)
    cot_all, back, upstream, down_full = back_call(place_now, cot_own, cot_other, down_near)
    half = tensors // 2
    left, right, back = lax.optimization_barrier((left, right, back))
    far = [shift(left[:half], "z", 1), shift(right[half:], "z", -1)]
    near_own = jnp.stack([resid_near, right, left])
    near_other = core_swap(near_own)
    far, near_other = lax.optimization_barrier((far, near_other))
    far_own = jnp.concatenate(far, axis=0)
    far_other = core_swap(far_own)

    sent_own, sent_other, hidden, mids, mid_source, gates = experts_call(
        place_now,
        (near_own, far_own, near_other, far_other),
        back,
        code_all,
        expert_full,
        packed,
        gain_second.reshape(tensors, part),
    )
    rows_own, rows_other = rows_call(mids, down_full)
    paired = pair_call(sent_own, core_swap(sent_other))
    paired, rows_own, rows_other = lax.optimization_barrier((paired, rows_own, rows_other))
    expert_rows = pair_call(
        rows_own.reshape(zs, rows, width), core_swap(rows_other).reshape(zs, rows, width)
    )
    expert_grads = grads_call(hidden, cot_all, mids, mid_source)
    cols, expert_rows, expert_grads = lax.optimization_barrier(
        (swap_near(paired, "tensor"), swap_near(expert_rows, "z"), expert_grads)
    )
    cols, expert_rows = lax.optimization_barrier((combine_call(cols), expert_rows))
    cols, expert_rows = lax.optimization_barrier(
        (swap_near(cols, "z"), columns_call(place_now, expert_rows))
    )
    cols, dots = finish_call(cols)
    grads_near, expert_rows = lax.optimization_barrier(
        (gather_near(cols, "tensor"), swap_near(expert_rows, "tensor"))
    )

    branch_feat, grad_proj, grad_own = attention_back_call(
        place_now,
        grads_near,
        dots,
        gates,
        hidden,
        resid_near,
        upstream,
        packed,
        projected,
        weights,
        gain_second.reshape(1, width),
    )
    grad_z = jnp.stack(gather_near(grad_proj, "z"))
    grad_other = core_swap(grad_z)
    branch_feat = lax.all_to_all(branch_feat, zc, split_axis=0, concat_axis=0, tiled=True)
    normed_cols = sum_near(
        normed_back_call(place_now, grad_proj, got, gain_first.reshape(1, width), packed), "tensor"
    )
    inner = normed_cols[:rows, part : part + 1] + normed_cols[:rows, part + 1 : part + 2]
    inner = inner / width
    gain_sum = (normed_cols[rows : rows + 4, :part] + normed_cols[rows + 4 : rows + 8, :part]).reshape(
        dps, peers, feats
    )
    gain_sum = gain_sum.transpose(1, 0, 2).reshape(peers, 1, dps * feats)
    gain_high = gain_sum.astype(BF16)
    gain_low = (gain_sum - gain_high.astype(F32)).astype(BF16)
    gain_rows = jnp.pad(
        jnp.concatenate([gain_high, gain_low], axis=1), ((0, 0), (0, 14), (0, 2 * part - dps * feats))
    )

    def own_cols(table):
        return lax.dynamic_slice_in_dim(table, me_y * part, part, table.ndim - 1)

    factor_first = lax.rsqrt(jnp.mean(resid_in * resid_in, axis=-1, keepdims=True) + EPSILON)
    input_part = grad_own + factor_first * (
        normed_cols[:rows, :part] * own_cols(gain_first) - own_cols(resid_in) * factor_first * inner
    )

    expert_grads = lax.psum_scatter(expert_grads, "dp", scatter_dimension=0, tiled=False)
    expert_grads = [expert_grads[here * i : here * (i + 1)].astype(F32) for i in range(3)]

    output_part = resid_part + total(expert_rows)

    final = jnp.concatenate([output_part.astype(BF16), input_part.astype(BF16)], axis=1)
    final = jnp.concatenate([final.reshape(peers, share, 2 * part), gain_rows], axis=1)
    final = lax.all_to_all(final, zc, split_axis=0, concat_axis=0, tiled=True)
    by_dp = tail_call(place_now, normed_feat, grad_z, grad_other, branch_feat, mixed_all)
    final, _ = lax.optimization_barrier((final, by_dp))
    gain_sum = jnp.sum(final[:, share : share + 2, : dps * feats].astype(F32), axis=(0, 1))
    gain_sum = gain_sum.reshape(dps, 1, feats)
    dp_index = lax.axis_index("dp")
    gain_sum = [
        lax.dynamic_index_in_dim(gain_sum, (dp_index + k) % dps, 0, keepdims=False) for k in range(dps)
    ]
    final = lax.dot_general(
        deal_matrix,
        final[:, :share].reshape(rows, 2 * part),
        (((0,), (0,)), ((), ())),
        preferred_element_type=F32,
    ).astype(BF16)
    by_dp, gain_sum, final, expert_grads = lax.optimization_barrier(
        (swap_near(by_dp, "dp"), swap_near(gain_sum, "dp"), final, expert_grads)
    )
    by_dp = total(by_dp)
    qkv_grad = by_dp[:, : 3 * head_width].reshape(feats, 3, head_width).transpose(1, 0, 2)
    out_grad = by_dp[:, 3 * head_width : 4 * head_width].T
    tail = by_dp[:, 4 * head_width :]
    router_grad = tail[:, :experts].T
    gain_second_grad = tail[:, experts] + tail[:, experts + 1]
    gain_first_grad = total(gain_sum)[0]

    return (
        final[:, :part],
        final[:, part:],
        qkv_grad,
        out_grad,
        router_grad,
        *expert_grads,
        gain_first_grad,
        gain_second_grad,
    )


def solution(mesh):
    sizes = mesh.shape
    split = Mesh(
        mesh.devices.reshape(sizes["dp"], sizes["expert"] // 2, 2, sizes["tensor"]),
        ("dp", "z", "core", "tensor"),
    )
    experts = ("z", "core")
    every = ("dp", "z", "core")
    placed = (
        P(every, None),
        P(every, None),
        P(every, None),
        P(every),
        P(every, None),
        P(every, None),
        P(None, every, "tensor"),
        P("tensor", every),
        P(None, every),
        P(experts, "dp", "tensor"),
        P(experts, "dp", "tensor"),
        P(experts, "dp", "tensor"),
        P(),
        P(),
    )
    return jax.shard_map(
        local,
        mesh=split,
        in_specs=placed,
        out_specs=(
            P(every, "tensor"),
            P(every, "tensor"),
            P(None, every, "tensor"),
            P("tensor", every),
            P(None, every),
            P(experts, "dp", "tensor"),
            P(experts, "dp", "tensor"),
            P(experts, "dp", "tensor"),
            P(every),
            P(every),
        ),
        check_vma=False,
    )
```

```python
import jax
import jax.numpy as jnp
from jax import lax
from jax.sharding import Mesh
from jax.sharding import PartitionSpec as P
from jax.experimental import pallas as pl
from jax.experimental.pallas import tpu as pltpu

HEAD_DIM = 128
EPSILON = 1e-05
F32 = jnp.float32
BF16 = jnp.bfloat16
BIG = 1 << 30
VMEM = pltpu.VMEM
ANY = pl.ANY


def shift(values, axis, step):
    size = lax.axis_size(axis)
    return lax.ppermute(values, axis, [(i, (i + step) % size) for i in range(size)])


def core_swap(values):
    return lax.ppermute(values, "core", [(0, 1), (1, 0)])


def gather_near(values, axis):
    size = lax.axis_size(axis)
    got = {k: shift(values, axis, -k) for k in (1, size - 1, 2)}
    return [values] + [got[k] for k in range(1, size)]


def sum_near(parts, axis):
    size = lax.axis_size(axis)
    total = parts[0].astype(F32)
    for k in (1, size - 1, 2):
        total = total + shift(parts[k], axis, k).astype(F32)
    return total


def swap_near(parts, axis):
    size = lax.axis_size(axis)
    return [parts[0]] + [shift(parts[k], axis, k) for k in (1, size - 1, 2)]


def total(parts):
    return sum(part.astype(F32) for part in parts)


def segment_of(seq_lengths, row_count):
    seq_ends = jnp.cumsum(seq_lengths)
    position = jnp.arange(row_count, dtype=jnp.int32)
    return jnp.sum((position[:, None] >= seq_ends[None, :]).astype(jnp.int32), axis=1)


def nt(a,b): return lax.dot_general(a,b,(((1,),(1,)),((),())),preferred_element_type=F32)
def tn(a,b): return lax.dot_general(a,b,(((0,),(0,)),((),())),preferred_element_type=F32)

def spec(space):
    return pl.BlockSpec(memory_space=space)


def params(megabytes=62):
    return pltpu.CompilerParams(vmem_limit_bytes=megabytes * 1024 * 1024)


def cost(flops, moved):
    return pl.CostEstimate(flops=flops, bytes_accessed=moved, transcendentals=0)


def pack_kernel(qkv, out, router, packed):
    for s in range(3):
        packed[:, s * 512 : (s + 1) * 512] = qkv[s]
    packed[:, 1536:2048] = out[...]
    wide = jnp.concatenate([router[...].astype(F32), jnp.zeros((112, 64), F32)], axis=0)
    packed[:, 2048:] = wide.T.astype(BF16)


def pack_call(qkv, out, router):
    return pl.pallas_call(
        pack_kernel,
        out_shape=jax.ShapeDtypeStruct((64, 2176), BF16),
        cost_estimate=cost(1000, 6 * 10**5),
        compiler_params=params(),
        grid=(1,),
        name="pack",
    )(qkv, out, router)


def spread_features(values, out, row):
    count = values.shape[0]
    for e in range(8):
        for d in range(4):
            at = d * 512 + e * 64
            out[e, row : row + count, d * 64 : (d + 1) * 64] = values[:, at : at + 64]


def norm_kernel(tokens, gain, normed_out, feat_out):
    values = tokens[...].astype(F32)
    factor = lax.rsqrt(jnp.mean(values * values, axis=-1, keepdims=True) + EPSILON)
    normed = (values * factor * gain[...]).astype(BF16)
    normed_out[...] = normed
    spread_features(normed, feat_out, 0)


def norm_call(tokens, gain):
    shape = jax.ShapeDtypeStruct
    return pl.pallas_call(
        norm_kernel,
        out_shape=(shape((128, 2048), BF16), shape((8, 128, 256), BF16)),
        cost_estimate=cost(10**6, 15 * 10**5),
        compiler_params=params(),
        grid=(1,),
        name="norm",
    )(tokens, gain)


def attention_kernel(
    where, normed, same, packed, proj_out, prob_out, mixed_out, b0, b1, b2, b3, w_buf, o_buf, sem_w, sem_o
):
    y0 = where[0]
    loads = [
        pltpu.make_async_copy(packed.at[:, s * 512 : (s + 1) * 512], w_buf.at[s], sem_w.at[s])
        for s in range(3)
    ]
    for load in loads:
        load.start()
    out_load = pltpu.make_async_copy(packed.at[:, 1536:2048], o_buf, sem_o)
    out_load.start()
    for s in range(3):
        loads[s].wait()
        proj_out[s] = jnp.dot(normed[...], w_buf[s], preferred_element_type=F32).astype(BF16)
    mask = same[...] > 0.5
    scale = HEAD_DIM ** (-0.5)
    for h in range(4):
        cols = slice(h * HEAD_DIM, (h + 1) * HEAD_DIM)
        scores = jnp.where(
            mask, nt(proj_out[0, :, cols], proj_out[1, :, cols]) * scale, -1000000000.0
        )
        grown = jnp.exp(scores - jnp.max(scores, axis=-1, keepdims=True))
        prob = grown / jnp.sum(grown, axis=-1, keepdims=True)
        prob_out[h] = prob
        mixed_out[:, cols] = jnp.dot(
            prob.astype(BF16), proj_out[2, :, cols], preferred_element_type=F32
        ).astype(BF16)
    out_load.wait()
    for k, branch in enumerate((b0, b1, b2, b3)):
        at = pl.multiple_of(((y0 + k) & 3) * 512, 512)
        branch[...] = nt(mixed_out[...], o_buf[pl.ds(at, 512), :]).astype(BF16)


def attention_call(where, normed, same, packed):
    shape = jax.ShapeDtypeStruct
    dma = pltpu.SemaphoreType.DMA
    return pl.pallas_call(
        attention_kernel,
        out_shape=(
            shape((3, 128, 512), BF16),
            shape((4, 128, 128), F32),
            shape((128, 512), BF16),
        )
        + (shape((128, 512), BF16),) * 4,
        in_specs=[spec(pltpu.SMEM), spec(VMEM), spec(VMEM), spec(ANY)],
        out_specs=(spec(VMEM),) * 7,
        scratch_shapes=[VMEM((3, 2048, 512), BF16), VMEM((2048, 512), BF16), dma((3,)), dma],
        compiler_params=params(),
        cost_estimate=cost(2 * 10**9, 10 * 10**6),
        grid=(1,),
        name="attention",
    )(where, normed, same, packed)


def attention_back_kernel(
    where, g0, g1, g2, g3, dots, gates, hidden, resid, cots, packed, proj_in, prob_in, gain,
    feat_out, grad_proj, own_out,
    o_buf, h_buf, c_buf, x_buf, d_buf, x_low, d_low, proj, prob, sem_o, sem_h, sem_c, sem_x, sem_d, sem_p,
):
    y0 = where[0]
    offs = [pl.multiple_of(((y0 + k) & 3) * 512, 512) for k in range(4)]
    d_loads = [
        pltpu.make_async_copy(g, d_low.at[:, pl.ds(offs[k], 512)], sem_d.at[k])
        for k, g in enumerate((g0, g1, g2, g3))
    ]
    x_loads = [
        pltpu.make_async_copy(resid.at[k], x_low.at[:, pl.ds(offs[k], 512)], sem_x.at[k])
        for k in range(4)
    ]
    h_load = pltpu.make_async_copy(hidden.at[0:128], h_buf, sem_h)
    o_load = pltpu.make_async_copy(packed.at[:, 1536:2176], o_buf, sem_o)
    c_load = pltpu.make_async_copy(cots, c_buf, sem_c)
    p_loads = [
        pltpu.make_async_copy(proj_in, proj, sem_p.at[0]),
        pltpu.make_async_copy(prob_in, prob, sem_p.at[1]),
    ]
    for load in [*x_loads, *d_loads, h_load, o_load, c_load, *p_loads]:
        load.start()
    for load in [*x_loads, *d_loads]:
        load.wait()
    x_buf[...] = x_low[...].astype(F32)
    d_buf[...] = d_low[...].astype(F32)
    share = gates[...]
    dot = dots[...]
    grad_logits = (share * (dot - jnp.sum(dot * share, axis=-1, keepdims=True))).astype(BF16)
    o_load.wait()
    h_load.wait()
    router = tn(grad_logits, h_buf[...])
    grad_hidden = d_buf[...] + nt(grad_logits, o_buf[:, 512:])
    resid_rows = x_buf[...]
    factor = lax.rsqrt(jnp.mean(resid_rows * resid_rows, axis=-1, keepdims=True) + EPSILON)
    unit = resid_rows * factor
    gain_sum = jnp.sum(grad_hidden * unit, axis=0, keepdims=True)
    scaled = grad_hidden * gain[...]
    c_load.wait()
    grad = c_buf[...].astype(F32) + factor * (
        scaled - unit * jnp.mean(scaled * unit, axis=-1, keepdims=True)
    )
    d_buf[...] = grad
    own_out[...] = d_buf[:, pl.ds(offs[0], 512)]
    low = grad.astype(BF16)
    spread_features(low, feat_out, 0)
    spread_features(router[:16].astype(BF16), feat_out, 128)
    high = gain_sum.astype(BF16)
    rest = (gain_sum - high.astype(F32)).astype(BF16)
    tail = jnp.concatenate(
        [high.astype(F32), rest.astype(F32), jnp.zeros((14, 2048), F32)], axis=0
    ).astype(BF16)
    spread_features(tail, feat_out, 144)
    mixed = jnp.dot(low, o_buf[:, :512], preferred_element_type=F32).astype(BF16)
    for load in p_loads:
        load.wait()
    scale = HEAD_DIM ** (-0.5)
    for h in range(4):
        cols = slice(h * HEAD_DIM, (h + 1) * HEAD_DIM)
        weights = prob[h]
        back = mixed[:, cols]
        grad_proj[:, 1024 + h * HEAD_DIM : 1024 + (h + 1) * HEAD_DIM] = tn(
            weights.astype(BF16), back
        ).astype(BF16)
        weight_grad = nt(back, proj[2, :, cols])
        offset = jnp.sum(weight_grad * weights, axis=-1, keepdims=True)
        score = (weights * (weight_grad - offset)).astype(BF16)
        grad_proj[:, cols] = (
            jnp.dot(score, proj[1, :, cols], preferred_element_type=F32) * scale
        ).astype(BF16)
        grad_proj[:, 512 + h * HEAD_DIM : 512 + (h + 1) * HEAD_DIM] = (
            tn(score, proj[0, :, cols]) * scale
        ).astype(BF16)


def attention_back_call(where, grads, dots, gates, hidden, resid, cots, packed, proj, prob, gain):
    shape = jax.ShapeDtypeStruct
    dma = pltpu.SemaphoreType.DMA
    return pl.pallas_call(
        attention_back_kernel,
        out_shape=(
            shape((8, 160, 256), BF16),
            shape((128, 1536), BF16),
            shape((128, 512), F32),
        ),
        in_specs=[spec(pltpu.SMEM)]
        + [spec(ANY)] * 4
        + [spec(VMEM)] * 2
        + [spec(ANY)] * 6
        + [spec(VMEM)],
        out_specs=(spec(VMEM),) * 3,
        scratch_shapes=[
            VMEM((2048, 640), BF16),
            VMEM((128, 2048), BF16),
            VMEM((128, 2048), BF16),
            VMEM((128, 2048), F32),
            VMEM((128, 2048), F32),
            VMEM((128, 2048), BF16),
            VMEM((128, 2048), BF16),
            VMEM((3, 128, 512), BF16),
            VMEM((4, 128, 128), F32),
            dma,
            dma,
            dma,
            dma((4,)),
            dma((4,)),
            dma((2,)),
        ],
        compiler_params=params(),
        cost_estimate=cost(10**9, 6 * 10**6),
        grid=(1,),
        name="attention_back",
    )(where, *grads, dots, gates, hidden, resid, cots, packed, proj, prob, gain)


def normed_back_kernel(where, grad_proj, tokens, gain, packed, o0, o1, o2, o3, w_buf, sem_w):
    y0 = where[0]
    outs = (o0, o1, o2, o3)
    order = [(y0 + k) & 3 for k in (1, 3, 2, 0)]
    loads = [
        pltpu.make_async_copy(
            packed.at[pl.ds(pl.multiple_of(at * 512, 512), 512), 0:1536], w_buf.at[i], sem_w.at[i]
        )
        for i, at in enumerate(order)
    ]
    for load in loads:
        load.start()
    values = tokens[...].astype(F32)
    factor = lax.rsqrt(jnp.mean(values * values, axis=-1, keepdims=True) + EPSILON)
    inner = jnp.zeros((128, 1), F32)
    sums = []
    for i, k in enumerate((1, 3, 2, 0)):
        loads[i].wait()
        grad = nt(grad_proj[...], w_buf[i])
        cols = pl.ds(pl.multiple_of(order[i] * 512, 512), 512)
        unit = tokens[:, cols].astype(F32) * factor
        inner = inner + jnp.sum(grad * unit * gain[:, cols], axis=-1, keepdims=True)
        sums.append(jnp.sum(grad * unit, axis=0, keepdims=True))
        outs[k][0:128, 0:512] = grad.astype(BF16)
    lane = lax.broadcasted_iota(jnp.int32, (128, 128), 1)
    high = inner.astype(BF16).astype(F32)
    both = jnp.where(lane == 0, high, jnp.where(lane == 1, inner - high, 0.0)).astype(BF16)
    row = lax.broadcasted_iota(jnp.int32, (16, 512), 0)
    table = jnp.zeros((16, 512), F32)
    for at, piece in zip(order, sums):
        top = piece.astype(BF16).astype(F32)
        table = jnp.where(row == at, top, jnp.where(row == at + 4, piece - top, table))
    for out in outs:
        out[0:128, 512:] = both
        out[128:, 0:512] = table.astype(BF16)
        out[128:, 512:] = jnp.zeros((16, 128), BF16)


def normed_back_call(where, grad_proj, tokens, gain, packed):
    return pl.pallas_call(
        normed_back_kernel,
        out_shape=(jax.ShapeDtypeStruct((144, 640), BF16),) * 4,
        in_specs=[spec(pltpu.SMEM), spec(VMEM), spec(VMEM), spec(VMEM), spec(ANY)],
        out_specs=(spec(VMEM),) * 4,
        scratch_shapes=[VMEM((4, 512, 1536), BF16), pltpu.SemaphoreType.DMA((4,))],
        compiler_params=params(),
        cost_estimate=cost(10**9, 8 * 10**6),
        grid=(1,),
        name="normed_back",
    )(where, grad_proj, tokens, gain, packed)


def pair_kernel(own, other, *outs):
    for k, out in enumerate(outs):
        out[...] = own[k] + other[k]


def pair_call(own, other):
    shape = own.shape[1:]
    block = (shape[0] // 4,) + shape[1:]
    rest = (0,) * (len(shape) - 1)
    return pl.pallas_call(
        pair_kernel,
        out_shape=(jax.ShapeDtypeStruct(shape, BF16),) * 4,
        grid=(4,),
        in_specs=[pl.BlockSpec((4,) + block, lambda i: (0, i) + rest)] * 2,
        out_specs=(pl.BlockSpec(block, lambda i: (i,) + rest),) * 4,
        compiler_params=params(),
        cost_estimate=cost(10**6, 6 * own.size),
        name="pair",
    )(own, other)


def join_dots(table):
    return jnp.concatenate(
        [table[0:16], table[16:32], jnp.zeros((16, 256), F32)], axis=1
    ).astype(BF16)


def combine_kernel(p0, p1, p2, p3, *outs):
    for r, out in enumerate(outs):
        total = (p0[r].astype(F32) + p1[r].astype(F32)) + (p2[r].astype(F32) + p3[r].astype(F32))
        out[0:128] = total[0:128].astype(BF16)
        dots = total[128:, 0:128] + total[128:, 128:256]
        high = dots.astype(BF16).astype(F32)
        out[128:] = join_dots(jnp.concatenate([high, dots - high], axis=0))


def combine_call(pieces):
    return pl.pallas_call(
        combine_kernel,
        out_shape=(jax.ShapeDtypeStruct((144, 512), BF16),) * 4,
        grid=(1,),
        compiler_params=params(),
        cost_estimate=cost(10**6, 3 * 10**6),
        name="combine",
    )(*pieces)


def finish_kernel(p0, p1, p2, p3, cols, dots):
    total = (p0[...].astype(F32) + p1[...].astype(F32)) + (p2[...].astype(F32) + p3[...].astype(F32))
    cols[...] = total[0:128].astype(BF16)
    table = total[128:, 0:128] + total[128:, 128:256]
    dots[...] = jnp.concatenate([table, jnp.zeros((112, 128), F32)], axis=0).T


def finish_call(pieces):
    shape = jax.ShapeDtypeStruct
    return pl.pallas_call(
        finish_kernel,
        out_shape=(shape((128, 512), BF16), shape((128, 128), F32)),
        cost_estimate=cost(10**6, 10**6),
        compiler_params=params(),
        grid=(1,),
        name="finish",
    )(*pieces)


def columns_kernel(where, p0, p1, p2, p3, *outs):
    y0 = where[0]
    for k, out in enumerate(outs):
        cols = pl.ds(pl.multiple_of(((y0 + k) & 3) * 512, 512), 512)
        total = (p0[:, cols].astype(F32) + p1[:, cols].astype(F32)) + (
            p2[:, cols].astype(F32) + p3[:, cols].astype(F32)
        )
        out[...] = total.astype(BF16)


def columns_call(where, pieces):
    return pl.pallas_call(
        columns_kernel,
        out_shape=(jax.ShapeDtypeStruct((128, 512), BF16),) * 4,
        grid=(4,),
        in_specs=[spec(pltpu.SMEM)] + [pl.BlockSpec((32, 2048), lambda i: (i, 0))] * 4,
        out_specs=(pl.BlockSpec((32, 512), lambda i: (i, 0)),) * 4,
        compiler_params=params(),
        cost_estimate=cost(10**6, 3 * 10**6),
        name="columns",
    )(where, *pieces)


def tail_kernel(
    where, normed, own, other, branch, mixed, o0, o1, o2, o3, n_buf, p_buf, a_buf, sem
):
    me, d0 = where[1], where[2]
    loads = [
        pltpu.make_async_copy(piece.at[r], p_buf.at[pl.ds((c * 4 + r) * 128, 128)], sem.at[c, r])
        for c, piece in enumerate((own, other))
        for r in range(4)
    ]
    for load in loads:
        load.start()
    for r in range(8):
        at = (((me >> 1) + (r & 3)) & 3) * 2 + (((me & 1) + (r >> 2)) & 1)
        n_buf[r * 128 : (r + 1) * 128] = normed[at]
    a_buf[:, 1536:2048] = tn(branch[:, 0:128, :].reshape(1024, 256), mixed[...])
    small = jnp.sum(branch[:, 128:160, :].astype(F32), axis=0)
    a_buf[:, 2048:] = jnp.concatenate([small, jnp.zeros((96, 256), F32)], axis=0).T
    for load in loads:
        load.wait()
    for s in range(3):
        a_buf[:, s * 512 : (s + 1) * 512] = tn(n_buf[...], p_buf[:, s * 512 : (s + 1) * 512])
    for k, out in enumerate((o0, o1, o2, o3)):
        out[...] = a_buf[pl.ds(pl.multiple_of(((d0 + k) & 3) * 64, 64), 64), :].astype(BF16)


def tail_call(where, normed, own, other, branch, mixed):
    dma = pltpu.SemaphoreType.DMA
    return pl.pallas_call(
        tail_kernel,
        out_shape=(jax.ShapeDtypeStruct((64, 2176), BF16),) * 4,
        in_specs=[spec(pltpu.SMEM), spec(VMEM), spec(ANY), spec(ANY)] + [spec(VMEM)] * 2,
        out_specs=(spec(VMEM),) * 4,
        scratch_shapes=[
            VMEM((1024, 256), BF16),
            VMEM((1024, 1536), BF16),
            VMEM((256, 2176), F32),
            dma((2, 4)),
        ],
        compiler_params=params(),
        cost_estimate=cost(10**9, 8 * 10**6),
        grid=(1,),
        name="tail",
    )(where, normed, own, other, branch, mixed)


def block_row(me, r, s):
    group = (((me >> 1) + (r & 3)) & 3) * 2 + (((me & 1) + (r >> 2)) & 1)
    source = (((s >> 1) - (me >> 1)) & 3) + (((s & 1) + (me & 1)) & 1) * 4
    return pl.multiple_of(r * 128 + s * 16, 16), pl.multiple_of(source * 128 + group * 16, 16)


def back_kernel(
    where, g_own, g_other, w0, w1, w2, w3, g_out, back, own_rows, w_out,
    g_buf, w_buf, z_buf, sem_g, sem_w, sem_o,
):
    y0, me = where[0], where[1]
    offs = [pl.multiple_of(((y0 + k) & 3) * 512, 512) for k in range(4)]
    loads = [
        pltpu.make_async_copy(
            piece.at[k], g_buf.at[pl.ds(c * 512, 512), pl.ds(offs[k], 512)], sem_g.at[c, k]
        )
        for c, piece in enumerate((g_own, g_other))
        for k in range(4)
    ]
    w_loads = [
        pltpu.make_async_copy(
            piece,
            w_buf.at[:, pl.ds(pl.multiple_of(((where[2] + k) & 3) * 512, 512), 512), :],
            sem_w.at[k],
        )
        for k, piece in enumerate((w0, w1, w2, w3))
    ]
    for load in loads + w_loads:
        load.start()
    for load in loads:
        load.wait()
    out = pltpu.make_async_copy(g_buf, g_out, sem_o.at[0])
    out.start()
    for load in w_loads:
        load.wait()
    down_out = pltpu.make_async_copy(w_buf, w_out, sem_o.at[1])
    down_out.start()
    for e in range(2):
        z_buf[:, e * 256 : (e + 1) * 256] = jnp.dot(g_buf[...], w_buf[e], preferred_element_type=F32)

    def move(i, _):
        to, at = block_row(me, i >> 3, i & 7)
        back[pl.ds(to, 16), :] = z_buf[pl.ds(at, 16), :]
        return 0

    lax.fori_loop(0, 64, move, 0)
    for s in range(8):
        _, at = block_row(me, 0, s)
        own_rows[s * 16 : (s + 1) * 16, :] = g_buf[pl.ds(at, 16), :]
    out.wait()
    down_out.wait()


def back_call(where, g_own, g_other, down):
    shape = jax.ShapeDtypeStruct
    dma = pltpu.SemaphoreType.DMA
    return pl.pallas_call(
        back_kernel,
        out_shape=(shape((1024, 2048), BF16), shape((1024, 512), F32), shape((128, 2048), BF16), shape((2, 2048, 256), BF16)),
        in_specs=[spec(pltpu.SMEM)] + [spec(ANY)] * 6,
        out_specs=(spec(ANY), spec(VMEM), spec(VMEM), spec(ANY)),
        scratch_shapes=[
            VMEM((1024, 2048), BF16),
            VMEM((2, 2048, 256), BF16),
            VMEM((1024, 512), F32),
            dma((2, 4)),
            dma((4,)),
            dma((2,)),
        ],
        compiler_params=params(),
        cost_estimate=cost(2 * 10**9, 13 * 10**6),
        grid=(1,),
        name="back",
    )(where, g_own, g_other, *down)


def expert_kernel(
    where, near_own, far_own, near_other, far_other, back, code, weights, packed, gain,
    sent_own, sent_other, h_out, mid_out, source_out, gates_out,
    x_buf, b_buf, w_buf, h_buf, d_buf, r_buf, mid, by_source,
    sem_x, sem_b, sem_w, sem_r, sem_h, sem_m, sem_d,
):
    y0, me = where[0], where[1]
    offs = [pl.multiple_of(((y0 + k) & 3) * 512, 512) for k in range(4)]
    x_loads = [
        [
            pltpu.make_async_copy(piece, x_buf.at[b, r], sem_x.at[b, r])
            for r, piece in enumerate((near.at[0], near.at[1], far, near.at[2]))
        ]
        for b, (near, far) in enumerate(((near_own, far_own), (near_other, far_other)))
    ]
    w_load = pltpu.make_async_copy(weights.at[pl.ds(0, 4)], w_buf, sem_w)
    r_load = pltpu.make_async_copy(packed.at[:, 2048:2176], r_buf, sem_r)
    b_load = pltpu.make_async_copy(back, b_buf, sem_b)
    for load in x_loads[0]:
        load.start()
    r_load.start()
    w_load.start()
    b_load.start()
    for load in x_loads[1]:
        load.start()
    stores = []
    lane = lax.broadcasted_iota(jnp.int32, (512, 128), 1)
    for b in range(2):
        for load in x_loads[b]:
            load.wait()

        def norm(r, _):
            square = jnp.zeros((128, 1), F32)
            for k in range(4):
                value = x_buf[b, r, k].astype(F32)
                square = square + jnp.sum(value * value, axis=-1, keepdims=True)
            factor = lax.rsqrt(square * (1.0 / 2048) + EPSILON)
            at = pl.ds(pl.multiple_of(b * 512 + r * 128, 128), 128)
            for k in range(4):
                part = gain[pl.ds((y0 + k) & 3, 1), :]
                h_buf[at, pl.ds(offs[k], 512)] = (x_buf[b, r, k].astype(F32) * factor * part).astype(BF16)
            return 0

        lax.fori_loop(0, 4, norm, 0)
        here = pl.ds(b * 512, 512)
        stores.append(pltpu.make_async_copy(h_buf.at[here], h_out.at[here], sem_h.at[b]))
        stores[-1].start()
        if b == 0:
            r_load.wait()
        logits = jnp.dot(h_buf[here, :], r_buf[...], preferred_element_type=F32)
        codes = code[here, :].astype(F32)
        chosen = codes > 0.5
        top = jnp.max(jnp.where(chosen, logits, -jnp.inf), axis=-1, keepdims=True)
        lifted = jnp.where(chosen, jnp.exp(logits - top), 0.0)
        gates = lifted / jnp.sum(lifted, axis=-1, keepdims=True)
        if b == 0:
            gates_out[...] = gates[:128]
            w_load.wait()
            b_load.wait()
        used = jnp.where(codes > 1.5, gates, 0.0)
        dots = jnp.zeros((512, 128), F32)
        for e in range(2):
            mine = lane == me * 2 + e
            use = jnp.sum(jnp.where(mine, used, 0.0), axis=-1, keepdims=True)
            keep = jnp.sum(jnp.where(mine & (codes > 1.5), 1.0, 0.0), axis=-1, keepdims=True)
            cols = pl.ds(e * 256, 256)
            u = jnp.dot(h_buf[here, :], w_buf[e], preferred_element_type=F32)
            w = jnp.dot(h_buf[here, :], w_buf[2 + e], preferred_element_type=F32)
            z = b_buf[here, cols]
            s = 1.0 / (1.0 + jnp.exp(-u))
            silu = u * s
            act = silu * w
            dot = jnp.sum(z * act, axis=-1, keepdims=True) * keep
            high = dot.astype(BF16).astype(F32)
            dots = jnp.where(mine, high, dots)
            dots = jnp.where(lane == me * 2 + e + 16, dot - high, dots)
            z = z * use
            mid[0, here, cols] = (z * w * s * (1.0 + u * (1.0 - s))).astype(BF16)
            mid[1, here, cols] = (z * silu).astype(BF16)
            mid[2, here, cols] = (act * use).astype(BF16)
        turned = [join_dots(dots[r * 128 : (r + 1) * 128].T) for r in range(4)]
        for k in range(4):
            acc = None
            for e in range(2):
                for m in range(2):
                    term = nt(mid[m, here, pl.ds(e * 256, 256)], w_buf[2 * m + e, pl.ds(offs[k], 512), :])
                    acc = term if acc is None else acc + term
            acc = acc.astype(BF16)
            for r in range(4):
                d_buf[b, k, r, 0:128] = acc[r * 128 : (r + 1) * 128]
                d_buf[b, k, r, 128:] = turned[r]
            target = (sent_own, sent_other)[b].at[k]
            stores.append(pltpu.make_async_copy(d_buf.at[b, k], target, sem_d.at[b, k]))
            stores[-1].start()
    stores.append(pltpu.make_async_copy(mid, mid_out, sem_m.at[0]))
    stores[-1].start()

    def move(i, _):
        at, to = block_row(me, i >> 3, i & 7)
        by_source[pl.ds(to, 16), :] = mid[2, pl.ds(at, 16), :]
        return 0

    lax.fori_loop(0, 64, move, 0)
    stores.append(pltpu.make_async_copy(by_source, source_out, sem_m.at[1]))
    stores[-1].start()
    for store in stores:
        store.wait()


def experts_call(where, resid, back, code, weights, packed, gain):
    shape = jax.ShapeDtypeStruct
    dma = pltpu.SemaphoreType.DMA
    return pl.pallas_call(
        expert_kernel,
        out_shape=(
            shape((4, 4, 144, 512), BF16),
            shape((4, 4, 144, 512), BF16),
            shape((1024, 2048), BF16),
            shape((3, 1024, 512), BF16),
            shape((1024, 512), BF16),
            shape((128, 128), F32),
        ),
        in_specs=[spec(pltpu.SMEM)]
        + [spec(ANY)] * 5
        + [spec(VMEM)]
        + [spec(ANY)] * 2
        + [spec(VMEM)],
        out_specs=(spec(ANY),) * 5 + (spec(VMEM),),
        scratch_shapes=[
            VMEM((2, 4, 4, 128, 512), BF16),
            VMEM((1024, 512), F32),
            VMEM((4, 2048, 256), BF16),
            VMEM((1024, 2048), BF16),
            VMEM((2, 4, 4, 144, 512), BF16),
            VMEM((2048, 128), BF16),
            VMEM((3, 1024, 512), BF16),
            VMEM((1024, 512), BF16),
            dma((2, 4)),
            dma,
            dma,
            dma,
            dma((2,)),
            dma((2,)),
            dma((2, 4)),
        ],
        compiler_params=params(),
        cost_estimate=cost(9 * 10**9, 26 * 10**6),
        grid=(1,),
        name="experts",
    )(where, *resid, back, code, weights, packed, gain)


def grads_kernel(h, g, mid, by_source, out):
    for i, (rows, cols) in enumerate(((h, mid[0]), (h, mid[1]), (g, by_source[...]))):
        grad = tn(rows[...], cols)
        for e in range(2):
            out[0, 2 * i + e] = grad[:, e * 256 : (e + 1) * 256].astype(BF16)


def grads_call(h, g, mid, by_source):
    return pl.pallas_call(
        grads_kernel,
        grid=(4,),
        out_shape=jax.ShapeDtypeStruct((4, 6, 512, 256), BF16),
        in_specs=[
            pl.BlockSpec((1024, 512), lambda j: (0, j)),
            pl.BlockSpec((1024, 512), lambda j: (0, j)),
            pl.BlockSpec((2, 1024, 512), lambda j: (0, 0, 0)),
            pl.BlockSpec((1024, 512), lambda j: (0, 0)),
        ],
        out_specs=pl.BlockSpec((1, 6, 512, 256), lambda j: (j, 0, 0, 0)),
        compiler_params=params(),
        cost_estimate=cost(7 * 10**9, 18 * 10**6),
        name="grads",
    )(h, g, mid, by_source)


def rows_kernel(mid, w, own, other):
    acc = nt(mid[0, :, 0:256], w[0]) + nt(mid[0, :, 256:512], w[1])
    own[...] = acc[:512].astype(BF16)
    other[...] = acc[512:].astype(BF16)


def rows_call(mid, weights):
    shape = jax.ShapeDtypeStruct
    return pl.pallas_call(
        rows_kernel,
        grid=(4,),
        out_shape=(shape((512, 2048), BF16),) * 2,
        in_specs=[
            pl.BlockSpec((1, 1024, 512), lambda j: (2, 0, 0)),
            pl.BlockSpec((2, 512, 256), lambda j: (0, j, 0)),
        ],
        out_specs=(pl.BlockSpec((512, 512), lambda j: (0, j)),) * 2,
        compiler_params=params(),
        cost_estimate=cost(2 * 10**9, 7 * 10**6),
        name="rows",
    )(mid, weights)


def local(
    tokens,
    cotangent,
    seq_lengths,
    deal_order,
    expert_ids,
    slot_order,
    qkv_weight,
    out_weight,
    router_weight,
    gate_weight,
    up_weight,
    down_weight,
    gain_first,
    gain_second,
):
    rows, width = tokens.shape
    zc = ("z", "core")
    peers = lax.axis_size("z") * lax.axis_size("core")
    tensors = lax.axis_size("tensor")
    dps = lax.axis_size("dp")
    zs = lax.axis_size("z")
    share = rows // peers
    part = width // tensors
    me_core = lax.axis_index("core")
    me_z = lax.axis_index("z")
    me = me_z * 2 + me_core
    me_y = lax.axis_index("tensor")
    experts = router_weight.shape[0]
    top = expert_ids.shape[1]
    capacity = (5 * rows * top + 4 * experts - 1) // (4 * experts)
    here = gate_weight.shape[0]
    head_width = qkv_weight.shape[2]
    feats = qkv_weight.shape[1]

    place_now = jnp.stack([me_y, me, lax.axis_index("dp")]).astype(jnp.int32)

    packed = lax.all_gather(
        pack_call(qkv_weight, out_weight.T, router_weight), ("dp", "z", "core"), axis=0, tiled=True
    )
    expert_local = jnp.concatenate([gate_weight, up_weight], axis=0)
    down_near = gather_near(down_weight, "dp")

    dest_group = deal_order // rows % peers
    place = dest_group * share + (deal_order % rows - me * share)
    deal_matrix = (place[None, :] == jnp.arange(rows, dtype=jnp.int32)[:, None]).astype(BF16)
    dealt = jnp.dot(deal_matrix, tokens, preferred_element_type=F32).astype(BF16)
    cot_part = lax.dynamic_slice_in_dim(cotangent, me_y * part, part, 1)
    cot_part = jnp.dot(deal_matrix, cot_part, preferred_element_type=F32).astype(BF16)

    match = expert_ids[:, :, None] == jnp.arange(experts, dtype=jnp.int32)[None, None, :]
    order = jnp.min(jnp.where(match, slot_order[:, :, None], BIG), axis=1)
    chosen = order < BIG
    earlier = jnp.sum((order[None, :, :] < order[:, None, :]).astype(jnp.int32), axis=1)
    code = chosen.astype(F32) + (chosen & (earlier < capacity)).astype(F32)
    table = jnp.pad(code, ((0, 0), (0, 128 - experts))).astype(BF16)
    cot_near = gather_near(jnp.concatenate([cot_part, table], axis=1), "z")
    code_own = jnp.stack([near[:, part:] for near in cot_near])
    code_all = jnp.stack([code_own, core_swap(code_own)]).reshape(peers * rows, 128)
    cot_own = jnp.stack([near[:, :part] for near in cot_near])
    dealt, cot_own = lax.optimization_barrier((dealt, cot_own))
    got = lax.all_to_all(
        dealt.reshape(peers, share, width), zc, split_axis=0, concat_axis=0, tiled=True
    ).reshape(rows, width)
    cot_own = jnp.stack(gather_near(cot_own, "tensor")).reshape(tensors, zs * rows, part)

    segment = segment_of(seq_lengths[0], rows)
    same_seq = (segment[:, None] == segment[None, :]).astype(F32)
    normed, normed_feat = norm_call(got, gain_first.reshape(1, width))
    normed_feat = lax.all_to_all(normed_feat, zc, split_axis=0, concat_axis=0, tiled=True)
    expert_local, normed = lax.optimization_barrier((expert_local, normed))
    expert_full = lax.all_gather(expert_local, "dp", axis=1, tiled=True)
    normed, normed_feat, cot_own, code_all, packed, down_near = lax.optimization_barrier(
        (normed, normed_feat, cot_own, code_all, packed, down_near)
    )
    cot_other = core_swap(cot_own)
    projected, weights, mixed, *branch = attention_call(place_now, normed, same_seq, packed)
    mixed_all = lax.all_gather(mixed, zc, axis=0, tiled=True)
    resid_in = got.astype(F32)
    resid_part = lax.dynamic_slice_in_dim(resid_in, me_y * part, part, 1) + sum_near(
        branch, "tensor"
    )
    resid_near = jnp.stack(gather_near(resid_part.astype(BF16), "tensor"))
    resid_near, cot_other = lax.optimization_barrier((resid_near, cot_other))
    left, right = shift(resid_near, "z", 1), shift(resid_near, "z", -1)
    cot_all, back, upstream, down_full = back_call(place_now, cot_own, cot_other, down_near)
    half = tensors // 2
    left, right, back = lax.optimization_barrier((left, right, back))
    far = [shift(left[:half], "z", 1), shift(right[half:], "z", -1)]
    near_own = jnp.stack([resid_near, right, left])
    near_other = core_swap(near_own)
    far, near_other = lax.optimization_barrier((far, near_other))
    far_own = jnp.concatenate(far, axis=0)
    far_other = core_swap(far_own)

    sent_own, sent_other, hidden, mids, mid_source, gates = experts_call(
        place_now,
        (near_own, far_own, near_other, far_other),
        back,
        code_all,
        expert_full,
        packed,
        gain_second.reshape(tensors, part),
    )
    rows_own, rows_other = rows_call(mids, down_full)
    paired = pair_call(sent_own, core_swap(sent_other))
    paired, rows_own, rows_other = lax.optimization_barrier((paired, rows_own, rows_other))
    expert_rows = pair_call(
        rows_own.reshape(zs, rows, width), core_swap(rows_other).reshape(zs, rows, width)
    )
    expert_grads = grads_call(hidden, cot_all, mids, mid_source)
    cols, expert_rows, expert_grads = lax.optimization_barrier(
        (swap_near(paired, "tensor"), swap_near(expert_rows, "z"), expert_grads)
    )
    cols, expert_rows = lax.optimization_barrier((combine_call(cols), expert_rows))
    cols, expert_rows = lax.optimization_barrier(
        (swap_near(cols, "z"), columns_call(place_now, expert_rows))
    )
    cols, dots = finish_call(cols)
    grads_near, expert_rows = lax.optimization_barrier(
        (gather_near(cols, "tensor"), swap_near(expert_rows, "tensor"))
    )

    branch_feat, grad_proj, grad_own = attention_back_call(
        place_now,
        grads_near,
        dots,
        gates,
        hidden,
        resid_near,
        upstream,
        packed,
        projected,
        weights,
        gain_second.reshape(1, width),
    )
    grad_z = jnp.stack(gather_near(grad_proj, "z"))
    grad_other = core_swap(grad_z)
    branch_feat = lax.all_to_all(branch_feat, zc, split_axis=0, concat_axis=0, tiled=True)
    normed_cols = sum_near(
        normed_back_call(place_now, grad_proj, got, gain_first.reshape(1, width), packed), "tensor"
    )
    inner = normed_cols[:rows, part : part + 1] + normed_cols[:rows, part + 1 : part + 2]
    inner = inner / width
    gain_sum = (normed_cols[rows : rows + 4, :part] + normed_cols[rows + 4 : rows + 8, :part]).reshape(
        dps, peers, feats
    )
    gain_sum = gain_sum.transpose(1, 0, 2).reshape(peers, 1, dps * feats)
    gain_high = gain_sum.astype(BF16)
    gain_low = (gain_sum - gain_high.astype(F32)).astype(BF16)
    gain_rows = jnp.pad(
        jnp.concatenate([gain_high, gain_low], axis=1), ((0, 0), (0, 14), (0, 2 * part - dps * feats))
    )

    def own_cols(table):
        return lax.dynamic_slice_in_dim(table, me_y * part, part, table.ndim - 1)

    factor_first = lax.rsqrt(jnp.mean(resid_in * resid_in, axis=-1, keepdims=True) + EPSILON)
    input_part = grad_own + factor_first * (
        normed_cols[:rows, :part] * own_cols(gain_first) - own_cols(resid_in) * factor_first * inner
    )

    expert_grads = lax.psum_scatter(expert_grads, "dp", scatter_dimension=0, tiled=False)
    expert_grads = [expert_grads[here * i : here * (i + 1)].astype(F32) for i in range(3)]

    output_part = resid_part + total(expert_rows)

    final = jnp.concatenate([output_part.astype(BF16), input_part.astype(BF16)], axis=1)
    final = jnp.concatenate([final.reshape(peers, share, 2 * part), gain_rows], axis=1)
    final = lax.all_to_all(final, zc, split_axis=0, concat_axis=0, tiled=True)
    by_dp = tail_call(place_now, normed_feat, grad_z, grad_other, branch_feat, mixed_all)
    final, _ = lax.optimization_barrier((final, by_dp))
    gain_sum = jnp.sum(final[:, share : share + 2, : dps * feats].astype(F32), axis=(0, 1))
    gain_sum = gain_sum.reshape(dps, 1, feats)
    dp_index = lax.axis_index("dp")
    gain_sum = [
        lax.dynamic_index_in_dim(gain_sum, (dp_index + k) % dps, 0, keepdims=False) for k in range(dps)
    ]
    final = lax.dot_general(
        deal_matrix,
        final[:, :share].reshape(rows, 2 * part),
        (((0,), (0,)), ((), ())),
        preferred_element_type=F32,
    ).astype(BF16)
    by_dp, gain_sum, final, expert_grads = lax.optimization_barrier(
        (swap_near(by_dp, "dp"), swap_near(gain_sum, "dp"), final, expert_grads)
    )
    by_dp = total(by_dp)
    qkv_grad = by_dp[:, : 3 * head_width].reshape(feats, 3, head_width).transpose(1, 0, 2)
    out_grad = by_dp[:, 3 * head_width : 4 * head_width].T
    tail = by_dp[:, 4 * head_width :]
    router_grad = tail[:, :experts].T
    gain_second_grad = tail[:, experts] + tail[:, experts + 1]
    gain_first_grad = total(gain_sum)[0]

    return (
        final[:, :part],
        final[:, part:],
        qkv_grad,
        out_grad,
        router_grad,
        *expert_grads,
        gain_first_grad,
        gain_second_grad,
    )


def solution(mesh):
    sizes = mesh.shape
    split = Mesh(
        mesh.devices.reshape(sizes["dp"], sizes["expert"] // 2, 2, sizes["tensor"]),
        ("dp", "z", "core", "tensor"),
    )
    experts = ("z", "core")
    every = ("dp", "z", "core")
    placed = (
        P(every, None),
        P(every, None),
        P(every, None),
        P(every),
        P(every, None),
        P(every, None),
        P(None, every, "tensor"),
        P("tensor", every),
        P(None, every),
        P(experts, "dp", "tensor"),
        P(experts, "dp", "tensor"),
        P(experts, "dp", "tensor"),
        P(),
        P(),
    )
    return jax.shard_map(
        local,
        mesh=split,
        in_specs=placed,
        out_specs=(
            P(every, "tensor"),
            P(every, "tensor"),
            P(None, every, "tensor"),
            P("tensor", every),
            P(None, every),
            P(experts, "dp", "tensor"),
            P(experts, "dp", "tensor"),
            P(experts, "dp", "tensor"),
            P(every),
            P(every),
        ),
        check_vma=False,
    )
```

```python
import jax
import jax.numpy as jnp
from jax import lax
from jax.sharding import Mesh
from jax.sharding import PartitionSpec as P
from jax.experimental import pallas as pl
from jax.experimental.pallas import tpu as pltpu

HEAD_DIM = 128
EPSILON = 1e-05
F32 = jnp.float32
BF16 = jnp.bfloat16
BIG = 1 << 30
VMEM = pltpu.VMEM
ANY = pl.ANY


def shift(values, axis, step):
    size = lax.axis_size(axis)
    return lax.ppermute(values, axis, [(i, (i + step) % size) for i in range(size)])


def core_swap(values):
    return lax.ppermute(values, "core", [(0, 1), (1, 0)])


def gather_near(values, axis):
    size = lax.axis_size(axis)
    got = {k: shift(values, axis, -k) for k in (1, size - 1, 2)}
    return [values] + [got[k] for k in range(1, size)]


def gather_ring(values, axis):
    half = values.shape[0] // 2
    left, right = shift(values, axis, 1), shift(values, axis, -1)
    far = [shift(left[:half], axis, 1), shift(right[half:], axis, -1)]
    return [values, right, jnp.concatenate(far, axis=0), left]


def sum_near(parts, axis):
    size = lax.axis_size(axis)
    total = parts[0].astype(F32)
    for k in (1, size - 1, 2):
        total = total + shift(parts[k], axis, k).astype(F32)
    return total


def swap_near(parts, axis):
    size = lax.axis_size(axis)
    return [parts[0]] + [shift(parts[k], axis, k) for k in (1, size - 1, 2)]


def total(parts):
    return sum(part.astype(F32) for part in parts)


def segment_of(seq_lengths, row_count):
    seq_ends = jnp.cumsum(seq_lengths)
    position = jnp.arange(row_count, dtype=jnp.int32)
    return jnp.sum((position[:, None] >= seq_ends[None, :]).astype(jnp.int32), axis=1)


def nt(a,b): return lax.dot_general(a,b,(((1,),(1,)),((),())),preferred_element_type=F32)
def tn(a,b): return lax.dot_general(a,b,(((0,),(0,)),((),())),preferred_element_type=F32)

def spec(space):
    return pl.BlockSpec(memory_space=space)


def params(megabytes=62):
    return pltpu.CompilerParams(vmem_limit_bytes=megabytes * 1024 * 1024)


def cost(flops, moved):
    return pl.CostEstimate(flops=flops, bytes_accessed=moved, transcendentals=0)


def pack_kernel(qkv, out, router, packed):
    for s in range(3):
        packed[:, s * 512 : (s + 1) * 512] = qkv[s]
    packed[:, 1536:2048] = out[...]
    wide = jnp.concatenate([router[...].astype(F32), jnp.zeros((112, 64), F32)], axis=0)
    packed[:, 2048:] = wide.T.astype(BF16)


def pack_call(qkv, out, router):
    return pl.pallas_call(
        pack_kernel,
        out_shape=jax.ShapeDtypeStruct((64, 2176), BF16),
        cost_estimate=cost(1000, 6 * 10**5),
        compiler_params=params(),
        grid=(1,),
        name="pack",
    )(qkv, out, router)


def spread_features(values, out, row):
    count = values.shape[0]
    for e in range(8):
        for d in range(4):
            at = d * 512 + e * 64
            out[e, row : row + count, d * 64 : (d + 1) * 64] = values[:, at : at + 64]


def norm_kernel(tokens, gain, normed_out, feat_out):
    values = tokens[...].astype(F32)
    factor = lax.rsqrt(jnp.mean(values * values, axis=-1, keepdims=True) + EPSILON)
    normed = (values * factor * gain[...]).astype(BF16)
    normed_out[...] = normed
    spread_features(normed, feat_out, 0)


def norm_call(tokens, gain):
    shape = jax.ShapeDtypeStruct
    return pl.pallas_call(
        norm_kernel,
        out_shape=(shape((128, 2048), BF16), shape((8, 128, 256), BF16)),
        cost_estimate=cost(10**6, 15 * 10**5),
        compiler_params=params(),
        grid=(1,),
        name="norm",
    )(tokens, gain)


def attention_kernel(
    where, normed, same, packed, proj_out, prob_out, mixed_out, b0, b1, b2, b3, w_buf, o_buf, sem_w, sem_o
):
    y0 = where[0]
    loads = [
        pltpu.make_async_copy(packed.at[:, s * 512 : (s + 1) * 512], w_buf.at[s], sem_w.at[s])
        for s in range(3)
    ]
    for load in loads:
        load.start()
    out_load = pltpu.make_async_copy(packed.at[:, 1536:2048], o_buf, sem_o)
    out_load.start()
    for s in range(3):
        loads[s].wait()
        proj_out[s] = jnp.dot(normed[...], w_buf[s], preferred_element_type=F32).astype(BF16)
    mask = same[...] > 0.5
    scale = HEAD_DIM ** (-0.5)
    for h in range(4):
        cols = slice(h * HEAD_DIM, (h + 1) * HEAD_DIM)
        scores = jnp.where(
            mask, nt(proj_out[0, :, cols], proj_out[1, :, cols]) * scale, -1000000000.0
        )
        grown = jnp.exp(scores - jnp.max(scores, axis=-1, keepdims=True))
        prob = grown / jnp.sum(grown, axis=-1, keepdims=True)
        prob_out[h] = prob
        mixed_out[:, cols] = jnp.dot(
            prob.astype(BF16), proj_out[2, :, cols], preferred_element_type=F32
        ).astype(BF16)
    out_load.wait()
    for k, branch in enumerate((b0, b1, b2, b3)):
        at = pl.multiple_of(((y0 + k) & 3) * 512, 512)
        branch[...] = nt(mixed_out[...], o_buf[pl.ds(at, 512), :]).astype(BF16)


def attention_call(where, normed, same, packed):
    shape = jax.ShapeDtypeStruct
    dma = pltpu.SemaphoreType.DMA
    return pl.pallas_call(
        attention_kernel,
        out_shape=(
            shape((3, 128, 512), BF16),
            shape((4, 128, 128), F32),
            shape((128, 512), BF16),
        )
        + (shape((128, 512), BF16),) * 4,
        in_specs=[spec(pltpu.SMEM), spec(VMEM), spec(VMEM), spec(ANY)],
        out_specs=(spec(VMEM),) * 7,
        scratch_shapes=[VMEM((3, 2048, 512), BF16), VMEM((2048, 512), BF16), dma((3,)), dma],
        compiler_params=params(),
        cost_estimate=cost(2 * 10**9, 10 * 10**6),
        grid=(1,),
        name="attention",
    )(where, normed, same, packed)


def attention_back_kernel(
    where, g0, g1, g2, g3, dots, gates, hidden, resid, cots, packed, proj_in, prob_in, gain,
    feat_out, grad_proj, own_out,
    o_buf, h_buf, c_buf, x_buf, d_buf, x_low, d_low, proj, prob, sem_o, sem_h, sem_c, sem_x, sem_d, sem_p,
):
    y0 = where[0]
    offs = [pl.multiple_of(((y0 + k) & 3) * 512, 512) for k in range(4)]
    d_loads = [
        pltpu.make_async_copy(g, d_low.at[:, pl.ds(offs[k], 512)], sem_d.at[k])
        for k, g in enumerate((g0, g1, g2, g3))
    ]
    x_loads = [
        pltpu.make_async_copy(resid.at[k], x_low.at[:, pl.ds(offs[k], 512)], sem_x.at[k])
        for k in range(4)
    ]
    h_load = pltpu.make_async_copy(hidden.at[0:128], h_buf, sem_h)
    o_load = pltpu.make_async_copy(packed.at[:, 1536:2176], o_buf, sem_o)
    c_load = pltpu.make_async_copy(cots, c_buf, sem_c)
    p_loads = [
        pltpu.make_async_copy(proj_in, proj, sem_p.at[0]),
        pltpu.make_async_copy(prob_in, prob, sem_p.at[1]),
    ]
    for load in [*x_loads, *d_loads, h_load, o_load, c_load, *p_loads]:
        load.start()
    for load in [*x_loads, *d_loads]:
        load.wait()
    x_buf[...] = x_low[...].astype(F32)
    d_buf[...] = d_low[...].astype(F32)
    share = gates[...]
    dot = dots[...]
    grad_logits = (share * (dot - jnp.sum(dot * share, axis=-1, keepdims=True))).astype(BF16)
    o_load.wait()
    h_load.wait()
    router = tn(grad_logits, h_buf[...])
    grad_hidden = d_buf[...] + nt(grad_logits, o_buf[:, 512:])
    resid_rows = x_buf[...]
    factor = lax.rsqrt(jnp.mean(resid_rows * resid_rows, axis=-1, keepdims=True) + EPSILON)
    unit = resid_rows * factor
    gain_sum = jnp.sum(grad_hidden * unit, axis=0, keepdims=True)
    scaled = grad_hidden * gain[...]
    c_load.wait()
    grad = c_buf[...].astype(F32) + factor * (
        scaled - unit * jnp.mean(scaled * unit, axis=-1, keepdims=True)
    )
    d_buf[...] = grad
    own_out[...] = d_buf[:, pl.ds(offs[0], 512)]
    low = grad.astype(BF16)
    spread_features(low, feat_out, 0)
    spread_features(router[:16].astype(BF16), feat_out, 128)
    high = gain_sum.astype(BF16)
    rest = (gain_sum - high.astype(F32)).astype(BF16)
    tail = jnp.concatenate(
        [high.astype(F32), rest.astype(F32), jnp.zeros((14, 2048), F32)], axis=0
    ).astype(BF16)
    spread_features(tail, feat_out, 144)
    mixed = jnp.dot(low, o_buf[:, :512], preferred_element_type=F32).astype(BF16)
    for load in p_loads:
        load.wait()
    scale = HEAD_DIM ** (-0.5)
    for h in range(4):
        cols = slice(h * HEAD_DIM, (h + 1) * HEAD_DIM)
        weights = prob[h]
        back = mixed[:, cols]
        grad_proj[:, 1024 + h * HEAD_DIM : 1024 + (h + 1) * HEAD_DIM] = tn(
            weights.astype(BF16), back
        ).astype(BF16)
        weight_grad = nt(back, proj[2, :, cols])
        offset = jnp.sum(weight_grad * weights, axis=-1, keepdims=True)
        score = (weights * (weight_grad - offset)).astype(BF16)
        grad_proj[:, cols] = (
            jnp.dot(score, proj[1, :, cols], preferred_element_type=F32) * scale
        ).astype(BF16)
        grad_proj[:, 512 + h * HEAD_DIM : 512 + (h + 1) * HEAD_DIM] = (
            tn(score, proj[0, :, cols]) * scale
        ).astype(BF16)


def attention_back_call(where, grads, dots, gates, hidden, resid, cots, packed, proj, prob, gain):
    shape = jax.ShapeDtypeStruct
    dma = pltpu.SemaphoreType.DMA
    return pl.pallas_call(
        attention_back_kernel,
        out_shape=(
            shape((8, 160, 256), BF16),
            shape((128, 1536), BF16),
            shape((128, 512), F32),
        ),
        in_specs=[spec(pltpu.SMEM)]
        + [spec(ANY)] * 4
        + [spec(VMEM)] * 2
        + [spec(ANY)] * 6
        + [spec(VMEM)],
        out_specs=(spec(VMEM),) * 3,
        scratch_shapes=[
            VMEM((2048, 640), BF16),
            VMEM((128, 2048), BF16),
            VMEM((128, 2048), BF16),
            VMEM((128, 2048), F32),
            VMEM((128, 2048), F32),
            VMEM((128, 2048), BF16),
            VMEM((128, 2048), BF16),
            VMEM((3, 128, 512), BF16),
            VMEM((4, 128, 128), F32),
            dma,
            dma,
            dma,
            dma((4,)),
            dma((4,)),
            dma((2,)),
        ],
        compiler_params=params(),
        cost_estimate=cost(10**9, 6 * 10**6),
        grid=(1,),
        name="attention_back",
    )(where, *grads, dots, gates, hidden, resid, cots, packed, proj, prob, gain)


def normed_back_kernel(where, grad_proj, tokens, gain, packed, o0, o1, o2, o3, w_buf, sem_w):
    y0 = where[0]
    outs = (o0, o1, o2, o3)
    order = [(y0 + k) & 3 for k in (1, 3, 2, 0)]
    loads = [
        pltpu.make_async_copy(
            packed.at[pl.ds(pl.multiple_of(at * 512, 512), 512), 0:1536], w_buf.at[i], sem_w.at[i]
        )
        for i, at in enumerate(order)
    ]
    for load in loads:
        load.start()
    values = tokens[...].astype(F32)
    factor = lax.rsqrt(jnp.mean(values * values, axis=-1, keepdims=True) + EPSILON)
    inner = jnp.zeros((128, 1), F32)
    sums = []
    for i, k in enumerate((1, 3, 2, 0)):
        loads[i].wait()
        grad = nt(grad_proj[...], w_buf[i])
        cols = pl.ds(pl.multiple_of(order[i] * 512, 512), 512)
        unit = tokens[:, cols].astype(F32) * factor
        inner = inner + jnp.sum(grad * unit * gain[:, cols], axis=-1, keepdims=True)
        sums.append(jnp.sum(grad * unit, axis=0, keepdims=True))
        outs[k][0:128, 0:512] = grad.astype(BF16)
    lane = lax.broadcasted_iota(jnp.int32, (128, 128), 1)
    high = inner.astype(BF16).astype(F32)
    both = jnp.where(lane == 0, high, jnp.where(lane == 1, inner - high, 0.0)).astype(BF16)
    row = lax.broadcasted_iota(jnp.int32, (16, 512), 0)
    table = jnp.zeros((16, 512), F32)
    for at, piece in zip(order, sums):
        top = piece.astype(BF16).astype(F32)
        table = jnp.where(row == at, top, jnp.where(row == at + 4, piece - top, table))
    for out in outs:
        out[0:128, 512:] = both
        out[128:, 0:512] = table.astype(BF16)
        out[128:, 512:] = jnp.zeros((16, 128), BF16)


def normed_back_call(where, grad_proj, tokens, gain, packed):
    return pl.pallas_call(
        normed_back_kernel,
        out_shape=(jax.ShapeDtypeStruct((144, 640), BF16),) * 4,
        in_specs=[spec(pltpu.SMEM), spec(VMEM), spec(VMEM), spec(VMEM), spec(ANY)],
        out_specs=(spec(VMEM),) * 4,
        scratch_shapes=[VMEM((4, 512, 1536), BF16), pltpu.SemaphoreType.DMA((4,))],
        compiler_params=params(),
        cost_estimate=cost(10**9, 8 * 10**6),
        grid=(1,),
        name="normed_back",
    )(where, grad_proj, tokens, gain, packed)


def pair_kernel(own, other, *outs):
    for k, out in enumerate(outs):
        out[...] = own[k] + other[k]


def pair_call(own, other):
    shape = own.shape[1:]
    block = (shape[0] // 4,) + shape[1:]
    rest = (0,) * (len(shape) - 1)
    return pl.pallas_call(
        pair_kernel,
        out_shape=(jax.ShapeDtypeStruct(shape, BF16),) * 4,
        grid=(4,),
        in_specs=[pl.BlockSpec((4,) + block, lambda i: (0, i) + rest)] * 2,
        out_specs=(pl.BlockSpec(block, lambda i: (i,) + rest),) * 4,
        compiler_params=params(),
        cost_estimate=cost(10**6, 6 * own.size),
        name="pair",
    )(own, other)


def join_dots(table):
    return jnp.concatenate(
        [table[0:16], table[16:32], jnp.zeros((16, 256), F32)], axis=1
    ).astype(BF16)


def combine_kernel(p0, p1, p2, p3, *outs):
    for r, out in enumerate(outs):
        total = (p0[r].astype(F32) + p1[r].astype(F32)) + (p2[r].astype(F32) + p3[r].astype(F32))
        out[0:128] = total[0:128].astype(BF16)
        dots = total[128:, 0:128] + total[128:, 128:256]
        high = dots.astype(BF16).astype(F32)
        out[128:] = join_dots(jnp.concatenate([high, dots - high], axis=0))


def combine_call(pieces):
    return pl.pallas_call(
        combine_kernel,
        out_shape=(jax.ShapeDtypeStruct((144, 512), BF16),) * 4,
        grid=(1,),
        compiler_params=params(),
        cost_estimate=cost(10**6, 3 * 10**6),
        name="combine",
    )(*pieces)


def finish_kernel(p0, p1, p2, p3, cols, dots):
    total = (p0[...].astype(F32) + p1[...].astype(F32)) + (p2[...].astype(F32) + p3[...].astype(F32))
    cols[...] = total[0:128].astype(BF16)
    table = total[128:, 0:128] + total[128:, 128:256]
    dots[...] = jnp.concatenate([table, jnp.zeros((112, 128), F32)], axis=0).T


def finish_call(pieces):
    shape = jax.ShapeDtypeStruct
    return pl.pallas_call(
        finish_kernel,
        out_shape=(shape((128, 512), BF16), shape((128, 128), F32)),
        cost_estimate=cost(10**6, 10**6),
        compiler_params=params(),
        grid=(1,),
        name="finish",
    )(*pieces)


def columns_kernel(where, p0, p1, p2, p3, *outs):
    y0 = where[0]
    for k, out in enumerate(outs):
        cols = pl.ds(pl.multiple_of(((y0 + k) & 3) * 512, 512), 512)
        total = (p0[:, cols].astype(F32) + p1[:, cols].astype(F32)) + (
            p2[:, cols].astype(F32) + p3[:, cols].astype(F32)
        )
        out[...] = total.astype(BF16)


def columns_call(where, pieces):
    return pl.pallas_call(
        columns_kernel,
        out_shape=(jax.ShapeDtypeStruct((128, 512), BF16),) * 4,
        grid=(4,),
        in_specs=[spec(pltpu.SMEM)] + [pl.BlockSpec((32, 2048), lambda i: (i, 0))] * 4,
        out_specs=(pl.BlockSpec((32, 512), lambda i: (i, 0)),) * 4,
        compiler_params=params(),
        cost_estimate=cost(10**6, 3 * 10**6),
        name="columns",
    )(where, *pieces)


def tail_kernel(
    where, normed, own, other, branch, mixed, o0, o1, o2, o3, n_buf, p_buf, a_buf, sem
):
    me, d0 = where[1], where[2]
    loads = [
        pltpu.make_async_copy(piece.at[r], p_buf.at[pl.ds((c * 4 + r) * 128, 128)], sem.at[c, r])
        for c, piece in enumerate((own, other))
        for r in range(4)
    ]
    for load in loads:
        load.start()
    for r in range(8):
        at = (((me >> 1) + (r & 3)) & 3) * 2 + (((me & 1) + (r >> 2)) & 1)
        n_buf[r * 128 : (r + 1) * 128] = normed[at]
    a_buf[:, 1536:2048] = tn(branch[:, 0:128, :].reshape(1024, 256), mixed[...])
    small = jnp.sum(branch[:, 128:160, :].astype(F32), axis=0)
    a_buf[:, 2048:] = jnp.concatenate([small, jnp.zeros((96, 256), F32)], axis=0).T
    for load in loads:
        load.wait()
    for s in range(3):
        a_buf[:, s * 512 : (s + 1) * 512] = tn(n_buf[...], p_buf[:, s * 512 : (s + 1) * 512])
    for k, out in enumerate((o0, o1, o2, o3)):
        out[...] = a_buf[pl.ds(pl.multiple_of(((d0 + k) & 3) * 64, 64), 64), :].astype(BF16)


def tail_call(where, normed, own, other, branch, mixed):
    dma = pltpu.SemaphoreType.DMA
    return pl.pallas_call(
        tail_kernel,
        out_shape=(jax.ShapeDtypeStruct((64, 2176), BF16),) * 4,
        in_specs=[spec(pltpu.SMEM), spec(VMEM), spec(ANY), spec(ANY)] + [spec(VMEM)] * 2,
        out_specs=(spec(VMEM),) * 4,
        scratch_shapes=[
            VMEM((1024, 256), BF16),
            VMEM((1024, 1536), BF16),
            VMEM((256, 2176), F32),
            dma((2, 4)),
        ],
        compiler_params=params(),
        cost_estimate=cost(10**9, 8 * 10**6),
        grid=(1,),
        name="tail",
    )(where, normed, own, other, branch, mixed)


def block_row(me, r, s):
    group = (((me >> 1) + (r & 3)) & 3) * 2 + (((me & 1) + (r >> 2)) & 1)
    source = (((s >> 1) - (me >> 1)) & 3) + (((s & 1) + (me & 1)) & 1) * 4
    return pl.multiple_of(r * 128 + s * 16, 16), pl.multiple_of(source * 128 + group * 16, 16)


def back_kernel(
    where, g_own, g_other, w0, w1, w2, w3, g_out, back, own_rows, w_out,
    g_buf, w_buf, z_buf, sem_g, sem_w, sem_o,
):
    y0, me = where[0], where[1]
    offs = [pl.multiple_of(((y0 + k) & 3) * 512, 512) for k in range(4)]
    loads = [
        pltpu.make_async_copy(
            piece.at[k], g_buf.at[pl.ds(c * 512, 512), pl.ds(offs[k], 512)], sem_g.at[c, k]
        )
        for c, piece in enumerate((g_own, g_other))
        for k in range(4)
    ]
    w_loads = [
        pltpu.make_async_copy(
            piece,
            w_buf.at[:, pl.ds(pl.multiple_of(((where[2] + k) & 3) * 512, 512), 512), :],
            sem_w.at[k],
        )
        for k, piece in enumerate((w0, w1, w2, w3))
    ]
    for load in loads + w_loads:
        load.start()
    for load in loads:
        load.wait()
    out = pltpu.make_async_copy(g_buf, g_out, sem_o.at[0])
    out.start()
    for load in w_loads:
        load.wait()
    down_out = pltpu.make_async_copy(w_buf, w_out, sem_o.at[1])
    down_out.start()
    for e in range(2):
        z_buf[:, e * 256 : (e + 1) * 256] = jnp.dot(g_buf[...], w_buf[e], preferred_element_type=F32)

    def move(i, _):
        to, at = block_row(me, i >> 3, i & 7)
        back[pl.ds(to, 16), :] = z_buf[pl.ds(at, 16), :]
        return 0

    lax.fori_loop(0, 64, move, 0)
    for s in range(8):
        _, at = block_row(me, 0, s)
        own_rows[s * 16 : (s + 1) * 16, :] = g_buf[pl.ds(at, 16), :]
    out.wait()
    down_out.wait()


def back_call(where, g_own, g_other, down):
    shape = jax.ShapeDtypeStruct
    dma = pltpu.SemaphoreType.DMA
    return pl.pallas_call(
        back_kernel,
        out_shape=(shape((1024, 2048), BF16), shape((1024, 512), F32), shape((128, 2048), BF16), shape((2, 2048, 256), BF16)),
        in_specs=[spec(pltpu.SMEM)] + [spec(ANY)] * 6,
        out_specs=(spec(ANY), spec(VMEM), spec(VMEM), spec(ANY)),
        scratch_shapes=[
            VMEM((1024, 2048), BF16),
            VMEM((2, 2048, 256), BF16),
            VMEM((1024, 512), F32),
            dma((2, 4)),
            dma((4,)),
            dma((2,)),
        ],
        compiler_params=params(),
        cost_estimate=cost(2 * 10**9, 13 * 10**6),
        grid=(1,),
        name="back",
    )(where, g_own, g_other, *down)


def expert_kernel(
    where, near_own, far_own, near_other, far_other, back, code, weights, packed, gain,
    sent_own, sent_other, h_out, mid_out, source_out, gates_out,
    x_buf, b_buf, w_buf, h_buf, d_buf, r_buf, mid, by_source,
    sem_x, sem_b, sem_w, sem_r, sem_h, sem_m, sem_d,
):
    y0, me = where[0], where[1]
    offs = [pl.multiple_of(((y0 + k) & 3) * 512, 512) for k in range(4)]
    x_loads = [
        [
            pltpu.make_async_copy(piece, x_buf.at[b, r], sem_x.at[b, r])
            for r, piece in enumerate((near.at[0], near.at[1], far, near.at[2]))
        ]
        for b, (near, far) in enumerate(((near_own, far_own), (near_other, far_other)))
    ]
    w_load = pltpu.make_async_copy(weights.at[pl.ds(0, 4)], w_buf, sem_w)
    r_load = pltpu.make_async_copy(packed.at[:, 2048:2176], r_buf, sem_r)
    b_load = pltpu.make_async_copy(back, b_buf, sem_b)
    for load in x_loads[0]:
        load.start()
    r_load.start()
    w_load.start()
    b_load.start()
    for load in x_loads[1]:
        load.start()
    stores = []
    lane = lax.broadcasted_iota(jnp.int32, (512, 128), 1)
    for b in range(2):
        for load in x_loads[b]:
            load.wait()

        def norm(r, _):
            square = jnp.zeros((128, 1), F32)
            for k in range(4):
                value = x_buf[b, r, k].astype(F32)
                square = square + jnp.sum(value * value, axis=-1, keepdims=True)
            factor = lax.rsqrt(square * (1.0 / 2048) + EPSILON)
            at = pl.ds(pl.multiple_of(b * 512 + r * 128, 128), 128)
            for k in range(4):
                part = gain[pl.ds((y0 + k) & 3, 1), :]
                h_buf[at, pl.ds(offs[k], 512)] = (x_buf[b, r, k].astype(F32) * factor * part).astype(BF16)
            return 0

        lax.fori_loop(0, 4, norm, 0)
        here = pl.ds(b * 512, 512)
        stores.append(pltpu.make_async_copy(h_buf.at[here], h_out.at[here], sem_h.at[b]))
        stores[-1].start()
        if b == 0:
            r_load.wait()
        logits = jnp.dot(h_buf[here, :], r_buf[...], preferred_element_type=F32)
        codes = code[here, :].astype(F32)
        chosen = codes > 0.5
        top = jnp.max(jnp.where(chosen, logits, -jnp.inf), axis=-1, keepdims=True)
        lifted = jnp.where(chosen, jnp.exp(logits - top), 0.0)
        gates = lifted / jnp.sum(lifted, axis=-1, keepdims=True)
        if b == 0:
            gates_out[...] = gates[:128]
            w_load.wait()
            b_load.wait()
        used = jnp.where(codes > 1.5, gates, 0.0)
        dots = jnp.zeros((512, 128), F32)
        for e in range(2):
            mine = lane == me * 2 + e
            use = jnp.sum(jnp.where(mine, used, 0.0), axis=-1, keepdims=True)
            keep = jnp.sum(jnp.where(mine & (codes > 1.5), 1.0, 0.0), axis=-1, keepdims=True)
            cols = pl.ds(e * 256, 256)
            u = jnp.dot(h_buf[here, :], w_buf[e], preferred_element_type=F32)
            w = jnp.dot(h_buf[here, :], w_buf[2 + e], preferred_element_type=F32)
            z = b_buf[here, cols]
            s = 1.0 / (1.0 + jnp.exp(-u))
            silu = u * s
            act = silu * w
            dot = jnp.sum(z * act, axis=-1, keepdims=True) * keep
            high = dot.astype(BF16).astype(F32)
            dots = jnp.where(mine, high, dots)
            dots = jnp.where(lane == me * 2 + e + 16, dot - high, dots)
            z = z * use
            mid[0, here, cols] = (z * w * s * (1.0 + u * (1.0 - s))).astype(BF16)
            mid[1, here, cols] = (z * silu).astype(BF16)
            mid[2, here, cols] = (act * use).astype(BF16)
        turned = [join_dots(dots[r * 128 : (r + 1) * 128].T) for r in range(4)]
        for k in range(4):
            acc = None
            for e in range(2):
                for m in range(2):
                    term = nt(mid[m, here, pl.ds(e * 256, 256)], w_buf[2 * m + e, pl.ds(offs[k], 512), :])
                    acc = term if acc is None else acc + term
            acc = acc.astype(BF16)
            for r in range(4):
                d_buf[b, k, r, 0:128] = acc[r * 128 : (r + 1) * 128]
                d_buf[b, k, r, 128:] = turned[r]
            target = (sent_own, sent_other)[b].at[k]
            stores.append(pltpu.make_async_copy(d_buf.at[b, k], target, sem_d.at[b, k]))
            stores[-1].start()
    stores.append(pltpu.make_async_copy(mid, mid_out, sem_m.at[0]))
    stores[-1].start()

    def move(i, _):
        at, to = block_row(me, i >> 3, i & 7)
        by_source[pl.ds(to, 16), :] = mid[2, pl.ds(at, 16), :]
        return 0

    lax.fori_loop(0, 64, move, 0)
    stores.append(pltpu.make_async_copy(by_source, source_out, sem_m.at[1]))
    stores[-1].start()
    for store in stores:
        store.wait()


def experts_call(where, resid, back, code, weights, packed, gain):
    shape = jax.ShapeDtypeStruct
    dma = pltpu.SemaphoreType.DMA
    return pl.pallas_call(
        expert_kernel,
        out_shape=(
            shape((4, 4, 144, 512), BF16),
            shape((4, 4, 144, 512), BF16),
            shape((1024, 2048), BF16),
            shape((3, 1024, 512), BF16),
            shape((1024, 512), BF16),
            shape((128, 128), F32),
        ),
        in_specs=[spec(pltpu.SMEM)]
        + [spec(ANY)] * 5
        + [spec(VMEM)]
        + [spec(ANY)] * 2
        + [spec(VMEM)],
        out_specs=(spec(ANY),) * 5 + (spec(VMEM),),
        scratch_shapes=[
            VMEM((2, 4, 4, 128, 512), BF16),
            VMEM((1024, 512), F32),
            VMEM((4, 2048, 256), BF16),
            VMEM((1024, 2048), BF16),
            VMEM((2, 4, 4, 144, 512), BF16),
            VMEM((2048, 128), BF16),
            VMEM((3, 1024, 512), BF16),
            VMEM((1024, 512), BF16),
            dma((2, 4)),
            dma,
            dma,
            dma,
            dma((2,)),
            dma((2,)),
            dma((2, 4)),
        ],
        compiler_params=params(),
        cost_estimate=cost(9 * 10**9, 26 * 10**6),
        grid=(1,),
        name="experts",
    )(where, *resid, back, code, weights, packed, gain)


def grads_kernel(h, g, mid, by_source, out):
    for i, (rows, cols) in enumerate(((h, mid[0]), (h, mid[1]), (g, by_source[...]))):
        grad = tn(rows[...], cols)
        for e in range(2):
            out[0, 2 * i + e] = grad[:, e * 256 : (e + 1) * 256].astype(BF16)


def grads_call(h, g, mid, by_source):
    return pl.pallas_call(
        grads_kernel,
        grid=(4,),
        out_shape=jax.ShapeDtypeStruct((4, 6, 512, 256), BF16),
        in_specs=[
            pl.BlockSpec((1024, 512), lambda j: (0, j)),
            pl.BlockSpec((1024, 512), lambda j: (0, j)),
            pl.BlockSpec((2, 1024, 512), lambda j: (0, 0, 0)),
            pl.BlockSpec((1024, 512), lambda j: (0, 0)),
        ],
        out_specs=pl.BlockSpec((1, 6, 512, 256), lambda j: (j, 0, 0, 0)),
        compiler_params=params(),
        cost_estimate=cost(7 * 10**9, 18 * 10**6),
        name="grads",
    )(h, g, mid, by_source)


def rows_kernel(mid, w, own, other):
    acc = nt(mid[0, :, 0:256], w[0]) + nt(mid[0, :, 256:512], w[1])
    own[...] = acc[:512].astype(BF16)
    other[...] = acc[512:].astype(BF16)


def rows_call(mid, weights):
    shape = jax.ShapeDtypeStruct
    return pl.pallas_call(
        rows_kernel,
        grid=(4,),
        out_shape=(shape((512, 2048), BF16),) * 2,
        in_specs=[
            pl.BlockSpec((1, 1024, 512), lambda j: (2, 0, 0)),
            pl.BlockSpec((2, 512, 256), lambda j: (0, j, 0)),
        ],
        out_specs=(pl.BlockSpec((512, 512), lambda j: (0, j)),) * 2,
        compiler_params=params(),
        cost_estimate=cost(2 * 10**9, 7 * 10**6),
        name="rows",
    )(mid, weights)


def local(
    tokens,
    cotangent,
    seq_lengths,
    deal_order,
    expert_ids,
    slot_order,
    qkv_weight,
    out_weight,
    router_weight,
    gate_weight,
    up_weight,
    down_weight,
    gain_first,
    gain_second,
):
    rows, width = tokens.shape
    zc = ("z", "core")
    peers = lax.axis_size("z") * lax.axis_size("core")
    tensors = lax.axis_size("tensor")
    dps = lax.axis_size("dp")
    zs = lax.axis_size("z")
    share = rows // peers
    part = width // tensors
    me_core = lax.axis_index("core")
    me_z = lax.axis_index("z")
    me = me_z * 2 + me_core
    me_y = lax.axis_index("tensor")
    experts = router_weight.shape[0]
    top = expert_ids.shape[1]
    capacity = (5 * rows * top + 4 * experts - 1) // (4 * experts)
    here = gate_weight.shape[0]
    head_width = qkv_weight.shape[2]
    feats = qkv_weight.shape[1]

    place_now = jnp.stack([me_y, me, lax.axis_index("dp")]).astype(jnp.int32)

    packed = lax.all_gather(
        pack_call(qkv_weight, out_weight.T, router_weight), ("dp", "z", "core"), axis=0, tiled=True
    )
    expert_local = jnp.concatenate([gate_weight, up_weight], axis=0)
    down_near = gather_ring(down_weight, "dp")

    dest_group = deal_order // rows % peers
    place = dest_group * share + (deal_order % rows - me * share)
    deal_matrix = (place[None, :] == jnp.arange(rows, dtype=jnp.int32)[:, None]).astype(BF16)
    dealt = jnp.dot(deal_matrix, tokens, preferred_element_type=F32).astype(BF16)
    cot_part = lax.dynamic_slice_in_dim(cotangent, me_y * part, part, 1)
    cot_part = jnp.dot(deal_matrix, cot_part, preferred_element_type=F32).astype(BF16)

    match = expert_ids[:, :, None] == jnp.arange(experts, dtype=jnp.int32)[None, None, :]
    order = jnp.min(jnp.where(match, slot_order[:, :, None], BIG), axis=1)
    chosen = order < BIG
    earlier = jnp.sum((order[None, :, :] < order[:, None, :]).astype(jnp.int32), axis=1)
    code = chosen.astype(F32) + (chosen & (earlier < capacity)).astype(F32)
    table = jnp.pad(code, ((0, 0), (0, 128 - experts))).astype(BF16)
    cot_near = gather_near(jnp.concatenate([cot_part, table], axis=1), "z")
    code_own = jnp.stack([near[:, part:] for near in cot_near])
    code_all = jnp.stack([code_own, core_swap(code_own)]).reshape(peers * rows, 128)
    cot_own = jnp.stack([near[:, :part] for near in cot_near])
    dealt, cot_own = lax.optimization_barrier((dealt, cot_own))
    got = lax.all_to_all(
        dealt.reshape(peers, share, width), zc, split_axis=0, concat_axis=0, tiled=True
    ).reshape(rows, width)
    cot_own = jnp.stack(gather_near(cot_own, "tensor")).reshape(tensors, zs * rows, part)

    segment = segment_of(seq_lengths[0], rows)
    same_seq = (segment[:, None] == segment[None, :]).astype(F32)
    normed, normed_feat = norm_call(got, gain_first.reshape(1, width))
    normed_feat = lax.all_to_all(normed_feat, zc, split_axis=0, concat_axis=0, tiled=True)
    expert_local, normed = lax.optimization_barrier((expert_local, normed))
    expert_full = lax.all_gather(expert_local, "dp", axis=1, tiled=True)
    normed, normed_feat, cot_own, code_all, packed, down_near = lax.optimization_barrier(
        (normed, normed_feat, cot_own, code_all, packed, down_near)
    )
    cot_other = core_swap(cot_own)
    projected, weights, mixed, *branch = attention_call(place_now, normed, same_seq, packed)
    mixed_all = lax.all_gather(mixed, zc, axis=0, tiled=True)
    resid_in = got.astype(F32)
    resid_part = lax.dynamic_slice_in_dim(resid_in, me_y * part, part, 1) + sum_near(
        branch, "tensor"
    )
    resid_near = jnp.stack(gather_near(resid_part.astype(BF16), "tensor"))
    resid_near, cot_other = lax.optimization_barrier((resid_near, cot_other))
    left, right = shift(resid_near, "z", 1), shift(resid_near, "z", -1)
    cot_all, back, upstream, down_full = back_call(place_now, cot_own, cot_other, down_near)
    half = tensors // 2
    left, right, back = lax.optimization_barrier((left, right, back))
    far = [shift(left[:half], "z", 1), shift(right[half:], "z", -1)]
    near_own = jnp.stack([resid_near, right, left])
    near_other = core_swap(near_own)
    far, near_other = lax.optimization_barrier((far, near_other))
    far_own = jnp.concatenate(far, axis=0)
    far_other = core_swap(far_own)

    sent_own, sent_other, hidden, mids, mid_source, gates = experts_call(
        place_now,
        (near_own, far_own, near_other, far_other),
        back,
        code_all,
        expert_full,
        packed,
        gain_second.reshape(tensors, part),
    )
    rows_own, rows_other = rows_call(mids, down_full)
    paired = pair_call(sent_own, core_swap(sent_other))
    paired, rows_own, rows_other = lax.optimization_barrier((paired, rows_own, rows_other))
    expert_rows = pair_call(
        rows_own.reshape(zs, rows, width), core_swap(rows_other).reshape(zs, rows, width)
    )
    expert_grads = grads_call(hidden, cot_all, mids, mid_source)
    cols, expert_rows, expert_grads = lax.optimization_barrier(
        (swap_near(paired, "tensor"), swap_near(expert_rows, "z"), expert_grads)
    )
    cols, expert_rows = lax.optimization_barrier((combine_call(cols), expert_rows))
    cols, expert_rows = lax.optimization_barrier(
        (swap_near(cols, "z"), columns_call(place_now, expert_rows))
    )
    cols, dots = finish_call(cols)
    grads_near, expert_rows = lax.optimization_barrier(
        (gather_near(cols, "tensor"), swap_near(expert_rows, "tensor"))
    )

    branch_feat, grad_proj, grad_own = attention_back_call(
        place_now,
        grads_near,
        dots,
        gates,
        hidden,
        resid_near,
        upstream,
        packed,
        projected,
        weights,
        gain_second.reshape(1, width),
    )
    grad_z = jnp.stack(gather_near(grad_proj, "z"))
    grad_other = core_swap(grad_z)
    branch_feat = lax.all_to_all(branch_feat, zc, split_axis=0, concat_axis=0, tiled=True)
    normed_cols = sum_near(
        normed_back_call(place_now, grad_proj, got, gain_first.reshape(1, width), packed), "tensor"
    )
    inner = normed_cols[:rows, part : part + 1] + normed_cols[:rows, part + 1 : part + 2]
    inner = inner / width
    gain_sum = (normed_cols[rows : rows + 4, :part] + normed_cols[rows + 4 : rows + 8, :part]).reshape(
        dps, peers, feats
    )
    gain_sum = gain_sum.transpose(1, 0, 2).reshape(peers, 1, dps * feats)
    gain_high = gain_sum.astype(BF16)
    gain_low = (gain_sum - gain_high.astype(F32)).astype(BF16)
    gain_rows = jnp.pad(
        jnp.concatenate([gain_high, gain_low], axis=1), ((0, 0), (0, 14), (0, 2 * part - dps * feats))
    )

    def own_cols(table):
        return lax.dynamic_slice_in_dim(table, me_y * part, part, table.ndim - 1)

    factor_first = lax.rsqrt(jnp.mean(resid_in * resid_in, axis=-1, keepdims=True) + EPSILON)
    input_part = grad_own + factor_first * (
        normed_cols[:rows, :part] * own_cols(gain_first) - own_cols(resid_in) * factor_first * inner
    )

    expert_grads = lax.psum_scatter(expert_grads, "dp", scatter_dimension=0, tiled=False)
    expert_grads = [expert_grads[here * i : here * (i + 1)].astype(F32) for i in range(3)]

    output_part = resid_part + total(expert_rows)

    final = jnp.concatenate([output_part.astype(BF16), input_part.astype(BF16)], axis=1)
    final = jnp.concatenate([final.reshape(peers, share, 2 * part), gain_rows], axis=1)
    final = lax.all_to_all(final, zc, split_axis=0, concat_axis=0, tiled=True)
    by_dp = tail_call(place_now, normed_feat, grad_z, grad_other, branch_feat, mixed_all)
    final, _ = lax.optimization_barrier((final, by_dp))
    gain_sum = jnp.sum(final[:, share : share + 2, : dps * feats].astype(F32), axis=(0, 1))
    gain_sum = gain_sum.reshape(dps, 1, feats)
    dp_index = lax.axis_index("dp")
    gain_sum = [
        lax.dynamic_index_in_dim(gain_sum, (dp_index + k) % dps, 0, keepdims=False) for k in range(dps)
    ]
    final = lax.dot_general(
        deal_matrix,
        final[:, :share].reshape(rows, 2 * part),
        (((0,), (0,)), ((), ())),
        preferred_element_type=F32,
    ).astype(BF16)
    by_dp, gain_sum, final, expert_grads = lax.optimization_barrier(
        (swap_near(by_dp, "dp"), swap_near(gain_sum, "dp"), final, expert_grads)
    )
    by_dp = total(by_dp)
    qkv_grad = by_dp[:, : 3 * head_width].reshape(feats, 3, head_width).transpose(1, 0, 2)
    out_grad = by_dp[:, 3 * head_width : 4 * head_width].T
    tail = by_dp[:, 4 * head_width :]
    router_grad = tail[:, :experts].T
    gain_second_grad = tail[:, experts] + tail[:, experts + 1]
    gain_first_grad = total(gain_sum)[0]

    return (
        final[:, :part],
        final[:, part:],
        qkv_grad,
        out_grad,
        router_grad,
        *expert_grads,
        gain_first_grad,
        gain_second_grad,
    )


def solution(mesh):
    sizes = mesh.shape
    split = Mesh(
        mesh.devices.reshape(sizes["dp"], sizes["expert"] // 2, 2, sizes["tensor"]),
        ("dp", "z", "core", "tensor"),
    )
    experts = ("z", "core")
    every = ("dp", "z", "core")
    placed = (
        P(every, None),
        P(every, None),
        P(every, None),
        P(every),
        P(every, None),
        P(every, None),
        P(None, every, "tensor"),
        P("tensor", every),
        P(None, every),
        P(experts, "dp", "tensor"),
        P(experts, "dp", "tensor"),
        P(experts, "dp", "tensor"),
        P(),
        P(),
    )
    return jax.shard_map(
        local,
        mesh=split,
        in_specs=placed,
        out_specs=(
            P(every, "tensor"),
            P(every, "tensor"),
            P(None, every, "tensor"),
            P("tensor", every),
            P(None, every),
            P(experts, "dp", "tensor"),
            P(experts, "dp", "tensor"),
            P(experts, "dp", "tensor"),
            P(every),
            P(every),
        ),
        check_vma=False,
    )
```

```python
import jax
import jax.numpy as jnp
from jax import lax
from jax.sharding import Mesh
from jax.sharding import PartitionSpec as P
from jax.experimental import pallas as pl
from jax.experimental.pallas import tpu as pltpu

HEAD_DIM = 128
EPSILON = 1e-05
F32 = jnp.float32
BF16 = jnp.bfloat16
BIG = 1 << 30
VMEM = pltpu.VMEM
ANY = pl.ANY


def shift(values, axis, step):
    size = lax.axis_size(axis)
    return lax.ppermute(values, axis, [(i, (i + step) % size) for i in range(size)])


def core_swap(values):
    return lax.ppermute(values, "core", [(0, 1), (1, 0)])


def gather_near(values, axis):
    size = lax.axis_size(axis)
    got = {k: shift(values, axis, -k) for k in (1, size - 1, 2)}
    return [values] + [got[k] for k in range(1, size)]


def gather_ring(values, axis):
    half = values.shape[0] // 2
    left, right = shift(values, axis, 1), shift(values, axis, -1)
    far = [shift(left[:half], axis, 1), shift(right[half:], axis, -1)]
    return [values, right, jnp.concatenate(far, axis=0), left]


def sum_near(parts, axis):
    size = lax.axis_size(axis)
    total = parts[0].astype(F32)
    for k in (1, size - 1, 2):
        total = total + shift(parts[k], axis, k).astype(F32)
    return total


def swap_near(parts, axis):
    size = lax.axis_size(axis)
    return [parts[0]] + [shift(parts[k], axis, k) for k in (1, size - 1, 2)]


def total(parts):
    return sum(part.astype(F32) for part in parts)


def segment_of(seq_lengths, row_count):
    seq_ends = jnp.cumsum(seq_lengths)
    position = jnp.arange(row_count, dtype=jnp.int32)
    return jnp.sum((position[:, None] >= seq_ends[None, :]).astype(jnp.int32), axis=1)


def nt(a,b): return lax.dot_general(a,b,(((1,),(1,)),((),())),preferred_element_type=F32)
def tn(a,b): return lax.dot_general(a,b,(((0,),(0,)),((),())),preferred_element_type=F32)

def spec(space):
    return pl.BlockSpec(memory_space=space)


def params(megabytes=62):
    return pltpu.CompilerParams(vmem_limit_bytes=megabytes * 1024 * 1024)


def cost(flops, moved):
    return pl.CostEstimate(flops=flops, bytes_accessed=moved, transcendentals=0)


def pack_kernel(qkv, out, router, packed):
    for s in range(3):
        packed[:, s * 512 : (s + 1) * 512] = qkv[s]
    packed[:, 1536:2048] = out[...]
    wide = jnp.concatenate([router[...].astype(F32), jnp.zeros((112, 64), F32)], axis=0)
    packed[:, 2048:] = wide.T.astype(BF16)


def pack_call(qkv, out, router):
    return pl.pallas_call(
        pack_kernel,
        out_shape=jax.ShapeDtypeStruct((64, 2176), BF16),
        cost_estimate=cost(1000, 6 * 10**5),
        compiler_params=params(),
        grid=(1,),
        name="pack",
    )(qkv, out, router)


def spread_features(values, out, row):
    count = values.shape[0]
    for e in range(8):
        for d in range(4):
            at = d * 512 + e * 64
            out[e, row : row + count, d * 64 : (d + 1) * 64] = values[:, at : at + 64]


def norm_kernel(tokens, gain, normed_out, feat_out):
    values = tokens[...].astype(F32)
    factor = lax.rsqrt(jnp.mean(values * values, axis=-1, keepdims=True) + EPSILON)
    normed = (values * factor * gain[...]).astype(BF16)
    normed_out[...] = normed
    spread_features(normed, feat_out, 0)


def norm_call(tokens, gain):
    shape = jax.ShapeDtypeStruct
    return pl.pallas_call(
        norm_kernel,
        out_shape=(shape((128, 2048), BF16), shape((8, 128, 256), BF16)),
        cost_estimate=cost(10**6, 15 * 10**5),
        compiler_params=params(),
        grid=(1,),
        name="norm",
    )(tokens, gain)


def attention_kernel(
    where, normed, same, packed, proj_out, prob_out, mixed_out, b0, b1, b2, b3, w_buf, o_buf, sem_w, sem_o
):
    y0 = where[0]
    loads = [
        pltpu.make_async_copy(packed.at[:, s * 512 : (s + 1) * 512], w_buf.at[s], sem_w.at[s])
        for s in range(3)
    ]
    for load in loads:
        load.start()
    out_load = pltpu.make_async_copy(packed.at[:, 1536:2048], o_buf, sem_o)
    out_load.start()
    for s in range(3):
        loads[s].wait()
        proj_out[s] = jnp.dot(normed[...], w_buf[s], preferred_element_type=F32).astype(BF16)
    mask = same[...] > 0.5
    scale = HEAD_DIM ** (-0.5)
    for h in range(4):
        cols = slice(h * HEAD_DIM, (h + 1) * HEAD_DIM)
        scores = jnp.where(
            mask, nt(proj_out[0, :, cols], proj_out[1, :, cols]) * scale, -1000000000.0
        )
        grown = jnp.exp(scores - jnp.max(scores, axis=-1, keepdims=True))
        prob = grown / jnp.sum(grown, axis=-1, keepdims=True)
        prob_out[h] = prob
        mixed_out[:, cols] = jnp.dot(
            prob.astype(BF16), proj_out[2, :, cols], preferred_element_type=F32
        ).astype(BF16)
    out_load.wait()
    for k, branch in enumerate((b0, b1, b2, b3)):
        at = pl.multiple_of(((y0 + k) & 3) * 512, 512)
        branch[...] = nt(mixed_out[...], o_buf[pl.ds(at, 512), :]).astype(BF16)


def attention_call(where, normed, same, packed):
    shape = jax.ShapeDtypeStruct
    dma = pltpu.SemaphoreType.DMA
    return pl.pallas_call(
        attention_kernel,
        out_shape=(
            shape((3, 128, 512), BF16),
            shape((4, 128, 128), F32),
            shape((128, 512), BF16),
        )
        + (shape((128, 512), BF16),) * 4,
        in_specs=[spec(pltpu.SMEM), spec(VMEM), spec(VMEM), spec(ANY)],
        out_specs=(spec(VMEM),) * 7,
        scratch_shapes=[VMEM((3, 2048, 512), BF16), VMEM((2048, 512), BF16), dma((3,)), dma],
        compiler_params=params(),
        cost_estimate=cost(2 * 10**9, 10 * 10**6),
        grid=(1,),
        name="attention",
    )(where, normed, same, packed)


def attention_back_kernel(
    where, g0, g1, g2, g3, dots, gates, hidden, resid, cots, packed, proj_in, prob_in, gain,
    feat_out, grad_proj, own_out,
    o_buf, h_buf, c_buf, x_buf, d_buf, x_low, d_low, proj, prob, sem_o, sem_h, sem_c, sem_x, sem_d, sem_p,
):
    y0 = where[0]
    offs = [pl.multiple_of(((y0 + k) & 3) * 512, 512) for k in range(4)]
    d_loads = [
        pltpu.make_async_copy(g, d_low.at[:, pl.ds(offs[k], 512)], sem_d.at[k])
        for k, g in enumerate((g0, g1, g2, g3))
    ]
    x_loads = [
        pltpu.make_async_copy(resid.at[k], x_low.at[:, pl.ds(offs[k], 512)], sem_x.at[k])
        for k in range(4)
    ]
    h_load = pltpu.make_async_copy(hidden.at[0:128], h_buf, sem_h)
    o_load = pltpu.make_async_copy(packed.at[:, 1536:2176], o_buf, sem_o)
    c_load = pltpu.make_async_copy(cots, c_buf, sem_c)
    p_loads = [
        pltpu.make_async_copy(proj_in, proj, sem_p.at[0]),
        pltpu.make_async_copy(prob_in, prob, sem_p.at[1]),
    ]
    for load in [*x_loads, *d_loads, h_load, o_load, c_load, *p_loads]:
        load.start()
    for load in [*x_loads, *d_loads]:
        load.wait()
    x_buf[...] = x_low[...].astype(F32)
    d_buf[...] = d_low[...].astype(F32)
    share = gates[...]
    dot = dots[...]
    grad_logits = (share * (dot - jnp.sum(dot * share, axis=-1, keepdims=True))).astype(BF16)
    o_load.wait()
    h_load.wait()
    router = tn(grad_logits, h_buf[...])
    grad_hidden = d_buf[...] + nt(grad_logits, o_buf[:, 512:])
    resid_rows = x_buf[...]
    factor = lax.rsqrt(jnp.mean(resid_rows * resid_rows, axis=-1, keepdims=True) + EPSILON)
    unit = resid_rows * factor
    gain_sum = jnp.sum(grad_hidden * unit, axis=0, keepdims=True)
    scaled = grad_hidden * gain[...]
    c_load.wait()
    grad = c_buf[...].astype(F32) + factor * (
        scaled - unit * jnp.mean(scaled * unit, axis=-1, keepdims=True)
    )
    d_buf[...] = grad
    own_out[...] = d_buf[:, pl.ds(offs[0], 512)]
    low = grad.astype(BF16)
    spread_features(low, feat_out, 0)
    spread_features(router[:16].astype(BF16), feat_out, 128)
    high = gain_sum.astype(BF16)
    rest = (gain_sum - high.astype(F32)).astype(BF16)
    tail = jnp.concatenate(
        [high.astype(F32), rest.astype(F32), jnp.zeros((14, 2048), F32)], axis=0
    ).astype(BF16)
    spread_features(tail, feat_out, 144)
    mixed = jnp.dot(low, o_buf[:, :512], preferred_element_type=F32).astype(BF16)
    for load in p_loads:
        load.wait()
    scale = HEAD_DIM ** (-0.5)
    for h in range(4):
        cols = slice(h * HEAD_DIM, (h + 1) * HEAD_DIM)
        weights = prob[h]
        back = mixed[:, cols]
        grad_proj[:, 1024 + h * HEAD_DIM : 1024 + (h + 1) * HEAD_DIM] = tn(
            weights.astype(BF16), back
        ).astype(BF16)
        weight_grad = nt(back, proj[2, :, cols])
        offset = jnp.sum(weight_grad * weights, axis=-1, keepdims=True)
        score = (weights * (weight_grad - offset)).astype(BF16)
        grad_proj[:, cols] = (
            jnp.dot(score, proj[1, :, cols], preferred_element_type=F32) * scale
        ).astype(BF16)
        grad_proj[:, 512 + h * HEAD_DIM : 512 + (h + 1) * HEAD_DIM] = (
            tn(score, proj[0, :, cols]) * scale
        ).astype(BF16)


def attention_back_call(where, grads, dots, gates, hidden, resid, cots, packed, proj, prob, gain):
    shape = jax.ShapeDtypeStruct
    dma = pltpu.SemaphoreType.DMA
    return pl.pallas_call(
        attention_back_kernel,
        out_shape=(
            shape((8, 160, 256), BF16),
            shape((128, 1536), BF16),
            shape((128, 512), F32),
        ),
        in_specs=[spec(pltpu.SMEM)]
        + [spec(ANY)] * 4
        + [spec(VMEM)] * 2
        + [spec(ANY)] * 6
        + [spec(VMEM)],
        out_specs=(spec(VMEM),) * 3,
        scratch_shapes=[
            VMEM((2048, 640), BF16),
            VMEM((128, 2048), BF16),
            VMEM((128, 2048), BF16),
            VMEM((128, 2048), F32),
            VMEM((128, 2048), F32),
            VMEM((128, 2048), BF16),
            VMEM((128, 2048), BF16),
            VMEM((3, 128, 512), BF16),
            VMEM((4, 128, 128), F32),
            dma,
            dma,
            dma,
            dma((4,)),
            dma((4,)),
            dma((2,)),
        ],
        compiler_params=params(),
        cost_estimate=cost(10**9, 6 * 10**6),
        grid=(1,),
        name="attention_back",
    )(where, *grads, dots, gates, hidden, resid, cots, packed, proj, prob, gain)


def normed_back_kernel(where, grad_proj, tokens, gain, packed, o0, o1, o2, o3, w_buf, sem_w):
    y0 = where[0]
    outs = (o0, o1, o2, o3)
    order = [(y0 + k) & 3 for k in (1, 3, 2, 0)]
    loads = [
        pltpu.make_async_copy(
            packed.at[pl.ds(pl.multiple_of(at * 512, 512), 512), 0:1536], w_buf.at[i], sem_w.at[i]
        )
        for i, at in enumerate(order)
    ]
    for load in loads:
        load.start()
    values = tokens[...].astype(F32)
    factor = lax.rsqrt(jnp.mean(values * values, axis=-1, keepdims=True) + EPSILON)
    inner = jnp.zeros((128, 1), F32)
    sums = []
    for i, k in enumerate((1, 3, 2, 0)):
        loads[i].wait()
        grad = nt(grad_proj[...], w_buf[i])
        cols = pl.ds(pl.multiple_of(order[i] * 512, 512), 512)
        unit = tokens[:, cols].astype(F32) * factor
        inner = inner + jnp.sum(grad * unit * gain[:, cols], axis=-1, keepdims=True)
        sums.append(jnp.sum(grad * unit, axis=0, keepdims=True))
        outs[k][0:128, 0:512] = grad.astype(BF16)
    lane = lax.broadcasted_iota(jnp.int32, (128, 128), 1)
    high = inner.astype(BF16).astype(F32)
    both = jnp.where(lane == 0, high, jnp.where(lane == 1, inner - high, 0.0)).astype(BF16)
    row = lax.broadcasted_iota(jnp.int32, (16, 512), 0)
    table = jnp.zeros((16, 512), F32)
    for at, piece in zip(order, sums):
        top = piece.astype(BF16).astype(F32)
        table = jnp.where(row == at, top, jnp.where(row == at + 4, piece - top, table))
    for out in outs:
        out[0:128, 512:] = both
        out[128:, 0:512] = table.astype(BF16)
        out[128:, 512:] = jnp.zeros((16, 128), BF16)


def normed_back_call(where, grad_proj, tokens, gain, packed):
    return pl.pallas_call(
        normed_back_kernel,
        out_shape=(jax.ShapeDtypeStruct((144, 640), BF16),) * 4,
        in_specs=[spec(pltpu.SMEM), spec(VMEM), spec(VMEM), spec(VMEM), spec(ANY)],
        out_specs=(spec(VMEM),) * 4,
        scratch_shapes=[VMEM((4, 512, 1536), BF16), pltpu.SemaphoreType.DMA((4,))],
        compiler_params=params(),
        cost_estimate=cost(10**9, 8 * 10**6),
        grid=(1,),
        name="normed_back",
    )(where, grad_proj, tokens, gain, packed)


def pair_kernel(own, other, *outs):
    for k, out in enumerate(outs):
        out[...] = own[k] + other[k]


def pair_call(own, other):
    shape = own.shape[1:]
    block = (shape[0] // 4,) + shape[1:]
    rest = (0,) * (len(shape) - 1)
    return pl.pallas_call(
        pair_kernel,
        out_shape=(jax.ShapeDtypeStruct(shape, BF16),) * 4,
        grid=(4,),
        in_specs=[pl.BlockSpec((4,) + block, lambda i: (0, i) + rest)] * 2,
        out_specs=(pl.BlockSpec(block, lambda i: (i,) + rest),) * 4,
        compiler_params=params(),
        cost_estimate=cost(10**6, 6 * own.size),
        name="pair",
    )(own, other)


def join_dots(table):
    return jnp.concatenate(
        [table[0:16], table[16:32], jnp.zeros((16, 256), F32)], axis=1
    ).astype(BF16)


def combine_kernel(p0, p1, p2, p3, *outs):
    for r, out in enumerate(outs):
        total = (p0[r].astype(F32) + p1[r].astype(F32)) + (p2[r].astype(F32) + p3[r].astype(F32))
        out[0:128] = total[0:128].astype(BF16)
        dots = total[128:, 0:128] + total[128:, 128:256]
        high = dots.astype(BF16).astype(F32)
        out[128:] = join_dots(jnp.concatenate([high, dots - high], axis=0))


def combine_call(pieces):
    return pl.pallas_call(
        combine_kernel,
        out_shape=(jax.ShapeDtypeStruct((144, 512), BF16),) * 4,
        grid=(1,),
        compiler_params=params(),
        cost_estimate=cost(10**6, 3 * 10**6),
        name="combine",
    )(*pieces)


def finish_kernel(p0, p1, p2, p3, cols, dots):
    total = (p0[...].astype(F32) + p1[...].astype(F32)) + (p2[...].astype(F32) + p3[...].astype(F32))
    cols[...] = total[0:128].astype(BF16)
    table = total[128:, 0:128] + total[128:, 128:256]
    dots[...] = jnp.concatenate([table, jnp.zeros((112, 128), F32)], axis=0).T


def finish_call(pieces):
    shape = jax.ShapeDtypeStruct
    return pl.pallas_call(
        finish_kernel,
        out_shape=(shape((128, 512), BF16), shape((128, 128), F32)),
        cost_estimate=cost(10**6, 10**6),
        compiler_params=params(),
        grid=(1,),
        name="finish",
    )(*pieces)


def columns_kernel(where, p0, p1, p2, p3, *outs):
    y0 = where[0]
    for k, out in enumerate(outs):
        cols = pl.ds(pl.multiple_of(((y0 + k) & 3) * 512, 512), 512)
        total = (p0[:, cols].astype(F32) + p1[:, cols].astype(F32)) + (
            p2[:, cols].astype(F32) + p3[:, cols].astype(F32)
        )
        out[...] = total.astype(BF16)


def columns_call(where, pieces):
    return pl.pallas_call(
        columns_kernel,
        out_shape=(jax.ShapeDtypeStruct((128, 512), BF16),) * 4,
        grid=(4,),
        in_specs=[spec(pltpu.SMEM)] + [pl.BlockSpec((32, 2048), lambda i: (i, 0))] * 4,
        out_specs=(pl.BlockSpec((32, 512), lambda i: (i, 0)),) * 4,
        compiler_params=params(),
        cost_estimate=cost(10**6, 3 * 10**6),
        name="columns",
    )(where, *pieces)


def tail_kernel(
    where, normed, own, other, branch, mixed, o0, o1, o2, o3, n_buf, p_buf, a_buf, sem
):
    me, d0 = where[1], where[2]
    loads = [
        pltpu.make_async_copy(piece.at[r], p_buf.at[pl.ds((c * 4 + r) * 128, 128)], sem.at[c, r])
        for c, piece in enumerate((own, other))
        for r in range(4)
    ]
    for load in loads:
        load.start()
    for r in range(8):
        at = (((me >> 1) + (r & 3)) & 3) * 2 + (((me & 1) + (r >> 2)) & 1)
        n_buf[r * 128 : (r + 1) * 128] = normed[at]
    a_buf[:, 1536:2048] = tn(branch[:, 0:128, :].reshape(1024, 256), mixed[...])
    small = jnp.sum(branch[:, 128:160, :].astype(F32), axis=0)
    a_buf[:, 2048:] = jnp.concatenate([small, jnp.zeros((96, 256), F32)], axis=0).T
    for load in loads:
        load.wait()
    for s in range(3):
        a_buf[:, s * 512 : (s + 1) * 512] = tn(n_buf[...], p_buf[:, s * 512 : (s + 1) * 512])
    for k, out in enumerate((o0, o1, o2, o3)):
        out[...] = a_buf[pl.ds(pl.multiple_of(((d0 + k) & 3) * 64, 64), 64), :].astype(BF16)


def tail_call(where, normed, own, other, branch, mixed):
    dma = pltpu.SemaphoreType.DMA
    return pl.pallas_call(
        tail_kernel,
        out_shape=(jax.ShapeDtypeStruct((64, 2176), BF16),) * 4,
        in_specs=[spec(pltpu.SMEM), spec(VMEM), spec(ANY), spec(ANY)] + [spec(VMEM)] * 2,
        out_specs=(spec(VMEM),) * 4,
        scratch_shapes=[
            VMEM((1024, 256), BF16),
            VMEM((1024, 1536), BF16),
            VMEM((256, 2176), F32),
            dma((2, 4)),
        ],
        compiler_params=params(),
        cost_estimate=cost(10**9, 8 * 10**6),
        grid=(1,),
        name="tail",
    )(where, normed, own, other, branch, mixed)


def block_row(me, r, s):
    group = (((me >> 1) + (r & 3)) & 3) * 2 + (((me & 1) + (r >> 2)) & 1)
    source = (((s >> 1) - (me >> 1)) & 3) + (((s & 1) + (me & 1)) & 1) * 4
    return pl.multiple_of(r * 128 + s * 16, 16), pl.multiple_of(source * 128 + group * 16, 16)


def back_kernel(
    where, g_own, g_other, w0, w1, w2, w3, g_out, back, own_rows, w_out,
    g_buf, w_buf, z_buf, sem_g, sem_w, sem_o,
):
    y0, me = where[0], where[1]
    offs = [pl.multiple_of(((y0 + k) & 3) * 512, 512) for k in range(4)]
    loads = [
        pltpu.make_async_copy(
            piece.at[k], g_buf.at[pl.ds(c * 512, 512), pl.ds(offs[k], 512)], sem_g.at[c, k]
        )
        for c, piece in enumerate((g_own, g_other))
        for k in range(4)
    ]
    w_loads = [
        pltpu.make_async_copy(
            piece,
            w_buf.at[:, pl.ds(pl.multiple_of(((where[2] + k) & 3) * 512, 512), 512), :],
            sem_w.at[k],
        )
        for k, piece in enumerate((w0, w1, w2, w3))
    ]
    for load in loads + w_loads:
        load.start()
    for load in loads:
        load.wait()
    out = pltpu.make_async_copy(g_buf, g_out, sem_o.at[0])
    out.start()
    for load in w_loads:
        load.wait()
    down_out = pltpu.make_async_copy(w_buf, w_out, sem_o.at[1])
    down_out.start()
    for e in range(2):
        z_buf[:, e * 256 : (e + 1) * 256] = jnp.dot(g_buf[...], w_buf[e], preferred_element_type=F32)

    def move(i, _):
        to, at = block_row(me, i >> 3, i & 7)
        back[pl.ds(to, 16), :] = z_buf[pl.ds(at, 16), :]
        return 0

    lax.fori_loop(0, 64, move, 0)
    for s in range(8):
        _, at = block_row(me, 0, s)
        own_rows[s * 16 : (s + 1) * 16, :] = g_buf[pl.ds(at, 16), :]
    out.wait()
    down_out.wait()


def back_call(where, g_own, g_other, down):
    shape = jax.ShapeDtypeStruct
    dma = pltpu.SemaphoreType.DMA
    return pl.pallas_call(
        back_kernel,
        out_shape=(shape((1024, 2048), BF16), shape((1024, 512), F32), shape((128, 2048), BF16), shape((2, 2048, 256), BF16)),
        in_specs=[spec(pltpu.SMEM)] + [spec(ANY)] * 6,
        out_specs=(spec(ANY), spec(VMEM), spec(VMEM), spec(ANY)),
        scratch_shapes=[
            VMEM((1024, 2048), BF16),
            VMEM((2, 2048, 256), BF16),
            VMEM((1024, 512), F32),
            dma((2, 4)),
            dma((4,)),
            dma((2,)),
        ],
        compiler_params=params(),
        cost_estimate=cost(2 * 10**9, 13 * 10**6),
        grid=(1,),
        name="back",
    )(where, g_own, g_other, *down)


def expert_kernel(
    where, near_own, far_own, near_other, far_other, back, code, weights, packed, gain,
    sent_own, sent_other, h_out, mid_out, source_out, gates_out,
    x_buf, b_buf, w_buf, h_buf, d_buf, r_buf, mid, by_source,
    sem_x, sem_b, sem_w, sem_r, sem_h, sem_m, sem_d,
):
    y0, me = where[0], where[1]
    offs = [pl.multiple_of(((y0 + k) & 3) * 512, 512) for k in range(4)]
    x_loads = [
        [
            pltpu.make_async_copy(piece, x_buf.at[b, r], sem_x.at[b, r])
            for r, piece in enumerate((near.at[0], near.at[1], far, near.at[2]))
        ]
        for b, (near, far) in enumerate(((near_own, far_own), (near_other, far_other)))
    ]
    w_load = pltpu.make_async_copy(weights.at[pl.ds(0, 4)], w_buf, sem_w)
    r_load = pltpu.make_async_copy(packed.at[:, 2048:2176], r_buf, sem_r)
    b_load = pltpu.make_async_copy(back, b_buf, sem_b)
    for load in x_loads[0]:
        load.start()
    r_load.start()
    w_load.start()
    b_load.start()
    for load in x_loads[1]:
        load.start()
    stores = []
    lane = lax.broadcasted_iota(jnp.int32, (512, 128), 1)
    for b in range(2):
        for load in x_loads[b]:
            load.wait()

        def norm(r, _):
            square = jnp.zeros((128, 1), F32)
            for k in range(4):
                value = x_buf[b, r, k].astype(F32)
                square = square + jnp.sum(value * value, axis=-1, keepdims=True)
            factor = lax.rsqrt(square * (1.0 / 2048) + EPSILON)
            at = pl.ds(pl.multiple_of(b * 512 + r * 128, 128), 128)
            for k in range(4):
                part = gain[pl.ds((y0 + k) & 3, 1), :]
                h_buf[at, pl.ds(offs[k], 512)] = (x_buf[b, r, k].astype(F32) * factor * part).astype(BF16)
            return 0

        lax.fori_loop(0, 4, norm, 0)
        here = pl.ds(b * 512, 512)
        stores.append(pltpu.make_async_copy(h_buf.at[here], h_out.at[here], sem_h.at[b]))
        stores[-1].start()
        if b == 0:
            r_load.wait()
        logits = jnp.dot(h_buf[here, :], r_buf[...], preferred_element_type=F32)
        codes = code[here, :].astype(F32)
        chosen = codes > 0.5
        top = jnp.max(jnp.where(chosen, logits, -jnp.inf), axis=-1, keepdims=True)
        lifted = jnp.where(chosen, jnp.exp(logits - top), 0.0)
        gates = lifted / jnp.sum(lifted, axis=-1, keepdims=True)
        if b == 0:
            gates_out[...] = gates[:128]
            w_load.wait()
            b_load.wait()
        used = jnp.where(codes > 1.5, gates, 0.0)
        dots = jnp.zeros((512, 128), F32)
        for e in range(2):
            mine = lane == me * 2 + e
            use = jnp.sum(jnp.where(mine, used, 0.0), axis=-1, keepdims=True)
            keep = jnp.sum(jnp.where(mine & (codes > 1.5), 1.0, 0.0), axis=-1, keepdims=True)
            cols = pl.ds(e * 256, 256)
            u = jnp.dot(h_buf[here, :], w_buf[e], preferred_element_type=F32)
            w = jnp.dot(h_buf[here, :], w_buf[2 + e], preferred_element_type=F32)
            z = b_buf[here, cols]
            s = 1.0 / (1.0 + jnp.exp(-u))
            silu = u * s
            act = silu * w
            dot = jnp.sum(z * act, axis=-1, keepdims=True) * keep
            high = dot.astype(BF16).astype(F32)
            dots = jnp.where(mine, high, dots)
            dots = jnp.where(lane == me * 2 + e + 16, dot - high, dots)
            z = z * use
            mid[0, here, cols] = (z * w * s * (1.0 + u * (1.0 - s))).astype(BF16)
            mid[1, here, cols] = (z * silu).astype(BF16)
            mid[2, here, cols] = (act * use).astype(BF16)
        turned = [join_dots(dots[r * 128 : (r + 1) * 128].T) for r in range(4)]
        for k in range(4):
            acc = None
            for e in range(2):
                for m in range(2):
                    term = nt(mid[m, here, pl.ds(e * 256, 256)], w_buf[2 * m + e, pl.ds(offs[k], 512), :])
                    acc = term if acc is None else acc + term
            acc = acc.astype(BF16)
            for r in range(4):
                d_buf[b, k, r, 0:128] = acc[r * 128 : (r + 1) * 128]
                d_buf[b, k, r, 128:] = turned[r]
            target = (sent_own, sent_other)[b].at[k]
            stores.append(pltpu.make_async_copy(d_buf.at[b, k], target, sem_d.at[b, k]))
            stores[-1].start()
    stores.append(pltpu.make_async_copy(mid, mid_out, sem_m.at[0]))
    stores[-1].start()

    def move(i, _):
        at, to = block_row(me, i >> 3, i & 7)
        by_source[pl.ds(to, 16), :] = mid[2, pl.ds(at, 16), :]
        return 0

    lax.fori_loop(0, 64, move, 0)
    stores.append(pltpu.make_async_copy(by_source, source_out, sem_m.at[1]))
    stores[-1].start()
    for store in stores:
        store.wait()


def experts_call(where, resid, back, code, weights, packed, gain):
    shape = jax.ShapeDtypeStruct
    dma = pltpu.SemaphoreType.DMA
    return pl.pallas_call(
        expert_kernel,
        out_shape=(
            shape((4, 4, 144, 512), BF16),
            shape((4, 4, 144, 512), BF16),
            shape((1024, 2048), BF16),
            shape((3, 1024, 512), BF16),
            shape((1024, 512), BF16),
            shape((128, 128), F32),
        ),
        in_specs=[spec(pltpu.SMEM)]
        + [spec(ANY)] * 5
        + [spec(VMEM)]
        + [spec(ANY)] * 2
        + [spec(VMEM)],
        out_specs=(spec(ANY),) * 5 + (spec(VMEM),),
        scratch_shapes=[
            VMEM((2, 4, 4, 128, 512), BF16),
            VMEM((1024, 512), F32),
            VMEM((4, 2048, 256), BF16),
            VMEM((1024, 2048), BF16),
            VMEM((2, 4, 4, 144, 512), BF16),
            VMEM((2048, 128), BF16),
            VMEM((3, 1024, 512), BF16),
            VMEM((1024, 512), BF16),
            dma((2, 4)),
            dma,
            dma,
            dma,
            dma((2,)),
            dma((2,)),
            dma((2, 4)),
        ],
        compiler_params=params(),
        cost_estimate=cost(9 * 10**9, 26 * 10**6),
        grid=(1,),
        name="experts",
    )(where, *resid, back, code, weights, packed, gain)


def grads_kernel(h, g, mid, by_source, out):
    for i, (rows, cols) in enumerate(((h, mid[0]), (h, mid[1]), (g, by_source[...]))):
        grad = tn(rows[...], cols)
        for e in range(2):
            out[0, 2 * i + e] = grad[:, e * 256 : (e + 1) * 256].astype(BF16)


def grads_call(h, g, mid, by_source):
    return pl.pallas_call(
        grads_kernel,
        grid=(4,),
        out_shape=jax.ShapeDtypeStruct((4, 6, 512, 256), BF16),
        in_specs=[
            pl.BlockSpec((1024, 512), lambda j: (0, j)),
            pl.BlockSpec((1024, 512), lambda j: (0, j)),
            pl.BlockSpec((2, 1024, 512), lambda j: (0, 0, 0)),
            pl.BlockSpec((1024, 512), lambda j: (0, 0)),
        ],
        out_specs=pl.BlockSpec((1, 6, 512, 256), lambda j: (j, 0, 0, 0)),
        compiler_params=params(),
        cost_estimate=cost(7 * 10**9, 18 * 10**6),
        name="grads",
    )(h, g, mid, by_source)


def rows_kernel(mid, w, own, other):
    acc = nt(mid[0, :, 0:256], w[0]) + nt(mid[0, :, 256:512], w[1])
    own[...] = acc[:512].astype(BF16)
    other[...] = acc[512:].astype(BF16)


def rows_call(mid, weights):
    shape = jax.ShapeDtypeStruct
    return pl.pallas_call(
        rows_kernel,
        grid=(4,),
        out_shape=(shape((512, 2048), BF16),) * 2,
        in_specs=[
            pl.BlockSpec((1, 1024, 512), lambda j: (2, 0, 0)),
            pl.BlockSpec((2, 512, 256), lambda j: (0, j, 0)),
        ],
        out_specs=(pl.BlockSpec((512, 512), lambda j: (0, j)),) * 2,
        compiler_params=params(),
        cost_estimate=cost(2 * 10**9, 7 * 10**6),
        name="rows",
    )(mid, weights)


def local(
    tokens,
    cotangent,
    seq_lengths,
    deal_order,
    expert_ids,
    slot_order,
    qkv_weight,
    out_weight,
    router_weight,
    gate_weight,
    up_weight,
    down_weight,
    gain_first,
    gain_second,
):
    rows, width = tokens.shape
    zc = ("z", "core")
    peers = lax.axis_size("z") * lax.axis_size("core")
    tensors = lax.axis_size("tensor")
    dps = lax.axis_size("dp")
    zs = lax.axis_size("z")
    share = rows // peers
    part = width // tensors
    me_core = lax.axis_index("core")
    me_z = lax.axis_index("z")
    me = me_z * 2 + me_core
    me_y = lax.axis_index("tensor")
    experts = router_weight.shape[0]
    top = expert_ids.shape[1]
    capacity = (5 * rows * top + 4 * experts - 1) // (4 * experts)
    here = gate_weight.shape[0]
    head_width = qkv_weight.shape[2]
    feats = qkv_weight.shape[1]

    place_now = jnp.stack([me_y, me, lax.axis_index("dp")]).astype(jnp.int32)

    packed = lax.all_gather(
        pack_call(qkv_weight, out_weight.T, router_weight), ("dp", "z", "core"), axis=0, tiled=True
    )
    expert_local = jnp.concatenate([gate_weight, up_weight], axis=0)
    down_near = gather_ring(down_weight, "dp")

    dest_group = deal_order // rows % peers
    place = dest_group * share + (deal_order % rows - me * share)
    deal_matrix = (place[None, :] == jnp.arange(rows, dtype=jnp.int32)[:, None]).astype(BF16)
    dealt = jnp.dot(deal_matrix, tokens, preferred_element_type=F32).astype(BF16)
    cot_part = lax.dynamic_slice_in_dim(cotangent, me_y * part, part, 1)
    cot_part = jnp.dot(deal_matrix, cot_part, preferred_element_type=F32).astype(BF16)

    match = expert_ids[:, :, None] == jnp.arange(experts, dtype=jnp.int32)[None, None, :]
    order = jnp.min(jnp.where(match, slot_order[:, :, None], BIG), axis=1)
    chosen = order < BIG
    earlier = jnp.sum((order[None, :, :] < order[:, None, :]).astype(jnp.int32), axis=1)
    code = chosen.astype(F32) + (chosen & (earlier < capacity)).astype(F32)
    table = jnp.pad(code, ((0, 0), (0, 128 - experts))).astype(BF16)
    cot_near = gather_near(jnp.concatenate([cot_part, table], axis=1), "z")
    code_own = jnp.stack([near[:, part:] for near in cot_near])
    code_all = jnp.stack([code_own, core_swap(code_own)]).reshape(peers * rows, 128)
    cot_own = jnp.stack([near[:, :part] for near in cot_near])
    dealt, cot_own = lax.optimization_barrier((dealt, cot_own))
    got = lax.all_to_all(
        dealt.reshape(peers, share, width), zc, split_axis=0, concat_axis=0, tiled=True
    ).reshape(rows, width)
    cot_own = jnp.stack(gather_near(cot_own, "tensor")).reshape(tensors, zs * rows, part)

    segment = segment_of(seq_lengths[0], rows)
    same_seq = (segment[:, None] == segment[None, :]).astype(F32)
    normed, normed_feat = norm_call(got, gain_first.reshape(1, width))
    normed_feat = lax.all_to_all(normed_feat, zc, split_axis=0, concat_axis=0, tiled=True)
    expert_local, normed = lax.optimization_barrier((expert_local, normed))
    expert_full = lax.all_gather(expert_local, "dp", axis=1, tiled=True)
    normed, normed_feat, cot_own, code_all, packed, down_near = lax.optimization_barrier(
        (normed, normed_feat, cot_own, code_all, packed, down_near)
    )
    cot_other = core_swap(cot_own)
    projected, weights, mixed, *branch = attention_call(place_now, normed, same_seq, packed)
    mixed_all = lax.all_gather(mixed, zc, axis=0, tiled=True)
    resid_in = got.astype(F32)
    resid_part = lax.dynamic_slice_in_dim(resid_in, me_y * part, part, 1) + sum_near(
        branch, "tensor"
    )
    resid_near = jnp.stack(gather_near(resid_part.astype(BF16), "tensor"))
    resid_near, cot_other = lax.optimization_barrier((resid_near, cot_other))
    left, right = shift(resid_near, "z", 1), shift(resid_near, "z", -1)
    cot_all, back, upstream, down_full = back_call(place_now, cot_own, cot_other, down_near)
    half = tensors // 2
    left, right, back = lax.optimization_barrier((left, right, back))
    far = [shift(left[:half], "z", 1), shift(right[half:], "z", -1)]
    near_own = jnp.stack([resid_near, right, left])
    near_other = core_swap(near_own)
    far, near_other = lax.optimization_barrier((far, near_other))
    far_own = jnp.concatenate(far, axis=0)
    far_other = core_swap(far_own)

    sent_own, sent_other, hidden, mids, mid_source, gates = experts_call(
        place_now,
        (near_own, far_own, near_other, far_other),
        back,
        code_all,
        expert_full,
        packed,
        gain_second.reshape(tensors, part),
    )
    rows_own, rows_other = rows_call(mids, down_full)
    paired = pair_call(sent_own, core_swap(sent_other))
    paired, rows_own, rows_other = lax.optimization_barrier((paired, rows_own, rows_other))
    expert_rows = pair_call(
        rows_own.reshape(zs, rows, width), core_swap(rows_other).reshape(zs, rows, width)
    )
    expert_grads = grads_call(hidden, cot_all, mids, mid_source)
    cols, expert_rows, expert_grads = lax.optimization_barrier(
        (swap_near(paired, "tensor"), swap_near(expert_rows, "z"), expert_grads)
    )
    cols, expert_rows = lax.optimization_barrier((combine_call(cols), expert_rows))
    cols, expert_rows = lax.optimization_barrier(
        (swap_near(cols, "z"), columns_call(place_now, expert_rows))
    )
    cols, dots = finish_call(cols)
    expert_rows = swap_near(expert_rows, "tensor")
    grads_near, expert_rows[:3] = lax.optimization_barrier(
        (gather_near(cols, "tensor"), expert_rows[:3])
    )

    branch_feat, grad_proj, grad_own = attention_back_call(
        place_now,
        grads_near,
        dots,
        gates,
        hidden,
        resid_near,
        upstream,
        packed,
        projected,
        weights,
        gain_second.reshape(1, width),
    )
    grad_z = jnp.stack(gather_near(grad_proj, "z"))
    grad_other = core_swap(grad_z)
    branch_feat = lax.all_to_all(branch_feat, zc, split_axis=0, concat_axis=0, tiled=True)
    normed_cols = sum_near(
        normed_back_call(place_now, grad_proj, got, gain_first.reshape(1, width), packed), "tensor"
    )
    inner = normed_cols[:rows, part : part + 1] + normed_cols[:rows, part + 1 : part + 2]
    inner = inner / width
    gain_sum = (normed_cols[rows : rows + 4, :part] + normed_cols[rows + 4 : rows + 8, :part]).reshape(
        dps, peers, feats
    )
    gain_sum = gain_sum.transpose(1, 0, 2).reshape(peers, 1, dps * feats)
    gain_high = gain_sum.astype(BF16)
    gain_low = (gain_sum - gain_high.astype(F32)).astype(BF16)
    gain_rows = jnp.pad(
        jnp.concatenate([gain_high, gain_low], axis=1), ((0, 0), (0, 14), (0, 2 * part - dps * feats))
    )

    def own_cols(table):
        return lax.dynamic_slice_in_dim(table, me_y * part, part, table.ndim - 1)

    factor_first = lax.rsqrt(jnp.mean(resid_in * resid_in, axis=-1, keepdims=True) + EPSILON)
    input_part = grad_own + factor_first * (
        normed_cols[:rows, :part] * own_cols(gain_first) - own_cols(resid_in) * factor_first * inner
    )

    expert_grads = lax.psum_scatter(expert_grads, "dp", scatter_dimension=0, tiled=False)
    expert_grads = [expert_grads[here * i : here * (i + 1)].astype(F32) for i in range(3)]

    output_part = resid_part + total(expert_rows)

    final = jnp.concatenate([output_part.astype(BF16), input_part.astype(BF16)], axis=1)
    final = jnp.concatenate([final.reshape(peers, share, 2 * part), gain_rows], axis=1)
    final = lax.all_to_all(final, zc, split_axis=0, concat_axis=0, tiled=True)
    by_dp = tail_call(place_now, normed_feat, grad_z, grad_other, branch_feat, mixed_all)
    final, _ = lax.optimization_barrier((final, by_dp))
    gain_sum = jnp.sum(final[:, share : share + 2, : dps * feats].astype(F32), axis=(0, 1))
    gain_sum = gain_sum.reshape(dps, 1, feats)
    dp_index = lax.axis_index("dp")
    gain_sum = [
        lax.dynamic_index_in_dim(gain_sum, (dp_index + k) % dps, 0, keepdims=False) for k in range(dps)
    ]
    final = lax.dot_general(
        deal_matrix,
        final[:, :share].reshape(rows, 2 * part),
        (((0,), (0,)), ((), ())),
        preferred_element_type=F32,
    ).astype(BF16)
    by_dp, gain_sum, final, expert_grads = lax.optimization_barrier(
        (swap_near(by_dp, "dp"), swap_near(gain_sum, "dp"), final, expert_grads)
    )
    by_dp = total(by_dp)
    qkv_grad = by_dp[:, : 3 * head_width].reshape(feats, 3, head_width).transpose(1, 0, 2)
    out_grad = by_dp[:, 3 * head_width : 4 * head_width].T
    tail = by_dp[:, 4 * head_width :]
    router_grad = tail[:, :experts].T
    gain_second_grad = tail[:, experts] + tail[:, experts + 1]
    gain_first_grad = total(gain_sum)[0]

    return (
        final[:, :part],
        final[:, part:],
        qkv_grad,
        out_grad,
        router_grad,
        *expert_grads,
        gain_first_grad,
        gain_second_grad,
    )


def solution(mesh):
    sizes = mesh.shape
    split = Mesh(
        mesh.devices.reshape(sizes["dp"], sizes["expert"] // 2, 2, sizes["tensor"]),
        ("dp", "z", "core", "tensor"),
    )
    experts = ("z", "core")
    every = ("dp", "z", "core")
    placed = (
        P(every, None),
        P(every, None),
        P(every, None),
        P(every),
        P(every, None),
        P(every, None),
        P(None, every, "tensor"),
        P("tensor", every),
        P(None, every),
        P(experts, "dp", "tensor"),
        P(experts, "dp", "tensor"),
        P(experts, "dp", "tensor"),
        P(),
        P(),
    )
    return jax.shard_map(
        local,
        mesh=split,
        in_specs=placed,
        out_specs=(
            P(every, "tensor"),
            P(every, "tensor"),
            P(None, every, "tensor"),
            P("tensor", every),
            P(None, every),
            P(experts, "dp", "tensor"),
            P(experts, "dp", "tensor"),
            P(experts, "dp", "tensor"),
            P(every),
            P(every),
        ),
        check_vma=False,
    )
```
